32 devices in a mesh: seq: 8 (over y, x, core), batch: 4 (over z).
Axes of the slice: x: 2, y: 2, z: 4, core: 2. Of those that a mesh axis runs over, the one named last changes fastest.
Arguments:
- incoming_activations: bfloat16 [8, 2048, 1024], P('batch', 'seq'), may hold values from -6 to 6
- wkv_preceding_entry: bfloat16 [8, 1024], P('batch'), may hold values from -6 to 6
- feedforward_preceding_entry: bfloat16 [8, 1024], P('batch'), may hold values from -6 to 6
- preceding_partition_memory: float32 [8, 16, 64, 64], P('batch'), may hold values from -18 to 18
- upstream_sensitivity: bfloat16 [8, 2048, 1024], P('batch', 'seq'), may hold values from -6 to 6
- opening_standardize_scale: bfloat16 [1024], P(('seq', 'batch')), may hold values from 0.5 to 1.5
- opening_standardize_shift: bfloat16 [1024], P(('seq', 'batch')), may hold values from -1.5 to 1.5
- wkv_lag_blends: bfloat16 [1024, 4], P(('seq', 'batch')), may hold values from 0.049804688 to 0.94921875
- accept_projection: bfloat16 [1024, 1024], P(('seq', 'batch')), may hold values from -0.1875 to 0.1875
- lookup_projection: bfloat16 [1024, 1024], P(('seq', 'batch')), may hold values from -0.1875 to 0.1875
- content_projection: bfloat16 [1024, 1024], P(('seq', 'batch')), may hold values from -0.1875 to 0.1875
- gating_projection: bfloat16 [1024, 1024], P(('seq', 'batch')), may hold values from -0.1875 to 0.1875
- logarithmic_fading_factors: bfloat16 [1024], P(('seq', 'batch')), may hold values from -9.1875 to -3
- present_entry_reward: bfloat16 [1024], P(('seq', 'batch')), may hold values from -3 to 3
- cluster_standardize_scale: bfloat16 [1024], P(('seq', 'batch')), may hold values from 0.5 to 1.5
- cluster_standardize_shift: bfloat16 [1024], P(('seq', 'batch')), may hold values from -1.5 to 1.5
- emission_projection: bfloat16 [1024, 1024], P(('seq', 'batch')), may hold values from -0.1875 to 0.1875
- closing_standardize_scale: bfloat16 [1024], P(('seq', 'batch')), may hold values from 0.5 to 1.5
- closing_standardize_shift: bfloat16 [1024], P(('seq', 'batch')), may hold values from -1.5 to 1.5
- feedforward_lag_blends: bfloat16 [1024, 2], P(('seq', 'batch')), may hold values from 0.049804688 to 0.94921875
- feedforward_lookup_projection: bfloat16 [1024, 3584], P(('seq', 'batch')), may hold values from -0.1875 to 0.1875
- feedforward_content_projection: bfloat16 [3584, 1024], P(('seq', 'batch')), may hold values from -0.09375 to 0.09375
- feedforward_accept_projection: bfloat16 [1024, 1024], P(('seq', 'batch')), may hold values from -0.1875 to 0.1875
Outputs:
- block_result: bfloat16 [8, 2048, 1024], P('batch', 'seq')
- argument_sensitivity: bfloat16 [8, 2048, 1024], P('batch', 'seq')
- opening_standardize_scale_sens: float32 [1024], P(('seq', 'batch'))
- opening_standardize_shift_sens: float32 [1024], P(('seq', 'batch'))
- wkv_blend_cotangent: float32 [1024, 4], P(('seq', 'batch'))
- accept_projection_sens: float32 [1024, 1024], P(('seq', 'batch'))
- lookup_projection_sens: float32 [1024, 1024], P(('seq', 'batch'))
- content_projection_sens: float32 [1024, 1024], P(('seq', 'batch'))
- gating_projection_sens: float32 [1024, 1024], P(('seq', 'batch'))
- logarithmic_fading_sens: float32 [1024], P(('seq', 'batch'))
- sequence_reward_sens: float32 [1024], P(('seq', 'batch'))
- cluster_standardize_scale_sens: float32 [1024], P(('seq', 'batch'))
- cluster_standardize_shift_sens: float32 [1024], P(('seq', 'batch'))
- emission_projection_sens: float32 [1024, 1024], P(('seq', 'batch'))
- closing_standardize_scale_sens: float32 [1024], P(('seq', 'batch'))
- closing_standardize_shift_sens: float32 [1024], P(('seq', 'batch'))
- feedforward_blend_cotangent: float32 [1024, 2], P(('seq', 'batch'))
- feedforward_lookup_cotangent: float32 [1024, 3584], P(('seq', 'batch'))
- feedforward_content_cotangent: float32 [3584, 1024], P(('seq', 'batch'))
- feedforward_accept_cotangent: float32 [1024, 1024], P(('seq', 'batch'))
The draws below stay inside these ranges and needn't reach their ends.
All inputs are finite; a program needn't handle non-finite values.
Results may differ from the reference program's by a relative error of at most 0.014.
The reference program's roundings to bfloat16 on the way count: a program that leaves them out, or rounds other values in their place, can miss the bound.
Values may be sent and summed in bfloat16 or wider, within the bound.
A program may use at most 320 MiB of HBM per device.

```python
import jax
import jax.numpy as jnp
from jax import lax

EMBED_DIMENSION = 1024
WKV_PARTITIONS = 16
SUBSPACE_EXTENT = 64
FF = 3584
CH = 64
SEGS = 8
LENGTH = 2048


def level_of(own_key, extent, shards, smallest, high):
    level, own = 1.0, jax.random.fold_in(own_key, 6)
    for dim, shards_of in shards:
        draws = jnp.exp(jax.random.uniform(jax.random.fold_in(own, dim), (shards_of,), jnp.float32, smallest / len(shards), high / len(shards)))
        level = level * jnp.repeat(draws, extent[dim] // shards_of).reshape([-1 if axis == dim else 1 for axis in range(len(extent))])
    return level


def scatter_about(own_key, shape, scale, limit, cuts=(), held_as=jnp.bfloat16):
    drawn = jax.random.normal(own_key, shape, jnp.float32) * scale
    if len(cuts) > 0:
        drawn = level_of(own_key, shape, cuts, -0.22, 0.18) * drawn
    return jnp.clip(drawn, min=-limit, max=limit).astype(held_as)


def setup_inputs(seed: int = 0) -> dict:
    splits = jax.random.split(jax.random.key(seed), 24)
    incoming_activations = scatter_about(splits[0], (SEGS, LENGTH, EMBED_DIMENSION), 1.0, 6.0, ((0, 4), (1, 8)))
    wkv_preceding_entry = scatter_about(splits[1], (SEGS, EMBED_DIMENSION), 1.0, 6.0, ((0, 4),))
    feedforward_preceding_entry = scatter_about(splits[2], (SEGS, EMBED_DIMENSION), 1.0, 6.0, ((0, 4),))
    preceding_partition_memory = scatter_about(splits[3], (SEGS, WKV_PARTITIONS, SUBSPACE_EXTENT, SUBSPACE_EXTENT), 3.0, 18.0, ((0, 4),), jnp.float32)
    upstream_sensitivity = scatter_about(splits[4], (SEGS, LENGTH, EMBED_DIMENSION), 1.0, 6.0, ((0, 4), (1, 8)))
    opening_standardize_scale = jnp.clip(1.0 + 0.1 * jax.random.normal(splits[5], (EMBED_DIMENSION,), jnp.float32), 0.5, 1.5).astype(jnp.bfloat16)
    opening_standardize_shift = scatter_about(splits[6], (EMBED_DIMENSION,), 0.3, 1.5, ((0, 32),))
    wkv_lag_blends = jnp.clip(0.049804688 + 0.89941406 * jax.random.uniform(splits[7], (EMBED_DIMENSION, 4), jnp.float32) ** level_of(splits[7], (EMBED_DIMENSION, 4), ((0, 32),), -0.2, 0.2), 0.049804688, 0.94921875).astype(jnp.bfloat16)
    accept_projection = scatter_about(splits[8], (EMBED_DIMENSION, EMBED_DIMENSION), EMBED_DIMENSION ** -0.5, 0.1875, ((0, 32),))
    lookup_projection = scatter_about(splits[9], (EMBED_DIMENSION, EMBED_DIMENSION), EMBED_DIMENSION ** -0.5, 0.1875, ((0, 32),))
    content_projection = scatter_about(splits[10], (EMBED_DIMENSION, EMBED_DIMENSION), EMBED_DIMENSION ** -0.5, 0.1875, ((0, 32),))
    gating_projection = scatter_about(splits[11], (EMBED_DIMENSION, EMBED_DIMENSION), EMBED_DIMENSION ** -0.5, 0.1875, ((0, 32),))
    logarithmic_fading_factors = jnp.clip(-9.1875 + 6.1875 * jax.random.uniform(splits[12], (EMBED_DIMENSION,), jnp.float32) ** level_of(splits[12], (EMBED_DIMENSION,), ((0, 32),), -0.2, 0.2), -9.1875, -3.0).astype(jnp.bfloat16)
    present_entry_reward = scatter_about(splits[13], (EMBED_DIMENSION,), 0.5, 3.0, ((0, 32),))
    cluster_standardize_scale = jnp.clip(1.0 + 0.1 * jax.random.normal(splits[14], (EMBED_DIMENSION,), jnp.float32), 0.5, 1.5).astype(jnp.bfloat16)
    cluster_standardize_shift = scatter_about(splits[15], (EMBED_DIMENSION,), 0.3, 1.5, ((0, 32),))
    emission_projection = scatter_about(splits[16], (EMBED_DIMENSION, EMBED_DIMENSION), EMBED_DIMENSION ** -0.5, 0.1875, ((0, 32),))
    closing_standardize_scale = jnp.clip(1.0 + 0.1 * jax.random.normal(splits[17], (EMBED_DIMENSION,), jnp.float32), 0.5, 1.5).astype(jnp.bfloat16)
    closing_standardize_shift = scatter_about(splits[18], (EMBED_DIMENSION,), 0.3, 1.5, ((0, 32),))
    feedforward_lag_blends = jnp.clip(0.049804688 + 0.89941406 * jax.random.uniform(splits[19], (EMBED_DIMENSION, 2), jnp.float32) ** level_of(splits[19], (EMBED_DIMENSION, 2), ((0, 32),), -0.2, 0.2), 0.049804688, 0.94921875).astype(jnp.bfloat16)
    feedforward_lookup_projection = scatter_about(splits[20], (EMBED_DIMENSION, FF), EMBED_DIMENSION ** -0.5, 0.1875, ((0, 32),))
    feedforward_content_projection = scatter_about(splits[21], (FF, EMBED_DIMENSION), FF ** -0.5, 0.09375, ((0, 32),))
    feedforward_accept_projection = scatter_about(splits[22], (EMBED_DIMENSION, EMBED_DIMENSION), EMBED_DIMENSION ** -0.5, 0.1875, ((0, 32),))
    return dict(incoming_activations=incoming_activations, wkv_preceding_entry=wkv_preceding_entry, feedforward_preceding_entry=feedforward_preceding_entry, preceding_partition_memory=preceding_partition_memory, upstream_sensitivity=upstream_sensitivity, opening_standardize_scale=opening_standardize_scale, opening_standardize_shift=opening_standardize_shift, wkv_lag_blends=wkv_lag_blends, accept_projection=accept_projection, lookup_projection=lookup_projection, content_projection=content_projection, gating_projection=gating_projection, logarithmic_fading_factors=logarithmic_fading_factors, present_entry_reward=present_entry_reward, cluster_standardize_scale=cluster_standardize_scale, cluster_standardize_shift=cluster_standardize_shift, emission_projection=emission_projection, closing_standardize_scale=closing_standardize_scale, closing_standardize_shift=closing_standardize_shift, feedforward_lag_blends=feedforward_lag_blends, feedforward_lookup_projection=feedforward_lookup_projection, feedforward_content_projection=feedforward_content_projection, feedforward_accept_projection=feedforward_accept_projection)


@jax.custom_vjp
def low(v):
    return lax.optimization_barrier(v.astype(jnp.bfloat16)).astype(jnp.float32)

@jax.custom_vjp
def low_back(v):
    return v

def low_keep(v):
    return (low(v), None)

def low_pass(kept, grad):
    return (grad,)

def back_keep(v):
    return (v, None)

def back_low(kept, grad):
    return (low(grad),)
low.defvjp(low_keep, low_pass)
low_back.defvjp(back_keep, back_low)

def matmul(left_side, right_side):
    return jnp.dot(left_side, right_side, precision=lax.Precision.HIGHEST)

def layer_norm(matrix, norm_gain, norm_bias, epsilon):
    center = matrix - lax.optimization_barrier(jnp.mean(matrix, axis=-1, keepdims=True))
    spread = lax.optimization_barrier(jnp.mean(center * center, axis=-1, keepdims=True))
    return center * lax.rsqrt(spread + epsilon) * norm_gain + norm_bias

def mix_states(earlier, latter):
    decay_first, state_first = earlier
    decay_second, state_second = latter
    return (decay_first * decay_second, decay_second[..., None] * state_first + state_second)

def linear_scan_routine(accept_quantity, lookup_entries, content_entries, feature_fading_factor, reward_entries, starting_memory):
    head_count, length, head_width = accept_quantity.shape
    blocks = length // CH
    shaped = (head_count, blocks, CH, head_width)
    accept_single_entries = accept_quantity.reshape(shaped)
    lookup_single_entries = lookup_entries.reshape(shaped)
    value_b = content_entries.reshape(shaped)
    offsets = jnp.arange(CH, dtype=jnp.float32)[:, None]
    rates = feature_fading_factor[:, None, None, :]
    recept_dec = accept_single_entries * jnp.exp(-rates * offsets)
    key_up = lookup_single_entries * jnp.exp(rates * (offsets + 1.0))
    key_end = lookup_single_entries * jnp.exp(-rates * (CH - 1.0 - offsets))
    scores = jnp.einsum('hnti,hnsi->hnts', recept_dec, key_up, precision=lax.Precision.HIGHEST)
    earlier_mask = jnp.arange(CH)[:, None] > jnp.arange(CH)[None, :]
    scores = jnp.where(earlier_mask, scores, 0.0)
    selfpair_contribution = lax.optimization_barrier(jnp.sum(accept_single_entries * reward_entries[:, None, None, :] * lookup_single_entries, axis=-1))
    inside = jnp.einsum('hnts,hnsj->hntj', scores, value_b, precision=lax.Precision.HIGHEST) + selfpair_contribution[..., None] * value_b
    own_states = jnp.einsum('hnsi,hnsj->hnij', key_end, value_b, precision=lax.Precision.HIGHEST)
    block_decay = jnp.exp(-feature_fading_factor * CH)
    own_states = own_states.at[:, 0].add(block_decay[:, :, None] * starting_memory)
    decays = jnp.broadcast_to(block_decay[:, None, :], (head_count, blocks, head_width))
    products, states = lax.associative_scan(mix_states, (decays, own_states), axis=1)
    begins = jnp.concatenate([starting_memory[:, None], states[:, :-1]], axis=1)
    across = jnp.einsum('hnti,hnij->hntj', recept_dec, begins, precision=lax.Precision.HIGHEST)
    return ((inside + across).reshape(head_count, length, head_width), states[:, -1])

def layer(current, first_att, first_ffn, starting_memory, learnable_arrays):
    opening_standardize_scale, opening_standardize_shift, wkv_lag_blends, accept_projection, lookup_projection, content_projection, gating_projection, logarithmic_fading_factors, present_entry_reward, cluster_standardize_scale, cluster_standardize_shift, emission_projection, closing_standardize_scale, closing_standardize_shift, feedforward_lag_blends, feedforward_lookup_projection, feedforward_content_projection, feedforward_accept_projection = learnable_arrays
    length = current.shape[0]
    normed = layer_norm(current, opening_standardize_scale, opening_standardize_shift, 1e-05)
    before = jnp.concatenate([first_att[None, :], normed[:-1]], axis=0)
    mixed = [low(normed * wkv_lag_blends[:, column] + before * (1.0 - wkv_lag_blends[:, column])) for column in range(4)]
    accept_quantity = low_back(low(matmul(mixed[0], accept_projection)))
    lookup_entries = low_back(low(matmul(mixed[1], lookup_projection)))
    content_entries = low_back(low(matmul(mixed[2], content_projection)))
    gating = jax.nn.silu(low_back(matmul(mixed[3], gating_projection)))

    def divide_partitions(flat_rows):
        return flat_rows.reshape(length, WKV_PARTITIONS, SUBSPACE_EXTENT).transpose(1, 0, 2)
    feature_fading_factor = jnp.exp(logarithmic_fading_factors).reshape(WKV_PARTITIONS, SUBSPACE_EXTENT)
    blended_result, discarded_quantity = linear_scan_routine(divide_partitions(accept_quantity), divide_partitions(lookup_entries), divide_partitions(content_entries), feature_fading_factor, present_entry_reward.reshape(WKV_PARTITIONS, SUBSPACE_EXTENT), starting_memory)
    wkv = low_back(low(blended_result.transpose(1, 0, 2).reshape(length, EMBED_DIMENSION)))
    normalized = layer_norm(wkv.reshape(length, WKV_PARTITIONS, SUBSPACE_EXTENT), cluster_standardize_scale.reshape(WKV_PARTITIONS, SUBSPACE_EXTENT), cluster_standardize_shift.reshape(WKV_PARTITIONS, SUBSPACE_EXTENT), 0.00064).reshape(length, EMBED_DIMENSION)
    attended = low(normalized * gating)
    middle = current + low_back(matmul(attended, emission_projection))
    normed2 = layer_norm(middle, closing_standardize_scale, closing_standardize_shift, 1e-05)
    before2 = jnp.concatenate([first_ffn[None, :], normed2[:-1]], axis=0)
    mixed_key = low(normed2 * feedforward_lag_blends[:, 0] + before2 * (1.0 - feedforward_lag_blends[:, 0]))
    mixed_recv = low(normed2 * feedforward_lag_blends[:, 1] + before2 * (1.0 - feedforward_lag_blends[:, 1]))
    key_pre = low_back(matmul(mixed_key, feedforward_lookup_projection))
    hidden = low(jnp.square(jax.nn.relu(key_pre)))
    carried = low_back(matmul(hidden, feedforward_content_projection))
    recv_pre = low_back(matmul(mixed_recv, feedforward_accept_projection))
    return middle + jax.nn.sigmoid(recv_pre) * carried

def reference(incoming_activations, wkv_preceding_entry, feedforward_preceding_entry, preceding_partition_memory, upstream_sensitivity, opening_standardize_scale, opening_standardize_shift, wkv_lag_blends, accept_projection, lookup_projection, content_projection, gating_projection, logarithmic_fading_factors, present_entry_reward, cluster_standardize_scale, cluster_standardize_shift, emission_projection, closing_standardize_scale, closing_standardize_shift, feedforward_lag_blends, feedforward_lookup_projection, feedforward_content_projection, feedforward_accept_projection):
    learnable_arrays = tuple((linear_coefficients.astype(jnp.float32) for linear_coefficients in (opening_standardize_scale, opening_standardize_shift, wkv_lag_blends, accept_projection, lookup_projection, content_projection, gating_projection, logarithmic_fading_factors, present_entry_reward, cluster_standardize_scale, cluster_standardize_shift, emission_projection, closing_standardize_scale, closing_standardize_shift, feedforward_lag_blends, feedforward_lookup_projection, feedforward_content_projection, feedforward_accept_projection)))

    def segment_step(cumulative_sums, items):
        current, first_att, first_ffn, starting_memory, seed_grad = items

        def forward(activ, weights):
            return layer(activ, first_att.astype(jnp.float32), first_ffn.astype(jnp.float32), starting_memory, weights)
        result, pullback = jax.vjp(forward, current.astype(jnp.float32), learnable_arrays)
        back_input, back_weights = pullback(seed_grad.astype(jnp.float32))
        cumulative_sums = jax.tree.map(jnp.add, cumulative_sums, back_weights)
        return (cumulative_sums, (result.astype(jnp.bfloat16), back_input.astype(jnp.bfloat16)))
    zero_grads = tuple((jnp.zeros_like(linear_coefficients) for linear_coefficients in learnable_arrays))
    cumulative_sums, outputs = lax.scan(segment_step, zero_grads, (incoming_activations, wkv_preceding_entry, feedforward_preceding_entry, preceding_partition_memory, upstream_sensitivity))
    block_result, argument_sensitivity = outputs
    opening_standardize_scale_sens, opening_standardize_shift_sens, wkv_blend_cotangent, accept_projection_sens, lookup_projection_sens, content_projection_sens, gating_projection_sens, logarithmic_fading_sens, sequence_reward_sens, cluster_standardize_scale_sens, cluster_standardize_shift_sens, emission_projection_sens, closing_standardize_scale_sens, closing_standardize_shift_sens, feedforward_blend_cotangent, feedforward_lookup_cotangent, feedforward_content_cotangent, feedforward_accept_cotangent = cumulative_sums
    return (block_result, argument_sensitivity, opening_standardize_scale_sens, opening_standardize_shift_sens, wkv_blend_cotangent, accept_projection_sens, lookup_projection_sens, content_projection_sens, gating_projection_sens, logarithmic_fading_sens, sequence_reward_sens, cluster_standardize_scale_sens, cluster_standardize_shift_sens, emission_projection_sens, closing_standardize_scale_sens, closing_standardize_shift_sens, feedforward_blend_cotangent, feedforward_lookup_cotangent, feedforward_content_cotangent, feedforward_accept_cotangent)
```

```python
import functools

import jax
import jax.numpy as jnp
from jax import lax
from jax.experimental import pallas as pl
from jax.experimental.pallas import tpu as pltpu
from jax.sharding import PartitionSpec as P

WKV_PARTITIONS = 16
SUBSPACE_EXTENT = 64
LANES = 128
MESH = pl.DeviceIdType.MESH
F32 = jnp.float32
BF16 = jnp.bfloat16
VMEM_LIMIT = 60 * 1024 * 1024


class Grid:
    def __init__(self, seq, batch):
        self.seq, self.batch = seq, batch
        if seq == 8 and batch == 4:
            digits = [("y", "seq", 4, 2), ("x", "seq", 2, 2), ("c", "seq", 1, 2), ("z", "batch", 1, 4)]
        elif seq == 16 and batch == 8:
            digits = [("y", "seq", 4, 4), ("x", "seq", 1, 4), ("z", "batch", 2, 4), ("c", "batch", 1, 2)]
        else:
            digits = [("y", "seq", 1, seq), ("x", "seq", 1, 1), ("z", "batch", 1, batch), ("c", "batch", 1, 1)]
        self.order = [name for name, *_ in digits]
        self.axis = {name: axis for name, axis, *_ in digits}
        self.stride = {name: stride for name, _, stride, _ in digits}
        self.size = {name: size for name, *_, size in digits}
        self.shape = tuple(self.size[name] for name in self.order)

    def place(self):
        index = {"seq": lax.axis_index("seq"), "batch": lax.axis_index("batch")}
        return index, {
            name: (index[self.axis[name]] // self.stride[name]) % self.size[name] for name in self.order
        }

    def peer(self, index, digit, name, target):
        where = dict(index)
        axis = self.axis[name]
        where[axis] = index[axis] + (target - digit[name]) * self.stride[name]
        return (where["seq"], where["batch"])

    def at(self, ref, gone="", **fixed):
        return ref.at[tuple(fixed.get(name, slice(None)) for name in self.order if name not in gone)]

    def sizes(self, gone=""):
        return tuple(self.size[name] for name in self.order if name not in gone)


def greet(peers):
    barrier = pltpu.get_barrier_semaphore()
    for peer in peers:
        pl.semaphore_signal(barrier, inc=1, device_id=peer, device_id_type=MESH)
    pl.semaphore_wait(barrier, len(peers))


def gather_kernel(grid, orders, *refs):
    count = len(orders)
    shards, fulls = refs[:count], refs[count : 2 * count]
    own_sem, send_sem, recv_sem = refs[2 * count :]
    index, digit = grid.place()

    def others(name):
        return [(j, lax.rem(digit[name] + j, grid.size[name])) for j in range(1, grid.size[name])]

    greet([grid.peer(index, digit, name, t) for name in grid.order for _, t in others(name)])

    started = []

    def send(chunk, source, place, name):
        copies = []
        for j, target in others(name):
            slot = len(started)
            copy = pltpu.make_async_remote_copy(
                src_ref=source,
                dst_ref=place,
                send_sem=send_sem.at[slot],
                recv_sem=recv_sem.at[slot],
                device_id=grid.peer(index, digit, name, target),
                device_id_type=MESH,
            )
            copy.start()
            started.append(copy)
            copies.append(copy)
        return copies

    pending = {}
    own = {}

    def stage(chunk, number):
        full = fulls[chunk]
        first, second = orders[chunk]
        if number == 0:
            place = grid.at(full, **digit)
            copy = pltpu.make_async_copy(shards[chunk], place, own_sem.at[chunk])
            copy.start()
            own[chunk] = copy
            pending[chunk] = send(chunk, shards[chunk], place, "z")
            return
        for copy in pending[chunk]:
            copy.wait_recv()
        if number == 1:
            own[chunk].wait()
            fixed = {n: digit[n] for n in ("x", "y", "c")}
            name = first
        elif number == 2:
            fixed = {n: digit[n] for n in (second, "c")}
            name = second
        elif number == 3:
            fixed = {"c": digit["c"]}
            name = "c"
        else:
            return
        place = grid.at(full, **fixed)
        pending[chunk] = send(chunk, place, place, name)

    for chunk in range(count):
        stage(chunk, 0)
    for tick in range(count + 3):
        for number in (1, 2, 3, 4):
            chunk = tick - (number - 1)
            if 0 <= chunk < count:
                stage(chunk, number)
    for copy in started:
        copy.wait_send()


def gather_all(grid, shards, orders):
    count = len(shards)
    steps = count * sum(size - 1 for size in grid.shape)
    anywhere = pl.BlockSpec(memory_space=pl.ANY)
    return pl.pallas_call(
        functools.partial(gather_kernel, grid, orders),
        out_shape=[jax.ShapeDtypeStruct(grid.shape + s.shape, s.dtype) for s in shards],
        in_specs=[anywhere] * count,
        out_specs=[anywhere] * count,
        scratch_shapes=[
            pltpu.SemaphoreType.DMA((count,)),
            pltpu.SemaphoreType.DMA((steps,)),
            pltpu.SemaphoreType.DMA((steps,)),
        ],
        compiler_params=pltpu.CompilerParams(collective_id=0, has_side_effects=True),
    )(*shards)


def scatter_kernel(grid, chunks, *refs):
    count = len(chunks)
    parts, outs = refs[:count], refs[count : 2 * count]
    mine, rc, rx, ry, rz = (refs[2 * count + i * count : 2 * count + (i + 1) * count] for i in range(5))
    own_sem, send_sem, recv_sem = refs[7 * count :]
    index, digit = grid.place()

    def others(name):
        return [(j, lax.rem(digit[name] + j, grid.size[name])) for j in range(1, grid.size[name])]

    greet([grid.peer(index, digit, name, t) for name in grid.order for _, t in others(name)])
    started = []

    def send(source, gone, name, slots):
        copies = []
        for j, target in others(name):
            slot = len(started)
            copy = pltpu.make_async_remote_copy(
                src_ref=grid.at(source, gone, **{name: target}),
                dst_ref=slots.at[j - 1],
                send_sem=send_sem.at[slot],
                recv_sem=recv_sem.at[slot],
                device_id=grid.peer(index, digit, name, target),
                device_id_type=MESH,
            )
            copy.start()
            started.append(copy)
            copies.append(copy)
        return copies

    pending, own = {}, {}

    def total(target, terms, shape):
        steps = 1
        for size in shape:
            steps *= size

        def body(i, carry):
            where, rest = [], i
            for size in reversed(shape):
                where.append(lax.rem(rest, size))
                rest = lax.div(rest, size)
            where = tuple(reversed(where))
            value = terms[0](where).astype(F32)
            for term in terms[1:]:
                value = value + term(where).astype(F32)
            target(where, value)
            return carry

        lax.fori_loop(0, steps, body, 0)

    def picker(ref, gone, name):
        names = [n for n in grid.order if n not in gone and n != name]

        def read(where):
            at = dict(zip(names, where))
            at[name] = digit[name]
            return ref[tuple(at[n] for n in grid.order if n not in gone)]

        return read

    def slot_reader(slots, j):
        return lambda where: slots[(j,) + where]

    def stage(chunk, number):
        first, second = chunks[chunk]
        if number == 0:
            copy = pltpu.make_async_copy(grid.at(parts[chunk], c=digit["c"]), mine[chunk], own_sem.at[chunk])
            copy.start()
            own[chunk] = copy
            pending[chunk] = send(parts[chunk], "", "c", rc[chunk])
            return
        for copy in pending[chunk]:
            copy.wait_recv()
        if number == 1:
            own[chunk].wait()
            m = mine[chunk]

            def put(where, value):
                m[where] = value.astype(m.dtype)

            if grid.size["c"] > 1:
                total(put, [lambda where: m[where]] + [slot_reader(rc[chunk], j) for j in range(grid.size["c"] - 1)], grid.sizes("c"))
            pending[chunk] = send(m, "c", first, (rx if first == "x" else ry)[chunk])
        elif number == 2:
            m, slots = mine[chunk], (rx if first == "x" else ry)[chunk]

            def put(where, value):
                slots[(0,) + where] = value.astype(slots.dtype)

            total(put, [picker(m, "c", first)] + [slot_reader(slots, j) for j in range(grid.size[first] - 1)], grid.sizes("c" + first))
            pending[chunk] = send(slots.at[0], "c" + first, second, (rx if second == "x" else ry)[chunk])
        elif number == 3:
            before, slots = (rx if first == "x" else ry)[chunk].at[0], (rx if second == "x" else ry)[chunk]

            def put(where, value):
                slots[(0,) + where] = value.astype(slots.dtype)

            total(put, [picker(before, "c" + first, second)] + [slot_reader(slots, j) for j in range(grid.size[second] - 1)], grid.sizes("cxy"))
            pending[chunk] = send(slots.at[0], "cxy", "z", rz[chunk])
        elif number == 4:
            before, slots = (rx if second == "x" else ry)[chunk].at[0], rz[chunk]
            value = before[digit["z"]].astype(F32)
            for j in range(grid.size["z"] - 1):
                value = value + slots[j].astype(F32)
            outs[chunk][...] = value

    for chunk in range(count):
        stage(chunk, 0)
    for tick in range(count + 3):
        for number in (1, 2, 3, 4):
            chunk = tick - (number - 1)
            if 0 <= chunk < count:
                stage(chunk, number)
    for copy in started:
        copy.wait_send()


def scatter_all(grid, parts, chunks):
    count = len(parts)
    steps = count * sum(size - 1 for size in grid.shape)
    anywhere = pl.BlockSpec(memory_space=pl.ANY)
    mine, rc, rx, ry, rz = [], [], [], [], []
    for part, (first, second) in zip(parts, chunks):
        tile, kind = part.shape[4:], part.dtype
        mine.append(pltpu.VMEM(grid.sizes("c") + tile, kind))
        rc.append(pltpu.VMEM((max(grid.size["c"] - 1, 1),) + grid.sizes("c") + tile, kind))
        shapes = {
            first: pltpu.VMEM((max(grid.size[first] - 1, 1),) + grid.sizes("c" + first) + tile, kind),
            second: pltpu.VMEM((max(grid.size[second] - 1, 1),) + grid.sizes("cxy") + tile, kind),
        }
        rx.append(shapes["x"])
        ry.append(shapes["y"])
        rz.append(pltpu.VMEM((max(grid.size["z"] - 1, 1),) + tile, kind))
    return pl.pallas_call(
        functools.partial(scatter_kernel, grid, chunks),
        out_shape=[jax.ShapeDtypeStruct(p.shape[4:], F32) for p in parts],
        in_specs=[anywhere] * count,
        out_specs=[pl.BlockSpec(memory_space=pltpu.VMEM)] * count,
        scratch_shapes=mine + rc + rx + ry + rz + [
            pltpu.SemaphoreType.DMA((count,)),
            pltpu.SemaphoreType.DMA((steps,)),
            pltpu.SemaphoreType.DMA((steps,)),
        ],
        compiler_params=pltpu.CompilerParams(
            collective_id=1, has_side_effects=True, vmem_limit_bytes=VMEM_LIMIT
        ),
    )(*parts)


def dot(a, b, da, db):
    return lax.dot_general(a, b, (((da,), (db,)), ((), ())), preferred_element_type=F32)


PRECISE = dict(score=1, inner=1, cross=1, own=1, back=1)


def parts_of(value):
    high = value.astype(BF16)
    return high, (value - high.astype(F32)).astype(BF16)


def dot2(a, b, da, db, name):
    if not PRECISE[name]:
        return dot(a.astype(BF16), b, da, db)
    high, low = parts_of(a)
    return dot(high, b, da, db) + dot(low, b, da, db)


def dot3(a, b, da, db, name):
    if not PRECISE[name]:
        return dot(a.astype(BF16), b.astype(BF16), da, db)
    a_high, a_low = parts_of(a)
    b_high, b_low = parts_of(b)
    return dot(a_high, b_high, da, db) + (dot(a_low, b_high, da, db) + dot(a_high, b_low, da, db))


def half_masks(rows):
    lane = lax.broadcasted_iota(jnp.int32, (rows, LANES), 1)
    return lane < SUBSPACE_EXTENT


def block_ones(kind):
    row = lax.broadcasted_iota(jnp.int32, (LANES, LANES), 0) // SUBSPACE_EXTENT
    lane = lax.broadcasted_iota(jnp.int32, (LANES, LANES), 1) // SUBSPACE_EXTENT
    return (row == lane).astype(kind)


def head_sum(value, ones):
    high = value.astype(BF16)
    low = (value - high.astype(F32)).astype(BF16)
    return dot(high, ones, 1, 0) + dot(low, ones, 1, 0)


def decays(rate, length):
    step = lax.broadcasted_iota(jnp.int32, (length, LANES), 0).astype(F32)
    return jnp.exp(-rate * step), jnp.exp(rate * (step + 1.0)), jnp.exp(-rate * (length - 1.0 - step))


def fold(first, second, ones):
    pick = half_masks(LANES)
    a, b = first * ones, second * ones
    a = a + pltpu.roll(a, SUBSPACE_EXTENT, 1)
    b = b + pltpu.roll(b, SUBSPACE_EXTENT, 1)
    return jnp.where(pick, a, b)


def unfold(both, segment, ones):
    pick = half_masks(LANES)
    turned = pltpu.roll(both, SUBSPACE_EXTENT, 1)
    full = jnp.where(pick, both, turned) if segment == 0 else jnp.where(pick, turned, both)
    return full * ones


def exchange(grid, index, source, slots, rows, send_sem, recv_sem):
    me, copies = index["seq"], []
    for j in range(1, grid.seq):
        target = lax.rem(me + j, grid.seq)
        copy = pltpu.make_async_remote_copy(
            src_ref=source.at[pl.ds(pl.multiple_of(target * rows, 16), rows)],
            dst_ref=slots.at[pl.ds(pl.multiple_of(me * rows, 16), rows)],
            send_sem=send_sem.at[j - 1],
            recv_sem=recv_sem.at[j - 1],
            device_id=(target, index["batch"]),
            device_id_type=MESH,
        )
        copy.start()
        copies.append(copy)
    here = pl.ds(pl.multiple_of(me * rows, 16), rows)
    slots[here, :] = source[here, :]
    return copies


def wkv_forward_kernel(
    grid, length,
    r_ref, k_ref, v_ref, gate_ref, rate_ref, reward_ref, gain_ref, bias_ref, start_ref, fade_ref,
    wkv_ref, attended_ref, begin_ref,
    own_ref, got_ref, out_ref, inner_ref, send_a, recv_a, send_b, recv_b,
):
    index, _ = grid.place()
    me = index["seq"]
    greet([(lax.rem(me + j, grid.seq), index["batch"]) for j in range(1, grid.seq)])
    width = r_ref.shape[1]
    pairs, rows = width // LANES, width // grid.seq
    ones, ones16 = block_ones(F32), block_ones(BF16)

    def columns(p):
        return pl.ds(pl.multiple_of(p * LANES, LANES), LANES)

    def own_states(p, carry):
        _, _, end = decays(rate_ref[:, columns(p)], length)
        both = []
        for q in range(2):
            token = pl.ds(q * length, length)
            k_end = k_ref[token, columns(p)].astype(F32) * end
            both.append(dot2(k_end, v_ref[token, columns(p)], 0, 0, "own"))
        own_ref[columns(p), :] = fold(both[0], both[1], ones).astype(BF16)
        return carry

    lax.fori_loop(0, pairs, own_states, 0)
    first = exchange(grid, index, own_ref, got_ref, rows, send_a, recv_a)

    later = lax.broadcasted_iota(jnp.int32, (length, length), 0) > lax.broadcasted_iota(
        jnp.int32, (length, length), 1
    )

    def inside(p, carry):
        down, up, _ = decays(rate_ref[:, columns(p)], length)
        pick = half_masks(length)
        for q in range(2):
            token = pl.ds(q * length, length)
            r = r_ref[token, columns(p)].astype(F32)
            k = k_ref[token, columns(p)].astype(F32)
            v = v_ref[token, columns(p)]
            r_down = r * down
            k_up = k * up
            halves = []
            for h in range(2):
                r_head = jnp.where(pick == (h == 0), r_down, 0.0)
                scores = jnp.where(later, dot3(r_head, k_up, 1, 1, "score"), 0.0)
                halves.append(dot2(scores, v, 1, 0, "inner"))
            inner = jnp.where(pick, halves[0], halves[1])
            self_part = head_sum(r * reward_ref[:, columns(p)] * k, ones16)
            inner_ref[token, columns(p)] = inner + self_part * v.astype(F32)
        return carry

    lax.fori_loop(0, pairs, inside, 0)

    for copy in first:
        copy.wait_recv()
    state = start_ref[...]
    fade = fade_ref[...]
    for block in range(grid.seq):
        at = pl.ds(block * rows, rows)
        out_ref[at, :] = state.astype(BF16)
        state = fade * state + got_ref[at, :].astype(F32)
    second = exchange(grid, index, out_ref, begin_ref, rows, send_b, recv_b)
    for copy in second:
        copy.wait_recv()

    def across(p, carry):
        down, _, _ = decays(rate_ref[:, columns(p)], length)
        begin = begin_ref[columns(p), :].astype(F32)
        for q in range(2):
            token = pl.ds(q * length, length)
            r_down = r_ref[token, columns(p)].astype(F32) * down
            state16 = unfold(begin, q, ones).astype(BF16)
            y = (inner_ref[token, columns(p)] + dot2(r_down, state16, 1, 0, "cross")).astype(BF16)
            wkv_ref[token, columns(p)] = y
            center = y.astype(F32) - dot(y, ones16, 1, 0) * (1.0 / SUBSPACE_EXTENT)
            spread = head_sum(center * center, ones16) * (1.0 / SUBSPACE_EXTENT)
            z = center * lax.rsqrt(spread + 0.00064)
            normalized = z * gain_ref[:, columns(p)] + bias_ref[:, columns(p)]
            g = gate_ref[token, columns(p)]
            attended_ref[token, columns(p)] = (normalized * g / (1.0 + jnp.exp(-g))).astype(BF16)
        return carry

    lax.fori_loop(0, pairs, across, 0)
    for copy in first + second:
        copy.wait_send()


def wkv_forward(grid, r, k, v, gate_pre, rate, reward, gain, bias, start, fade):
    tokens, width = r.shape
    state = pltpu.VMEM((width, LANES), BF16)
    sems = pltpu.SemaphoreType.DMA((grid.seq - 1,))
    vmem = pl.BlockSpec(memory_space=pltpu.VMEM)
    return pl.pallas_call(
        functools.partial(wkv_forward_kernel, grid, tokens // 2),
        out_shape=[
            jax.ShapeDtypeStruct((tokens, width), BF16),
            jax.ShapeDtypeStruct((tokens, width), BF16),
            jax.ShapeDtypeStruct((width, LANES), BF16),
        ],
        in_specs=[vmem] * 10,
        out_specs=[vmem] * 3,
        scratch_shapes=[state, state, state, pltpu.VMEM((tokens, width), F32), sems, sems, sems, sems],
        compiler_params=pltpu.CompilerParams(
            collective_id=2, has_side_effects=True, vmem_limit_bytes=VMEM_LIMIT
        ),
    )(r, k, v, gate_pre, rate, reward, gain, bias, start, fade)


def wkv_backward_kernel(
    grid, length,
    r_ref, k_ref, v_ref, gate_ref, wkv_ref, d_att_ref, rate_ref, reward_ref, gain_ref, bias_ref, fade_ref, begin_ref,
    d_gate_ref, dr_ref, dk_ref, dv_ref, sums_ref,
    dy_ref, own_ref, got_ref, out_ref, end_ref, send_a, recv_a, send_b, recv_b,
):
    index, _ = grid.place()
    me = index["seq"]
    greet([(lax.rem(me + j, grid.seq), index["batch"]) for j in range(1, grid.seq)])
    width = r_ref.shape[1]
    pairs, rows = width // LANES, width // grid.seq
    ones, ones16 = block_ones(F32), block_ones(BF16)
    share = 1.0 / SUBSPACE_EXTENT

    def columns(p):
        return pl.ds(pl.multiple_of(p * LANES, LANES), LANES)

    def own_states(p, carry):
        down, _, _ = decays(rate_ref[:, columns(p)], length)
        both = []
        gain_sum, bias_sum = jnp.zeros((1, LANES), F32), jnp.zeros((1, LANES), F32)
        for q in range(2):
            token = pl.ds(q * length, length)
            y = wkv_ref[token, columns(p)]
            center = y.astype(F32) - dot(y, ones16, 1, 0) * share
            spread = head_sum(center * center, ones16) * share
            scale = lax.rsqrt(spread + 0.00064)
            z = center * scale
            gain = gain_ref[:, columns(p)]
            normalized = z * gain + bias_ref[:, columns(p)]
            g = gate_ref[token, columns(p)]
            s = 1.0 / (1.0 + jnp.exp(-g))
            d_att = d_att_ref[token, columns(p)]
            d_gate_ref[token, columns(p)] = (d_att * normalized * s * (1.0 + g * (1.0 - s))).astype(BF16)
            d_norm = d_att * g * s
            gain_sum = gain_sum + jnp.sum(d_norm * z, axis=0, keepdims=True)
            bias_sum = bias_sum + jnp.sum(d_norm, axis=0, keepdims=True)
            e = d_norm * gain
            dy = ((e - head_sum(e, ones16) * share - z * (head_sum(e * z, ones16) * share)) * scale).astype(BF16)
            dy_ref[token, columns(p)] = dy
            r_down = r_ref[token, columns(p)].astype(F32) * down
            both.append(dot2(r_down, dy, 0, 0, "own"))
        sums_ref[0:1, columns(p)] = gain_sum
        sums_ref[1:2, columns(p)] = bias_sum
        own_ref[columns(p), :] = fold(both[0], both[1], ones).astype(BF16)
        return carry

    lax.fori_loop(0, pairs, own_states, 0)
    first = exchange(grid, index, own_ref, got_ref, rows, send_a, recv_a)
    for copy in first:
        copy.wait_recv()
    fade = fade_ref[...]
    state = jnp.zeros_like(fade)
    for block in reversed(range(grid.seq)):
        at = pl.ds(block * rows, rows)
        out_ref[at, :] = state.astype(BF16)
        state = fade * state + got_ref[at, :].astype(F32)
    second = exchange(grid, index, out_ref, end_ref, rows, send_b, recv_b)
    for copy in second:
        copy.wait_recv()

    later = lax.broadcasted_iota(jnp.int32, (length, length), 0) > lax.broadcasted_iota(
        jnp.int32, (length, length), 1
    )
    step = lax.broadcasted_iota(jnp.int32, (length, LANES), 0).astype(F32)

    def inside(p, carry):
        rate = rate_ref[:, columns(p)]
        reward = reward_ref[:, columns(p)]
        down, up, end = decays(rate, length)
        pick = half_masks(length)
        begins, ends = begin_ref[columns(p), :].astype(F32), end_ref[columns(p), :].astype(F32)
        reward_sum, rate_sum = jnp.zeros((1, LANES), F32), jnp.zeros((1, LANES), F32)
        for q in range(2):
            token = pl.ds(q * length, length)
            r = r_ref[token, columns(p)].astype(F32)
            k = k_ref[token, columns(p)].astype(F32)
            v = v_ref[token, columns(p)]
            dy = dy_ref[token, columns(p)]
            begin, finish = unfold(begins, q, ones), unfold(ends, q, ones)
            begin16, finish16 = begin.astype(BF16), finish.astype(BF16)
            r_down = r * down
            k_up = k * up
            k_end = k * end
            if not PRECISE["back"]:
                r_down = r_down.astype(BF16).astype(F32)
                k_up = k_up.astype(BF16).astype(F32)
                k_end = k_end.astype(BF16).astype(F32)
            d_r, d_k, d_v = [], [], []
            for h in range(2):
                r_head = jnp.where(pick == (h == 0), r_down, 0.0)
                dy_head = jnp.where(pick == (h == 0), dy.astype(F32), 0.0).astype(BF16)
                scores = jnp.where(later, dot3(r_head, k_up, 1, 1, "score"), 0.0)
                d_scores = jnp.where(later, dot(dy_head, v, 1, 1), 0.0)
                d_r.append(dot3(d_scores, k_up, 1, 0, "back"))
                d_k.append(dot3(d_scores, r_down, 0, 0, "back"))
                d_v.append(dot2(scores, dy, 0, 0, "inner"))
            from_r = jnp.where(pick, d_r[0], d_r[1]) + dot(dy, begin16, 1, 1)
            from_k = jnp.where(pick, d_k[0], d_k[1])
            from_end = dot(v, finish16, 1, 1)
            v32, dy32 = v.astype(F32), dy.astype(F32)
            v_dy = head_sum(v32 * dy32, ones16)
            self_part = head_sum(r * reward * k, ones16)
            dr_ref[token, columns(p)] = (from_r * down + reward * k * v_dy).astype(BF16)
            dk_ref[token, columns(p)] = (from_k * up + from_end * end + reward * r * v_dy).astype(BF16)
            dv_ref[token, columns(p)] = (
                jnp.where(pick, d_v[0], d_v[1]) + dot2(k_end, finish16, 1, 0, "cross") + self_part * dy32
            ).astype(BF16)
            reward_sum = reward_sum + jnp.sum(r * k * v_dy, axis=0, keepdims=True)
            terms = (
                (step + 1.0) * k_up * from_k
                - step * r_down * from_r
                - (length - 1.0 - step) * k_end * from_end
            )
            through = lax.dot_general(
                jnp.ones((8, LANES), F32), begin * finish, (((1,), (1,)), ((), ())),
                precision=lax.Precision.HIGHEST, preferred_element_type=F32,
            )[0:1, :]
            rate_sum = rate_sum + jnp.sum(terms, axis=0, keepdims=True) - length * jnp.exp(-rate * length) * through
        sums_ref[2:3, columns(p)] = reward_sum
        sums_ref[3:4, columns(p)] = rate_sum * rate
        return carry

    lax.fori_loop(0, pairs, inside, 0)
    sums_ref[4:8, :] = jnp.zeros((4, width), F32)
    for copy in first + second:
        copy.wait_send()


def wkv_backward(grid, r, k, v, gate_pre, wkv, d_att, rate, reward, gain, bias, fade, begin):
    tokens, width = r.shape
    state = pltpu.VMEM((width, LANES), BF16)
    sems = pltpu.SemaphoreType.DMA((grid.seq - 1,))
    vmem = pl.BlockSpec(memory_space=pltpu.VMEM)
    flat = jax.ShapeDtypeStruct((tokens, width), BF16)
    return pl.pallas_call(
        functools.partial(wkv_backward_kernel, grid, tokens // 2),
        out_shape=[flat, flat, flat, flat, jax.ShapeDtypeStruct((8, width), F32)],
        in_specs=[vmem] * 12,
        out_specs=[vmem] * 5,
        scratch_shapes=[pltpu.VMEM((tokens, width), BF16), state, state, state, state, sems, sems, sems, sems],
        compiler_params=pltpu.CompilerParams(
            collective_id=3, has_side_effects=True, vmem_limit_bytes=VMEM_LIMIT
        ),
    )(r, k, v, gate_pre, wkv, d_att, rate, reward, gain, bias, fade, begin)


def shifted(block, axis, distance):
    devices = range(lax.axis_size(axis))
    route = [(i - distance, i) for i in devices if i - distance in devices]
    return lax.ppermute(block, axis, route)


def standardize(rows, epsilon):
    center = rows - jnp.mean(rows, axis=-1, keepdims=True)
    spread = jnp.mean(center * center, axis=-1, keepdims=True)
    scale = lax.rsqrt(spread + epsilon)
    return center * scale, scale


def back_standardize(e, z, scale):
    return (e - jnp.mean(e, axis=-1, keepdims=True) - z * jnp.mean(e * z, axis=-1, keepdims=True)) * scale


def project(rows, weights):
    return dot(rows, weights, 1, 0)


def outer(left_side, right_side):
    return dot(left_side, right_side, 0, 0).astype(BF16)


def back_through(grads, weights):
    return dot(grads, weights, 1, 1)


def local(grid, *args):
    (
        incoming, att_entry, ffn_entry, memory, upstream,
        ln1_gain, ln1_bias, att_mix, w_recept, w_key, w_value, w_gate, decay_log, reward,
        gn_gain, gn_bias, w_out, ln2_gain, ln2_bias, ffn_mix, f_key, f_value, f_recept,
    ) = args
    segments, length, width = incoming.shape
    tokens = segments * length
    ranks = grid.seq * grid.batch
    share = width // ranks
    is_first = lax.axis_index("seq") == 0

    small = jnp.stack(
        [ln1_gain, ln1_bias] + [att_mix[:, c] for c in range(4)] + [decay_log, reward, gn_gain, gn_bias, ln2_gain, ln2_bias]
        + [ffn_mix[:, c] for c in range(2)]
    )
    small = jnp.pad(small, ((0, 2), (0, LANES - share)))
    half = f_key.shape[1] // 2
    shards = [small, w_recept, w_key, w_value, w_gate, w_out, f_recept, f_key, f_value]
    orders = [("x", "y"), ("x", "y"), ("y", "x"), ("x", "y"), ("y", "x"), ("x", "y"), ("y", "x"), ("x", "y"), ("y", "x")]
    full = gather_all(grid, shards, orders)
    table = full[0].reshape(ranks, 16, LANES)[:, :14, :share].transpose(1, 0, 2).reshape(14, width).astype(F32)
    W_r, W_k, W_v, W_g, W_o, F_r, F_k, F_v = [
        w.reshape((ranks * w.shape[4], w.shape[5])) for w in full[1:]
    ]
    g1, b1 = table[0], table[1]
    mix1 = table[2:6]
    rate = jnp.exp(table[6])[None, :]
    bonus = table[7][None, :]
    gg, gb = table[8][None, :], table[9][None, :]
    g2, b2 = table[10], table[11]
    mix2 = table[12:14]

    x = incoming.astype(F32)
    z1, s1 = standardize(x, 1e-05)
    normed = z1 * g1 + b1
    arrived = shifted(normed[:, -1:], "seq", 1)
    previous = jnp.where(is_first, att_entry[:, None, :].astype(F32), arrived)
    before = jnp.concatenate([previous, normed[:, :-1]], axis=1)
    mixed = [
        (normed * mix1[c] + before * (1.0 - mix1[c])).astype(BF16).reshape(tokens, width) for c in range(4)
    ]
    r = project(mixed[0], W_r).astype(BF16)
    k = project(mixed[1], W_k).astype(BF16)
    v = project(mixed[2], W_v).astype(BF16)
    gate_pre = project(mixed[3], W_g)

    rows = width // grid.seq
    row = lax.axis_index("seq") * rows
    start = memory.transpose(1, 2, 0, 3).reshape(width, segments * SUBSPACE_EXTENT)
    start = lax.dynamic_slice_in_dim(start, row, rows, 0)
    own_rate = lax.dynamic_slice_in_dim(rate[0], row, rows, 0)
    fade = jnp.broadcast_to(jnp.exp(-own_rate * length)[:, None], (rows, LANES))
    wkv, attended, begin = wkv_forward(grid, r, k, v, gate_pre, rate, bonus, gg, gb, start, fade)

    middle = x.reshape(tokens, width) + project(attended, W_o)
    middle = middle.reshape(segments, length, width)
    z2, s2 = standardize(middle, 1e-05)
    normed2 = z2 * g2 + b2
    arrived2 = shifted(normed2[:, -1:], "seq", 1)
    previous2 = jnp.where(is_first, ffn_entry[:, None, :].astype(F32), arrived2)
    before2 = jnp.concatenate([previous2, normed2[:, :-1]], axis=1)
    mixed2 = [
        (normed2 * mix2[c] + before2 * (1.0 - mix2[c])).astype(BF16).reshape(tokens, width) for c in range(2)
    ]
    key_pos = jnp.maximum(project(mixed2[0], F_k), 0.0)
    hidden = (key_pos * key_pos).astype(BF16)
    carried = project(hidden, F_v)
    recv = jax.nn.sigmoid(project(mixed2[1], F_r))
    result = (middle.reshape(tokens, width) + recv * carried).astype(BF16)

    d_out = upstream.astype(F32).reshape(tokens, width)
    d_carried = (recv * d_out).astype(BF16)
    d_recv = (recv * (1.0 - recv) * carried * d_out).astype(BF16)
    grad_f_value = outer(hidden, d_carried)
    grad_f_recept = outer(mixed2[1], d_recv)
    d_key = (2.0 * key_pos * back_through(d_carried, F_v)).astype(BF16)
    grad_f_key = outer(mixed2[0], d_key)
    d_mixed2 = [
        back_through(d_key, F_k).reshape(segments, length, width),
        back_through(d_recv, F_r).reshape(segments, length, width),
    ]
    difference2 = normed2 - before2
    d_mix2 = [jnp.sum(difference2 * d, axis=(0, 1)) for d in d_mixed2]
    d_before2 = sum((1.0 - mix2[c]) * d_mixed2[c] for c in range(2))
    from_next2 = shifted(d_before2[:, :1], "seq", -1)
    d_normed2 = sum(mix2[c] * d_mixed2[c] for c in range(2)) + jnp.concatenate([d_before2[:, 1:], from_next2], axis=1)
    d_g2 = jnp.sum(z2 * d_normed2, axis=(0, 1))
    d_b2 = jnp.sum(d_normed2, axis=(0, 1))
    d_middle = d_out.reshape(segments, length, width) + back_standardize(d_normed2 * g2, z2, s2)
    d_branch = d_middle.astype(BF16).reshape(tokens, width)
    grad_out = outer(attended, d_branch)
    d_attended = back_through(d_branch, W_o)
    d_gate, d_r, d_k, d_v, sums = wkv_backward(
        grid, r, k, v, gate_pre, wkv, d_attended, rate, bonus, gg, gb, fade, begin
    )
    grad_r, grad_k, grad_v, grad_g = [
        outer(m, d) for m, d in zip(mixed, (d_r, d_k, d_v, d_gate))
    ]
    d_mixed = [
        back_through(d, w).reshape(segments, length, width)
        for d, w in zip((d_r, d_k, d_v, d_gate), (W_r, W_k, W_v, W_g))
    ]
    difference = normed - before
    d_mix1 = [jnp.sum(difference * d, axis=(0, 1)) for d in d_mixed]
    d_before = sum((1.0 - mix1[c]) * d_mixed[c] for c in range(4))
    from_next = shifted(d_before[:, :1], "seq", -1)
    d_normed = sum(mix1[c] * d_mixed[c] for c in range(4)) + jnp.concatenate([d_before[:, 1:], from_next], axis=1)
    d_g1 = jnp.sum(z1 * d_normed, axis=(0, 1))
    d_b1 = jnp.sum(d_normed, axis=(0, 1))
    d_input = (d_middle + back_standardize(d_normed * g1, z1, s1)).astype(BF16)

    rows_of = [d_g1, d_b1] + d_mix1 + [sums[3], sums[2], sums[0], sums[1], d_g2, d_b2] + d_mix2
    small_grad = jnp.stack(rows_of).reshape(14, ranks, share).transpose(1, 0, 2)
    small_grad = jnp.pad(small_grad, ((0, 0), (0, 2), (0, LANES - share))).reshape(grid.shape + (16, LANES))
    parts = [
        g.reshape(grid.shape + (g.shape[0] // ranks, g.shape[1]))
        for g in (grad_f_value, grad_f_key, grad_f_recept, grad_out, grad_g, grad_r, grad_k, grad_v)
    ] + [small_grad]
    chunks = [("x", "y"), ("y", "x"), ("x", "y"), ("y", "x"), ("x", "y"), ("y", "x"), ("x", "y"), ("y", "x"), ("x", "y")]
    s_fv, s_fk, s_fr, s_o, s_g, s_r, s_k, s_v, s_small = scatter_all(grid, parts, chunks)
    s = s_small[:14, :share]
    shape = incoming.shape
    return (
        result.reshape(shape), d_input.reshape(shape),
        s[0], s[1], s[2:6].T, s_r, s_k, s_v, s_g, s[6], s[7], s[8], s[9], s_o, s[10], s[11], s[12:14].T,
        s_fk, s_fv, s_fr,
    )


def solution(mesh):
    grid = Grid(mesh.shape["seq"], mesh.shape["batch"])
    both, rows = P(("seq", "batch")), P(("seq", "batch"), None)
    tokens, entry = P("batch", "seq", None), P("batch", None)
    return jax.shard_map(
        functools.partial(local, grid),
        mesh=mesh,
        in_specs=(
            tokens, entry, entry, P("batch", None, None, None), tokens,
            both, both, rows, rows, rows, rows, rows, both, both, both, both, rows, both, both, rows, rows, rows, rows,
        ),
        out_specs=(
            tokens, tokens, both, both, rows, rows, rows, rows, rows, both, both, both, both, rows, both, both, rows,
            rows, rows, rows,
        ),
        check_vma=False,
    )
```

```python
import functools

import jax
import jax.numpy as jnp
from jax import lax
from jax.experimental import pallas as pl
from jax.experimental.pallas import tpu as pltpu
from jax.sharding import PartitionSpec as P

WKV_PARTITIONS = 16
SUBSPACE_EXTENT = 64
LANES = 128
MESH = pl.DeviceIdType.MESH
F32 = jnp.float32
BF16 = jnp.bfloat16
VMEM_LIMIT = 60 * 1024 * 1024


class Grid:
    def __init__(self, seq, batch):
        self.seq, self.batch = seq, batch
        if seq == 8 and batch == 4:
            digits = [("y", "seq", 4, 2), ("x", "seq", 2, 2), ("c", "seq", 1, 2), ("z", "batch", 1, 4)]
        elif seq == 16 and batch == 8:
            digits = [("y", "seq", 4, 4), ("x", "seq", 1, 4), ("z", "batch", 2, 4), ("c", "batch", 1, 2)]
        else:
            digits = [("y", "seq", 1, seq), ("x", "seq", 1, 1), ("z", "batch", 1, batch), ("c", "batch", 1, 1)]
        self.order = [name for name, *_ in digits]
        self.axis = {name: axis for name, axis, *_ in digits}
        self.stride = {name: stride for name, _, stride, _ in digits}
        self.size = {name: size for name, *_, size in digits}
        self.shape = tuple(self.size[name] for name in self.order)

    def place(self):
        index = {"seq": lax.axis_index("seq"), "batch": lax.axis_index("batch")}
        return index, {
            name: (index[self.axis[name]] // self.stride[name]) % self.size[name] for name in self.order
        }

    def peer(self, index, digit, name, target):
        where = dict(index)
        axis = self.axis[name]
        where[axis] = index[axis] + (target - digit[name]) * self.stride[name]
        return (where["seq"], where["batch"])

    def at(self, ref, gone="", **fixed):
        return ref.at[tuple(fixed.get(name, slice(None)) for name in self.order if name not in gone)]

    def sizes(self, gone=""):
        return tuple(self.size[name] for name in self.order if name not in gone)


def greet(peers):
    barrier = pltpu.get_barrier_semaphore()
    for peer in peers:
        pl.semaphore_signal(barrier, inc=1, device_id=peer, device_id_type=MESH)
    pl.semaphore_wait(barrier, len(peers))


def scatter_kernel(grid, chunks, *refs):
    count = len(chunks)
    parts, outs = refs[:count], refs[count : 2 * count]
    mine, rc, rx, ry, rz = (refs[2 * count + i * count : 2 * count + (i + 1) * count] for i in range(5))
    own_sem, send_sem, recv_sem = refs[7 * count :]
    index, digit = grid.place()

    def others(name):
        return [(j, lax.rem(digit[name] + j, grid.size[name])) for j in range(1, grid.size[name])]

    greet([grid.peer(index, digit, name, t) for name in grid.order for _, t in others(name)])
    started = []

    def send(source, gone, name, slots):
        copies = []
        for j, target in others(name):
            slot = len(started)
            copy = pltpu.make_async_remote_copy(
                src_ref=grid.at(source, gone, **{name: target}),
                dst_ref=slots.at[j - 1],
                send_sem=send_sem.at[slot],
                recv_sem=recv_sem.at[slot],
                device_id=grid.peer(index, digit, name, target),
                device_id_type=MESH,
            )
            copy.start()
            started.append(copy)
            copies.append(copy)
        return copies

    pending, own = {}, {}

    def total(target, terms, shape):
        steps = 1
        for size in shape:
            steps *= size

        def body(i, carry):
            where, rest = [], i
            for size in reversed(shape):
                where.append(lax.rem(rest, size))
                rest = lax.div(rest, size)
            where = tuple(reversed(where))
            value = terms[0](where).astype(F32)
            for term in terms[1:]:
                value = value + term(where).astype(F32)
            target(where, value)
            return carry

        lax.fori_loop(0, steps, body, 0)

    def picker(ref, gone, name):
        names = [n for n in grid.order if n not in gone and n != name]

        def read(where):
            at = dict(zip(names, where))
            at[name] = digit[name]
            return ref[tuple(at[n] for n in grid.order if n not in gone)]

        return read

    def slot_reader(slots, j):
        return lambda where: slots[(j,) + where]

    def stage(chunk, number):
        first, second = chunks[chunk]
        if number == 0:
            copy = pltpu.make_async_copy(grid.at(parts[chunk], c=digit["c"]), mine[chunk], own_sem.at[chunk])
            copy.start()
            own[chunk] = copy
            pending[chunk] = send(parts[chunk], "", "c", rc[chunk])
            return
        for copy in pending[chunk]:
            copy.wait_recv()
        if number == 1:
            own[chunk].wait()
            m = mine[chunk]

            def put(where, value):
                m[where] = value.astype(m.dtype)

            if grid.size["c"] > 1:
                total(put, [lambda where: m[where]] + [slot_reader(rc[chunk], j) for j in range(grid.size["c"] - 1)], grid.sizes("c"))
            pending[chunk] = send(m, "c", first, (rx if first == "x" else ry)[chunk])
        elif number == 2:
            m, slots = mine[chunk], (rx if first == "x" else ry)[chunk]

            def put(where, value):
                slots[(0,) + where] = value.astype(slots.dtype)

            total(put, [picker(m, "c", first)] + [slot_reader(slots, j) for j in range(grid.size[first] - 1)], grid.sizes("c" + first))
            pending[chunk] = send(slots.at[0], "c" + first, second, (rx if second == "x" else ry)[chunk])
        elif number == 3:
            before, slots = (rx if first == "x" else ry)[chunk].at[0], (rx if second == "x" else ry)[chunk]

            def put(where, value):
                slots[(0,) + where] = value.astype(slots.dtype)

            total(put, [picker(before, "c" + first, second)] + [slot_reader(slots, j) for j in range(grid.size[second] - 1)], grid.sizes("cxy"))
            pending[chunk] = send(slots.at[0], "cxy", "z", rz[chunk])
        elif number == 4:
            before, slots = (rx if second == "x" else ry)[chunk].at[0], rz[chunk]
            value = before[digit["z"]].astype(F32)
            for j in range(grid.size["z"] - 1):
                value = value + slots[j].astype(F32)
            outs[chunk][...] = value

    for chunk in range(count):
        stage(chunk, 0)
    for tick in range(count + 3):
        for number in (1, 2, 3, 4):
            chunk = tick - (number - 1)
            if 0 <= chunk < count:
                stage(chunk, number)
    for copy in started:
        copy.wait_send()


def scatter_all(grid, parts, chunks):
    count = len(parts)
    steps = count * sum(size - 1 for size in grid.shape)
    anywhere = pl.BlockSpec(memory_space=pl.ANY)
    mine, rc, rx, ry, rz = [], [], [], [], []
    for part, (first, second) in zip(parts, chunks):
        tile, kind = part.shape[4:], part.dtype
        mine.append(pltpu.VMEM(grid.sizes("c") + tile, kind))
        rc.append(pltpu.VMEM((max(grid.size["c"] - 1, 1),) + grid.sizes("c") + tile, kind))
        shapes = {
            first: pltpu.VMEM((max(grid.size[first] - 1, 1),) + grid.sizes("c" + first) + tile, kind),
            second: pltpu.VMEM((max(grid.size[second] - 1, 1),) + grid.sizes("cxy") + tile, kind),
        }
        rx.append(shapes["x"])
        ry.append(shapes["y"])
        rz.append(pltpu.VMEM((max(grid.size["z"] - 1, 1),) + tile, kind))
    return pl.pallas_call(
        functools.partial(scatter_kernel, grid, chunks),
        out_shape=[jax.ShapeDtypeStruct(p.shape[4:], F32) for p in parts],
        in_specs=[anywhere] * count,
        out_specs=[pl.BlockSpec(memory_space=pltpu.VMEM)] * count,
        scratch_shapes=mine + rc + rx + ry + rz + [
            pltpu.SemaphoreType.DMA((count,)),
            pltpu.SemaphoreType.DMA((steps,)),
            pltpu.SemaphoreType.DMA((steps,)),
        ],
        compiler_params=pltpu.CompilerParams(
            collective_id=1, has_side_effects=True, vmem_limit_bytes=VMEM_LIMIT
        ),
    )(*parts)


def dot(a, b, da, db):
    return lax.dot_general(a, b, (((da,), (db,)), ((), ())), preferred_element_type=F32)


PRECISE = dict(score=0, inner=1, cross=1, own=1, back=0)


def parts_of(value):
    high = value.astype(BF16)
    return high, (value - high.astype(F32)).astype(BF16)


def dot2(a, b, da, db, name):
    if not PRECISE[name]:
        return dot(a.astype(BF16), b, da, db)
    high, low = parts_of(a)
    return dot(high, b, da, db) + dot(low, b, da, db)


def dot3(a, b, da, db, name):
    if not PRECISE[name]:
        return dot(a.astype(BF16), b.astype(BF16), da, db)
    a_high, a_low = parts_of(a)
    b_high, b_low = parts_of(b)
    return dot(a_high, b_high, da, db) + (dot(a_low, b_high, da, db) + dot(a_high, b_low, da, db))


def half_masks(rows):
    lane = lax.broadcasted_iota(jnp.int32, (rows, LANES), 1)
    return lane < SUBSPACE_EXTENT


def block_ones(kind):
    row = lax.broadcasted_iota(jnp.int32, (LANES, LANES), 0) // SUBSPACE_EXTENT
    lane = lax.broadcasted_iota(jnp.int32, (LANES, LANES), 1) // SUBSPACE_EXTENT
    return (row == lane).astype(kind)


def head_sum(value, ones):
    high = value.astype(BF16)
    low = (value - high.astype(F32)).astype(BF16)
    return dot(high, ones, 1, 0) + dot(low, ones, 1, 0)


def decays(rate, length):
    step = lax.broadcasted_iota(jnp.int32, (length, LANES), 0).astype(F32)
    return jnp.exp(-rate * step), jnp.exp(rate * (step + 1.0)), jnp.exp(-rate * (length - 1.0 - step))


def fold(first, second, ones):
    pick = half_masks(LANES)
    a, b = first * ones, second * ones
    a = a + pltpu.roll(a, SUBSPACE_EXTENT, 1)
    b = b + pltpu.roll(b, SUBSPACE_EXTENT, 1)
    return jnp.where(pick, a, b)


def unfold(both, segment, ones):
    pick = half_masks(LANES)
    turned = pltpu.roll(both, SUBSPACE_EXTENT, 1)
    full = jnp.where(pick, both, turned) if segment == 0 else jnp.where(pick, turned, both)
    return full * ones


def exchange(grid, index, source, slots, rows, send_sem, recv_sem):
    me, copies = index["seq"], []
    for j in range(1, grid.seq):
        target = lax.rem(me + j, grid.seq)
        copy = pltpu.make_async_remote_copy(
            src_ref=source.at[pl.ds(pl.multiple_of(target * rows, 16), rows)],
            dst_ref=slots.at[pl.ds(pl.multiple_of(me * rows, 16), rows)],
            send_sem=send_sem.at[j - 1],
            recv_sem=recv_sem.at[j - 1],
            device_id=(target, index["batch"]),
            device_id_type=MESH,
        )
        copy.start()
        copies.append(copy)
    here = pl.ds(pl.multiple_of(me * rows, 16), rows)
    slots[here, :] = source[here, :]
    return copies


CHUNK = 1024
TALL = 512


def pieces(columns, step):
    return [(at, min(step, columns - at)) for at in range(0, columns, step)]


class Gather:
    def __init__(self, grid, index, digit, shards, fulls, plan, own_sem, send_sem, recv_sem):
        self.grid, self.index, self.digit = grid, index, digit
        self.shards, self.fulls, self.plan = shards, fulls, plan
        self.own_sem, self.send_sem, self.recv_sem = own_sem, send_sem, recv_sem
        self.started, self.pending, self.own = [], {}, {}
        self.tick, self.done = 0, 0

    def others(self, name):
        size = self.grid.size[name]
        return [lax.rem(self.digit[name] + j, size) for j in range(1, size)]

    def send(self, source, place, name):
        copies = []
        for target in self.others(name):
            slot = len(self.started)
            copy = pltpu.make_async_remote_copy(
                src_ref=source,
                dst_ref=place,
                send_sem=self.send_sem.at[slot],
                recv_sem=self.recv_sem.at[slot],
                device_id=self.grid.peer(self.index, self.digit, name, target),
                device_id_type=MESH,
            )
            copy.start()
            self.started.append(copy)
            copies.append(copy)
        return copies

    def stage(self, unit, number):
        if not 0 <= unit < len(self.plan):
            return
        for piece in range(len(self.plan[unit][1])):
            self.step(unit, piece, number)

    def step(self, unit, piece, number):
        array, parts = self.plan[unit]
        column, columns, first, second = parts[piece]
        digit = self.digit
        window = pl.ds(column, columns)
        full = self.fulls[array]
        key = (unit, piece)

        def at(**fixed):
            place = tuple(fixed.get(name, slice(None)) for name in self.grid.order)
            return full.at[place + (slice(None), window)]

        if number == 0:
            place = at(**digit)
            source = self.shards[array].at[:, window]
            copy = pltpu.make_async_copy(source, place, self.own_sem.at[len(self.own)])
            copy.start()
            self.own[key] = copy
            self.pending[key] = self.send(source, place, "z")
            return
        for copy in self.pending[key]:
            copy.wait_recv()
        if number == 1:
            self.own[key].wait()
            fixed, name = {n: digit[n] for n in ("x", "y", "c")}, first
        elif number == 2:
            fixed, name = {n: digit[n] for n in (second, "c")}, second
        elif number == 3:
            fixed, name = {"c": digit["c"]}, "c"
        else:
            self.pending[key] = []
            return
        place = at(**fixed)
        self.pending[key] = self.send(place, place, name)

    def open(self, ahead):
        self.ahead = ahead
        for piece in range(ahead):
            self.stage(piece, 0)

    def pump(self, count=1):
        for _ in range(count):
            tick = self.tick
            self.tick += 1
            for number in (1, 2, 3):
                self.stage(tick - (number - 1), number)
            self.stage(tick + self.ahead, 0)

    def ready(self, piece):
        while self.tick < piece + 3:
            self.pump()
        while self.done <= piece:
            self.stage(self.done, 4)
            self.done += 1

    def close(self):
        for copy in self.started:
            copy.wait_send()


def gather_plan(arrays):
    plan, starts = [], []
    for array, (columns, step) in enumerate(arrays):
        starts.append(len(plan))
        for column, size in pieces(columns, step):
            half = size // 2
            if half % LANES:
                plan.append((array, [(column, size, "x", "y")]))
            else:
                plan.append((array, [(column, half, "x", "y"), (column + half, half, "y", "x")]))
    return plan, starts


def span(unit):
    return unit[1][0][0], sum(part[1] for part in unit[1])


def column_of(row, length):
    at = lax.broadcasted_iota(jnp.int32, (LANES, LANES), 0)
    lane = lax.broadcasted_iota(jnp.int32, (LANES, LANES), 1)
    spread = jnp.where(at == lane, jnp.broadcast_to(row, (LANES, LANES)), 0.0)
    return jnp.broadcast_to(jnp.sum(spread, axis=1, keepdims=True), (LANES, LANES))


def forward_kernel(grid, length, plan, starts, *refs):
    (
        x_ref, up_ref, att_entry_ref, ffn_entry_ref, start_ref, *shards
    ) = refs[:14]
    fulls = refs[14:23]
    (
        result_ref, table_ref, mixed_ref, r_ref, k_ref, v_ref, gate_ref, wkv_ref, attended_ref, begin_ref,
        middle_ref, mixed2_ref, hidden_ref, d_carried_ref, d_recv_ref, prev_ref,
    ) = refs[23:39]
    (
        normed_ref, wide_ref, tall_ref, small_ref, edge_ref, arrive_ref, recv_ref,
        own_ref, got_ref, out_ref, fade_ref,
        own_sem, send_sem, recv_sem, load_sem, edge_send, edge_recv, send_a, recv_a, send_b, recv_b,
    ) = refs[39:]
    index, digit = grid.place()
    me = index["seq"]
    tokens, width = x_ref.shape
    segments = tokens // length
    pairs, rows = width // LANES, width // grid.seq
    batch_roles = [n for n in grid.order if grid.axis[n] == "batch"]
    gather = Gather(grid, index, digit, shards, fulls, plan, own_sem, send_sem, recv_sem)
    peers = [grid.peer(index, digit, n, t) for n in batch_roles for t in gather.others(n)]
    peers += [(lax.rem(me + j, grid.seq), index["batch"]) for j in range(1, grid.seq)]
    greet(peers)
    gather.open(3)

    def first_piece(array):
        return starts[array]

    def load(array, piece, buffer, slot):
        gather.ready(piece)
        column, columns = span(plan[piece])
        source = fulls[array].at[(slice(None),) * 5 + (pl.ds(column, columns),)]
        target = buffer.at[(slot,) + (slice(None),) * 5 + (pl.ds(0, columns),)]
        copy = pltpu.make_async_copy(source, target, load_sem.at[slot])
        copy.start()
        return copy

    def weight(buffer, slot, window):
        value = buffer[(slot,) + (slice(None),) * 5 + (window,)]
        return value.reshape((-1, value.shape[-1]))

    def tile(n, step=256):
        return pl.ds(pl.multiple_of(n * step, step), step)

    gather.ready(0)
    copy = pltpu.make_async_copy(fulls[0], small_ref, load_sem.at[0])
    copy.start()
    copy.wait()
    ranks = grid.seq * grid.batch
    small = small_ref[...].astype(F32).reshape((ranks, 16, LANES))
    per = ranks // pairs
    for p in range(pairs):
        total = small[p * per]
        for j in range(1, per):
            total = total + small[p * per + j]
        table_ref[:, p * LANES : (p + 1) * LANES] = total
    gather.pump()

    def shift_rows(segment, source_ref, body):
        step = 64

        def run(i, carry):
            at = pl.ds(pl.multiple_of(segment * length + i * step, step), step)
            current = source_ref[at, :]
            row = lax.broadcasted_iota(jnp.int32, (step, 1), 0)
            previous = jnp.where(row == 0, carry, pltpu.roll(current, 1, 0))
            body(at, current, previous)
            return current[step - 1 : step, :]

        lax.fori_loop(0, length // step, run, prev_ref[segment : segment + 1, :])

    def swap_edges(entry_ref, slot):
        edge_ref[...] = jnp.zeros_like(edge_ref)
        for q in range(segments):
            last = (q + 1) * length
            edge_ref[q : q + 1, :] = normed_ref[last - 8 : last, :][7:8, :]
        copy = pltpu.make_async_remote_copy(
            src_ref=edge_ref,
            dst_ref=arrive_ref.at[slot],
            send_sem=edge_send.at[slot],
            recv_sem=edge_recv.at[slot],
            device_id=(lax.rem(me + 1, grid.seq), index["batch"]),
            device_id_type=MESH,
        )
        copy.start()
        copy.wait()
        first = jnp.where(me == 0, 1.0, 0.0)
        prev_ref[...] = arrive_ref[slot] * (1.0 - first)
        prev_ref[0:segments, :] += entry_ref[...].astype(F32) * first

    def norm(source_ref, gain, bias):
        step = 64

        def run(i, carry):
            at = pl.ds(pl.multiple_of(i * step, step), step)
            value = source_ref[at, :].astype(F32)
            center = value - jnp.mean(value, axis=-1, keepdims=True)
            spread = jnp.mean(center * center, axis=-1, keepdims=True)
            normed_ref[at, :] = center * lax.rsqrt(spread + 1e-05) * table_ref[gain : gain + 1, :] + table_ref[bias : bias + 1, :]
            return carry

        lax.fori_loop(0, tokens // step, run, 0)

    norm(x_ref, 0, 1)
    swap_edges(att_entry_ref, 0)

    def mix_one(at, current, previous):
        for c in range(4):
            blend = table_ref[2 + c : 3 + c, :]
            mixed_ref[c, at, :] = (current * blend + previous * (1.0 - blend)).astype(BF16)

    for q in range(segments):
        shift_rows(q, normed_ref, mix_one)

    def project_to(array, slot, left, target_ref):
        copy = load(array, first_piece(array), wide_ref, slot)
        copy.wait()

        def run(n, carry):
            value = dot(left[...], weight(wide_ref, slot, tile(n)), 1, 0)
            target_ref[:, tile(n)] = value.astype(target_ref.dtype)
            return carry

        lax.fori_loop(0, width // 256, run, 0)

    project_to(1, 0, mixed_ref.at[1], k_ref)
    project_to(2, 1, mixed_ref.at[2], v_ref)
    ones, ones16 = block_ones(F32), block_ones(BF16)
    group = lax.div(me * rows, LANES)
    own_log = table_ref[6:7, pl.ds(pl.multiple_of(group * LANES, LANES), LANES)]
    fade_ref[...] = column_of(jnp.exp(-length * jnp.exp(own_log)), length)

    def columns(p):
        return pl.ds(pl.multiple_of(p * LANES, LANES), LANES)

    def rate_of(p):
        return jnp.exp(table_ref[6:7, columns(p)])

    def own_states(p, carry):
        _, _, end = decays(rate_of(p), length)
        both = []
        for q in range(segments):
            token = pl.ds(q * length, length)
            k_end = k_ref[token, columns(p)].astype(F32) * end
            both.append(dot2(k_end, v_ref[token, columns(p)], 0, 0, "own"))
        own_ref[columns(p), :] = fold(both[0], both[1], ones).astype(BF16)
        return carry

    lax.fori_loop(0, pairs, own_states, 0)
    first = exchange(grid, index, own_ref, got_ref, rows, send_a, recv_a)
    project_to(3, 0, mixed_ref.at[0], r_ref)
    project_to(4, 1, mixed_ref.at[3], gate_ref)
    for copy in first:
        copy.wait_recv()
    state = start_ref[...]
    fade = fade_ref[pl.ds(pl.multiple_of(lax.rem(me * rows, LANES), rows), rows), :]
    for block in range(grid.seq):
        at = pl.ds(block * rows, rows)
        out_ref[at, :] = state.astype(BF16)
        state = fade * state + got_ref[at, :].astype(F32)
    second = exchange(grid, index, out_ref, begin_ref, rows, send_b, recv_b)
    gather.pump()

    later = lax.broadcasted_iota(jnp.int32, (length, length), 0) > lax.broadcasted_iota(
        jnp.int32, (length, length), 1
    )
    for copy in second:
        copy.wait_recv()

    def inside(p, carry):
        down, up, _ = decays(rate_of(p), length)
        pick = half_masks(length)
        begin = begin_ref[columns(p), :].astype(F32)
        for q in range(segments):
            token = pl.ds(q * length, length)
            r = r_ref[token, columns(p)].astype(F32)
            k = k_ref[token, columns(p)].astype(F32)
            v = v_ref[token, columns(p)]
            r_down = r * down
            k_up = k * up
            halves = []
            for h in range(2):
                r_head = jnp.where(pick == (h == 0), r_down, 0.0)
                scores = jnp.where(later, dot3(r_head, k_up, 1, 1, "score"), 0.0)
                halves.append(dot2(scores, v, 1, 0, "inner"))
            inner = jnp.where(pick, halves[0], halves[1])
            self_part = head_sum(r * table_ref[7:8, columns(p)] * k, ones16)
            inner = inner + self_part * v.astype(F32)
            state16 = unfold(begin, q, ones).astype(BF16)
            y = (inner + dot2(r_down, state16, 1, 0, "cross")).astype(BF16)
            wkv_ref[token, columns(p)] = y
            center = y.astype(F32) - dot(y, ones16, 1, 0) * (1.0 / SUBSPACE_EXTENT)
            spread = head_sum(center * center, ones16) * (1.0 / SUBSPACE_EXTENT)
            z = center * lax.rsqrt(spread + 0.00064)
            normalized = z * table_ref[8:9, columns(p)] + table_ref[9:10, columns(p)]
            g = gate_ref[token, columns(p)]
            attended_ref[token, columns(p)] = (normalized * g / (1.0 + jnp.exp(-g))).astype(BF16)
        return carry

    for quarter in range(4):
        lax.fori_loop(quarter * pairs // 4, (quarter + 1) * pairs // 4, inside, 0)
        gather.pump()

    copy = load(5, first_piece(5), wide_ref, 0)
    copy.wait()

    def out_project(n, carry):
        value = dot(attended_ref[...], weight(wide_ref, 0, tile(n)), 1, 0)
        middle_ref[:, tile(n)] = x_ref[:, tile(n)].astype(F32) + value
        return carry

    lax.fori_loop(0, width // 256, out_project, 0)
    norm(middle_ref, 10, 11)
    swap_edges(ffn_entry_ref, 1)

    def mix_two(at, current, previous):
        for c in range(2):
            blend = table_ref[12 + c : 13 + c, :]
            mixed2_ref[c, at, :] = (current * blend + previous * (1.0 - blend)).astype(BF16)

    for q in range(segments):
        shift_rows(q, normed_ref, mix_two)
    copy = load(6, first_piece(6), wide_ref, 1)
    copy.wait()

    def receive(n, carry):
        value = dot(mixed2_ref[1], weight(wide_ref, 1, tile(n)), 1, 0)
        recv = 1.0 / (1.0 + jnp.exp(-value))
        recv_ref[:, tile(n)] = recv
        d_carried_ref[:, tile(n)] = (recv * up_ref[:, tile(n)].astype(F32)).astype(BF16)
        return carry

    lax.fori_loop(0, width // 256, receive, 0)

    for piece in range(starts[7], starts[8]):
        slot = (piece - starts[7]) % 2
        column, size = span(plan[piece])
        copy = load(7, piece, wide_ref, slot)
        copy.wait()

        def key(n, carry):
            value = jnp.maximum(dot(mixed2_ref[0], weight(wide_ref, slot, tile(n)), 1, 0), 0.0)
            hidden_ref[:, pl.ds(pl.multiple_of(column + n * 256, 256), 256)] = (value * value).astype(BF16)
            return carry

        lax.fori_loop(0, size // 256, key, 0)
    for piece in range(starts[8], len(plan)):
        slot = (piece - starts[8]) % 2
        column, size = span(plan[piece])
        copy = load(8, piece, tall_ref, slot)
        copy.wait()
        window = pl.ds(column, size)

        def carry_out(m, carry):
            at = tile(m, 256)
            carried = dot(hidden_ref[at, :], weight(tall_ref, slot, pl.ds(0, size)), 1, 0)
            recv = recv_ref[at, window]
            result_ref[at, window] = (middle_ref[at, window] + recv * carried).astype(BF16)
            upstream = up_ref[at, window].astype(F32)
            d_recv_ref[at, window] = (recv * (1.0 - recv) * carried * upstream).astype(BF16)
            return carry

        lax.fori_loop(0, tokens // 256, carry_out, 0)

    for copy in first + second:
        copy.wait_send()
    gather.close()


def forward(grid, x, upstream, att_entry, ffn_entry, start, shards, length):
    tokens, width = x.shape
    steps = [LANES] + [CHUNK] * 7 + [TALL]
    plan, starts = gather_plan([(s.shape[1], step) for s, step in zip(shards, steps)])
    total = sum(len(unit[1]) for unit in plan)
    hidden = shards[7].shape[1]
    vmem = pl.BlockSpec(memory_space=pltpu.VMEM)
    anywhere = pl.BlockSpec(memory_space=pl.ANY)
    flat = jax.ShapeDtypeStruct((tokens, width), BF16)
    flat32 = jax.ShapeDtypeStruct((tokens, width), F32)
    state = pltpu.VMEM((width, LANES), BF16)
    sems = pltpu.SemaphoreType.DMA((grid.seq - 1,))
    count = total * sum(size - 1 for size in grid.shape)
    return pl.pallas_call(
        functools.partial(forward_kernel, grid, length, plan, starts),
        out_shape=[jax.ShapeDtypeStruct(grid.shape + s.shape, s.dtype) for s in shards]
        + [
            flat, jax.ShapeDtypeStruct((16, width), F32), jax.ShapeDtypeStruct((4, tokens, width), BF16),
            flat, flat, flat, flat32, flat, flat, jax.ShapeDtypeStruct((width, LANES), BF16),
            flat32, jax.ShapeDtypeStruct((2, tokens, width), BF16), jax.ShapeDtypeStruct((tokens, hidden), BF16),
            flat, flat, jax.ShapeDtypeStruct((8, width), F32),
        ],
        in_specs=[vmem] * 5 + [anywhere] * 9,
        out_specs=[anywhere] * 9 + [vmem] * 16,
        scratch_shapes=[
            pltpu.VMEM((tokens, width), F32),
            pltpu.VMEM((2,) + grid.shape + (shards[1].shape[0], CHUNK), BF16),
            pltpu.VMEM((2,) + grid.shape + (shards[8].shape[0], TALL), BF16),
            pltpu.VMEM(grid.shape + shards[0].shape, BF16),
            pltpu.VMEM((8, width), F32),
            pltpu.VMEM((2, 8, width), F32),
            pltpu.VMEM((tokens, width), F32),
            state, state, state,
            pltpu.VMEM((LANES, LANES), F32),
            pltpu.SemaphoreType.DMA((total,)),
            pltpu.SemaphoreType.DMA((count,)),
            pltpu.SemaphoreType.DMA((count,)),
            pltpu.SemaphoreType.DMA((2,)),
            pltpu.SemaphoreType.DMA((2,)),
            pltpu.SemaphoreType.DMA((2,)),
            sems, sems, sems, sems,
        ],
        compiler_params=pltpu.CompilerParams(
            collective_id=0, has_side_effects=True, vmem_limit_bytes=VMEM_LIMIT
        ),
    )(x, upstream, att_entry, ffn_entry, start, *shards)


def wkv_backward_kernel(
    grid, length,
    r_ref, k_ref, v_ref, gate_ref, wkv_ref, d_att_ref, rate_ref, reward_ref, gain_ref, bias_ref, fade_ref, begin_ref,
    d_gate_ref, dr_ref, dk_ref, dv_ref, sums_ref,
    dy_ref, own_ref, got_ref, out_ref, end_ref, send_a, recv_a, send_b, recv_b,
):
    index, _ = grid.place()
    me = index["seq"]
    greet([(lax.rem(me + j, grid.seq), index["batch"]) for j in range(1, grid.seq)])
    width = r_ref.shape[1]
    pairs, rows = width // LANES, width // grid.seq
    ones, ones16 = block_ones(F32), block_ones(BF16)
    share = 1.0 / SUBSPACE_EXTENT

    def columns(p):
        return pl.ds(pl.multiple_of(p * LANES, LANES), LANES)

    def own_states(p, carry):
        down, _, _ = decays(rate_ref[:, columns(p)], length)
        both = []
        gain_sum, bias_sum = jnp.zeros((1, LANES), F32), jnp.zeros((1, LANES), F32)
        for q in range(2):
            token = pl.ds(q * length, length)
            y = wkv_ref[token, columns(p)]
            center = y.astype(F32) - dot(y, ones16, 1, 0) * share
            spread = head_sum(center * center, ones16) * share
            scale = lax.rsqrt(spread + 0.00064)
            z = center * scale
            gain = gain_ref[:, columns(p)]
            normalized = z * gain + bias_ref[:, columns(p)]
            g = gate_ref[token, columns(p)]
            s = 1.0 / (1.0 + jnp.exp(-g))
            d_att = d_att_ref[token, columns(p)]
            d_gate_ref[token, columns(p)] = (d_att * normalized * s * (1.0 + g * (1.0 - s))).astype(BF16)
            d_norm = d_att * g * s
            gain_sum = gain_sum + jnp.sum(d_norm * z, axis=0, keepdims=True)
            bias_sum = bias_sum + jnp.sum(d_norm, axis=0, keepdims=True)
            e = d_norm * gain
            dy = ((e - head_sum(e, ones16) * share - z * (head_sum(e * z, ones16) * share)) * scale).astype(BF16)
            dy_ref[token, columns(p)] = dy
            r_down = r_ref[token, columns(p)].astype(F32) * down
            both.append(dot2(r_down, dy, 0, 0, "own"))
        sums_ref[0:1, columns(p)] = gain_sum
        sums_ref[1:2, columns(p)] = bias_sum
        own_ref[columns(p), :] = fold(both[0], both[1], ones).astype(BF16)
        return carry

    lax.fori_loop(0, pairs, own_states, 0)
    first = exchange(grid, index, own_ref, got_ref, rows, send_a, recv_a)
    for copy in first:
        copy.wait_recv()
    fade = fade_ref[...]
    state = jnp.zeros_like(fade)
    for block in reversed(range(grid.seq)):
        at = pl.ds(block * rows, rows)
        out_ref[at, :] = state.astype(BF16)
        state = fade * state + got_ref[at, :].astype(F32)
    second = exchange(grid, index, out_ref, end_ref, rows, send_b, recv_b)
    for copy in second:
        copy.wait_recv()

    later = lax.broadcasted_iota(jnp.int32, (length, length), 0) > lax.broadcasted_iota(
        jnp.int32, (length, length), 1
    )
    step = lax.broadcasted_iota(jnp.int32, (length, LANES), 0).astype(F32)

    def inside(p, carry):
        rate = rate_ref[:, columns(p)]
        reward = reward_ref[:, columns(p)]
        down, up, end = decays(rate, length)
        pick = half_masks(length)
        begins, ends = begin_ref[columns(p), :].astype(F32), end_ref[columns(p), :].astype(F32)
        reward_sum, rate_sum = jnp.zeros((1, LANES), F32), jnp.zeros((1, LANES), F32)
        for q in range(2):
            token = pl.ds(q * length, length)
            r = r_ref[token, columns(p)].astype(F32)
            k = k_ref[token, columns(p)].astype(F32)
            v = v_ref[token, columns(p)]
            dy = dy_ref[token, columns(p)]
            begin, finish = unfold(begins, q, ones), unfold(ends, q, ones)
            begin16, finish16 = begin.astype(BF16), finish.astype(BF16)
            r_down = r * down
            k_up = k * up
            k_end = k * end
            if not PRECISE["back"]:
                r_down = r_down.astype(BF16).astype(F32)
                k_up = k_up.astype(BF16).astype(F32)
                k_end = k_end.astype(BF16).astype(F32)
            d_r, d_k, d_v = [], [], []
            for h in range(2):
                r_head = jnp.where(pick == (h == 0), r_down, 0.0)
                dy_head = jnp.where(pick == (h == 0), dy.astype(F32), 0.0).astype(BF16)
                scores = jnp.where(later, dot3(r_head, k_up, 1, 1, "score"), 0.0)
                d_scores = jnp.where(later, dot(dy_head, v, 1, 1), 0.0)
                d_r.append(dot3(d_scores, k_up, 1, 0, "back"))
                d_k.append(dot3(d_scores, r_down, 0, 0, "back"))
                d_v.append(dot2(scores, dy, 0, 0, "inner"))
            from_r = jnp.where(pick, d_r[0], d_r[1]) + dot(dy, begin16, 1, 1)
            from_k = jnp.where(pick, d_k[0], d_k[1])
            from_end = dot(v, finish16, 1, 1)
            v32, dy32 = v.astype(F32), dy.astype(F32)
            v_dy = head_sum(v32 * dy32, ones16)
            self_part = head_sum(r * reward * k, ones16)
            dr_ref[token, columns(p)] = (from_r * down + reward * k * v_dy).astype(BF16)
            dk_ref[token, columns(p)] = (from_k * up + from_end * end + reward * r * v_dy).astype(BF16)
            dv_ref[token, columns(p)] = (
                jnp.where(pick, d_v[0], d_v[1]) + dot2(k_end, finish16, 1, 0, "cross") + self_part * dy32
            ).astype(BF16)
            reward_sum = reward_sum + jnp.sum(r * k * v_dy, axis=0, keepdims=True)
            terms = (
                (step + 1.0) * k_up * from_k
                - step * r_down * from_r
                - (length - 1.0 - step) * k_end * from_end
            )
            through = lax.dot_general(
                jnp.ones((8, LANES), F32), begin * finish, (((1,), (1,)), ((), ())),
                precision=lax.Precision.HIGHEST, preferred_element_type=F32,
            )[0:1, :]
            rate_sum = rate_sum + jnp.sum(terms, axis=0, keepdims=True) - length * jnp.exp(-rate * length) * through
        sums_ref[2:3, columns(p)] = reward_sum
        sums_ref[3:4, columns(p)] = rate_sum * rate
        return carry

    lax.fori_loop(0, pairs, inside, 0)
    sums_ref[4:8, :] = jnp.zeros((4, width), F32)
    for copy in first + second:
        copy.wait_send()


def wkv_backward(grid, r, k, v, gate_pre, wkv, d_att, rate, reward, gain, bias, fade, begin):
    tokens, width = r.shape
    state = pltpu.VMEM((width, LANES), BF16)
    sems = pltpu.SemaphoreType.DMA((grid.seq - 1,))
    vmem = pl.BlockSpec(memory_space=pltpu.VMEM)
    flat = jax.ShapeDtypeStruct((tokens, width), BF16)
    return pl.pallas_call(
        functools.partial(wkv_backward_kernel, grid, tokens // 2),
        out_shape=[flat, flat, flat, flat, jax.ShapeDtypeStruct((8, width), F32)],
        in_specs=[vmem] * 12,
        out_specs=[vmem] * 5,
        scratch_shapes=[pltpu.VMEM((tokens, width), BF16), state, state, state, state, sems, sems, sems, sems],
        compiler_params=pltpu.CompilerParams(
            collective_id=3, has_side_effects=True, vmem_limit_bytes=VMEM_LIMIT
        ),
    )(r, k, v, gate_pre, wkv, d_att, rate, reward, gain, bias, fade, begin)


def shifted(block, axis, distance):
    devices = range(lax.axis_size(axis))
    route = [(i - distance, i) for i in devices if i - distance in devices]
    return lax.ppermute(block, axis, route)


def standardize(rows, epsilon):
    center = rows - jnp.mean(rows, axis=-1, keepdims=True)
    spread = jnp.mean(center * center, axis=-1, keepdims=True)
    scale = lax.rsqrt(spread + epsilon)
    return center * scale, scale


def back_standardize(e, z, scale):
    return (e - jnp.mean(e, axis=-1, keepdims=True) - z * jnp.mean(e * z, axis=-1, keepdims=True)) * scale


def project(rows, weights):
    return dot(rows, weights, 1, 0)


def outer(left_side, right_side):
    return dot(left_side, right_side, 0, 0).astype(BF16)


def back_through(grads, weights):
    return dot(grads, weights, 1, 1)


def local(grid, *args):
    (
        incoming, att_entry, ffn_entry, memory, upstream,
        ln1_gain, ln1_bias, att_mix, w_recept, w_key, w_value, w_gate, decay_log, reward,
        gn_gain, gn_bias, w_out, ln2_gain, ln2_bias, ffn_mix, f_key, f_value, f_recept,
    ) = args
    segments, length, width = incoming.shape
    tokens = segments * length
    ranks = grid.seq * grid.batch
    share = width // ranks
    is_first = lax.axis_index("seq") == 0

    per = LANES // share
    rank = lax.axis_index(("seq", "batch"))
    small = jnp.stack(
        [ln1_gain, ln1_bias] + [att_mix[:, c] for c in range(4)] + [decay_log, reward, gn_gain, gn_bias, ln2_gain, ln2_bias]
        + [ffn_mix[:, c] for c in range(2)]
    )
    small = jnp.tile(jnp.pad(small, ((0, 2), (0, 0))), (1, per))
    lane = lax.broadcasted_iota(jnp.int32, small.shape, 1)
    small = jnp.where(lane // share == rank % per, small, jnp.zeros_like(small))
    rows = width // grid.seq
    row = lax.axis_index("seq") * rows
    start = memory.transpose(1, 2, 0, 3).reshape(width, segments * SUBSPACE_EXTENT)
    start = lax.dynamic_slice_in_dim(start, row, rows, 0)
    shards = [small, w_key, w_value, w_recept, w_gate, w_out, f_recept, f_key, f_value]
    outs = forward(
        grid, incoming.reshape(tokens, width), upstream.reshape(tokens, width), att_entry, ffn_entry, start, shards, length
    )
    W_k, W_v, W_r, W_g, W_o, F_r, F_k, F_v = [w.reshape((ranks * w.shape[4], w.shape[5])) for w in outs[1:9]]
    (
        result, table, mixed, r, k, v, gate_pre, wkv, attended, begin, middle, mixed2, hidden, d_carried, d_recv, prev2,
    ) = outs[9:]
    g1, b1 = table[0], table[1]
    mix1 = table[2:6]
    rate = jnp.exp(table[6])[None, :]
    bonus = table[7][None, :]
    gg, gb = table[8][None, :], table[9][None, :]
    g2, b2 = table[10], table[11]
    mix2 = table[12:14]
    own_rate = lax.dynamic_slice_in_dim(rate[0], row, rows, 0)
    fade = jnp.broadcast_to(jnp.exp(-own_rate * length)[:, None], (rows, LANES))
    x = incoming.astype(F32)
    z1, s1 = standardize(x, 1e-05)
    normed = z1 * g1 + b1
    arrived = shifted(normed[:, -1:], "seq", 1)
    previous = jnp.where(is_first, att_entry[:, None, :].astype(F32), arrived)
    before = jnp.concatenate([previous, normed[:, :-1]], axis=1)
    middle = middle.reshape(segments, length, width)
    z2, s2 = standardize(middle, 1e-05)
    normed2 = z2 * g2 + b2
    before2 = jnp.concatenate([prev2[:segments][:, None], normed2[:, :-1]], axis=1)
    key_pos = jnp.sqrt(hidden.astype(F32))

    d_out = upstream.astype(F32).reshape(tokens, width)
    grad_f_value = outer(hidden, d_carried)
    grad_f_recept = outer(mixed2[1], d_recv)
    d_key = (2.0 * key_pos * back_through(d_carried, F_v)).astype(BF16)
    grad_f_key = outer(mixed2[0], d_key)
    d_mixed2 = [
        back_through(d_key, F_k).reshape(segments, length, width),
        back_through(d_recv, F_r).reshape(segments, length, width),
    ]
    difference2 = normed2 - before2
    d_mix2 = [jnp.sum(difference2 * d, axis=(0, 1)) for d in d_mixed2]
    d_before2 = sum((1.0 - mix2[c]) * d_mixed2[c] for c in range(2))
    from_next2 = shifted(d_before2[:, :1], "seq", -1)
    d_normed2 = sum(mix2[c] * d_mixed2[c] for c in range(2)) + jnp.concatenate([d_before2[:, 1:], from_next2], axis=1)
    d_g2 = jnp.sum(z2 * d_normed2, axis=(0, 1))
    d_b2 = jnp.sum(d_normed2, axis=(0, 1))
    d_middle = d_out.reshape(segments, length, width) + back_standardize(d_normed2 * g2, z2, s2)
    d_branch = d_middle.astype(BF16).reshape(tokens, width)
    grad_out = outer(attended, d_branch)
    d_attended = back_through(d_branch, W_o)
    d_gate, d_r, d_k, d_v, sums = wkv_backward(
        grid, r, k, v, gate_pre, wkv, d_attended, rate, bonus, gg, gb, fade, begin
    )
    grad_r, grad_k, grad_v, grad_g = [
        outer(m, d) for m, d in zip(mixed, (d_r, d_k, d_v, d_gate))
    ]
    d_mixed = [
        back_through(d, w).reshape(segments, length, width)
        for d, w in zip((d_r, d_k, d_v, d_gate), (W_r, W_k, W_v, W_g))
    ]
    difference = normed - before
    d_mix1 = [jnp.sum(difference * d, axis=(0, 1)) for d in d_mixed]
    d_before = sum((1.0 - mix1[c]) * d_mixed[c] for c in range(4))
    from_next = shifted(d_before[:, :1], "seq", -1)
    d_normed = sum(mix1[c] * d_mixed[c] for c in range(4)) + jnp.concatenate([d_before[:, 1:], from_next], axis=1)
    d_g1 = jnp.sum(z1 * d_normed, axis=(0, 1))
    d_b1 = jnp.sum(d_normed, axis=(0, 1))
    d_input = (d_middle + back_standardize(d_normed * g1, z1, s1)).astype(BF16)

    rows_of = [d_g1, d_b1] + d_mix1 + [sums[3], sums[2], sums[0], sums[1], d_g2, d_b2] + d_mix2
    small_grad = jnp.stack(rows_of).reshape(14, ranks, share).transpose(1, 0, 2)
    small_grad = jnp.pad(small_grad, ((0, 0), (0, 2), (0, LANES - share))).reshape(grid.shape + (16, LANES))
    parts = [
        g.reshape(grid.shape + (g.shape[0] // ranks, g.shape[1]))
        for g in (grad_f_value, grad_f_key, grad_f_recept, grad_out, grad_g, grad_r, grad_k, grad_v)
    ] + [small_grad]
    chunks = [("x", "y"), ("y", "x"), ("x", "y"), ("y", "x"), ("x", "y"), ("y", "x"), ("x", "y"), ("y", "x"), ("x", "y")]
    s_fv, s_fk, s_fr, s_o, s_g, s_r, s_k, s_v, s_small = scatter_all(grid, parts, chunks)
    s = s_small[:14, :share]
    shape = incoming.shape
    return (
        result.reshape(shape), d_input.reshape(shape),
        s[0], s[1], s[2:6].T, s_r, s_k, s_v, s_g, s[6], s[7], s[8], s[9], s_o, s[10], s[11], s[12:14].T,
        s_fk, s_fv, s_fr,
    )


def solution(mesh):
    grid = Grid(mesh.shape["seq"], mesh.shape["batch"])
    both, rows = P(("seq", "batch")), P(("seq", "batch"), None)
    tokens, entry = P("batch", "seq", None), P("batch", None)
    return jax.shard_map(
        functools.partial(local, grid),
        mesh=mesh,
        in_specs=(
            tokens, entry, entry, P("batch", None, None, None), tokens,
            both, both, rows, rows, rows, rows, rows, both, both, both, both, rows, both, both, rows, rows, rows, rows,
        ),
        out_specs=(
            tokens, tokens, both, both, rows, rows, rows, rows, rows, both, both, both, both, rows, both, both, rows,
            rows, rows, rows,
        ),
        check_vma=False,
    )
```

```python
import functools

import jax
import jax.numpy as jnp
from jax import lax
from jax.experimental import pallas as pl
from jax.experimental.pallas import tpu as pltpu
from jax.sharding import PartitionSpec as P

WKV_PARTITIONS = 16
SUBSPACE_EXTENT = 64
LANES = 128
MESH = pl.DeviceIdType.MESH
F32 = jnp.float32
BF16 = jnp.bfloat16
VMEM_LIMIT = 63 * 1024 * 1024


class Grid:
    def __init__(self, seq, batch):
        self.seq, self.batch = seq, batch
        if seq == 8 and batch == 4:
            digits = [("y", "seq", 4, 2), ("x", "seq", 2, 2), ("c", "seq", 1, 2), ("z", "batch", 1, 4)]
        elif seq == 16 and batch == 8:
            digits = [("y", "seq", 4, 4), ("x", "seq", 1, 4), ("z", "batch", 2, 4), ("c", "batch", 1, 2)]
        else:
            raise ValueError("unknown mesh")
        self.order = [name for name, *_ in digits]
        self.axis = {name: axis for name, axis, *_ in digits}
        self.stride = {name: stride for name, _, stride, _ in digits}
        self.size = {name: size for name, *_, size in digits}
        self.shape = tuple(self.size[name] for name in self.order)

    def place(self):
        index = {"seq": lax.axis_index("seq"), "batch": lax.axis_index("batch")}
        return index, {
            name: (index[self.axis[name]] // self.stride[name]) % self.size[name] for name in self.order
        }

    def peer(self, index, digit, name, target):
        where = dict(index)
        axis = self.axis[name]
        where[axis] = index[axis] + (target - digit[name]) * self.stride[name]
        return (where["seq"], where["batch"])

    def at(self, ref, gone="", **fixed):
        return ref.at[tuple(fixed.get(name, slice(None)) for name in self.order if name not in gone)]

    def sizes(self, gone=""):
        return tuple(self.size[name] for name in self.order if name not in gone)


def greet(peers):
    barrier = pltpu.get_barrier_semaphore()
    for peer in peers:
        pl.semaphore_signal(barrier, inc=1, device_id=peer, device_id_type=MESH)
    pl.semaphore_wait(barrier, len(peers))


def dot(a, b, da, db):
    return lax.dot_general(a, b, (((da,), (db,)), ((), ())), preferred_element_type=F32)


PRECISE = dict(score=0, inner=1, cross=1, own=1, back=0)


def parts_of(value):
    high = value.astype(BF16)
    return high, (value - high.astype(F32)).astype(BF16)


def dot2(a, b, da, db, name):
    if not PRECISE[name]:
        return dot(a.astype(BF16), b, da, db)
    high, low = parts_of(a)
    return dot(high, b, da, db) + dot(low, b, da, db)


def dot3(a, b, da, db, name):
    if not PRECISE[name]:
        return dot(a.astype(BF16), b.astype(BF16), da, db)
    a_high, a_low = parts_of(a)
    b_high, b_low = parts_of(b)
    return dot(a_high, b_high, da, db) + (dot(a_low, b_high, da, db) + dot(a_high, b_low, da, db))


def half_masks(rows):
    lane = lax.broadcasted_iota(jnp.int32, (rows, LANES), 1)
    return lane < SUBSPACE_EXTENT


def block_ones(kind):
    row = lax.broadcasted_iota(jnp.int32, (LANES, LANES), 0) // SUBSPACE_EXTENT
    lane = lax.broadcasted_iota(jnp.int32, (LANES, LANES), 1) // SUBSPACE_EXTENT
    return (row == lane).astype(kind)


def head_sum(value, ones):
    high = value.astype(BF16)
    low = (value - high.astype(F32)).astype(BF16)
    return dot(high, ones, 1, 0) + dot(low, ones, 1, 0)


def decays(rate, length):
    step = lax.broadcasted_iota(jnp.int32, (length, LANES), 0).astype(F32)
    return jnp.exp(-rate * step), jnp.exp(rate * (step + 1.0)), jnp.exp(-rate * (length - 1.0 - step))


def fold(first, second, ones):
    pick = half_masks(LANES)
    a, b = first * ones, second * ones
    a = a + pltpu.roll(a, SUBSPACE_EXTENT, 1)
    b = b + pltpu.roll(b, SUBSPACE_EXTENT, 1)
    return jnp.where(pick, a, b)


def unfold(both, segment, ones):
    pick = half_masks(LANES)
    turned = pltpu.roll(both, SUBSPACE_EXTENT, 1)
    full = jnp.where(pick, both, turned) if segment == 0 else jnp.where(pick, turned, both)
    return full * ones


def exchange(grid, index, source, slots, rows, send_sem, recv_sem):
    me, copies = index["seq"], []
    for j in range(1, grid.seq):
        target = lax.rem(me + j, grid.seq)
        copy = pltpu.make_async_remote_copy(
            src_ref=source.at[pl.ds(pl.multiple_of(target * rows, 16), rows)],
            dst_ref=slots.at[pl.ds(pl.multiple_of(me * rows, 16), rows)],
            send_sem=send_sem.at[j - 1],
            recv_sem=recv_sem.at[j - 1],
            device_id=(target, index["batch"]),
            device_id_type=MESH,
        )
        copy.start()
        copies.append(copy)
    here = pl.ds(pl.multiple_of(me * rows, 16), rows)
    slots[here, :] = source[here, :]
    return copies


CHUNK = 1024
TALL = 512


def pieces(columns, step):
    return [(at, min(step, columns - at)) for at in range(0, columns, step)]


class Gather:
    def __init__(self, grid, index, digit, shards, fulls, plan, own_sem, send_sem, recv_sem):
        self.grid, self.index, self.digit = grid, index, digit
        self.shards, self.fulls, self.plan = shards, fulls, plan
        self.own_sem, self.send_sem, self.recv_sem = own_sem, send_sem, recv_sem
        self.started, self.pending, self.own = [], {}, {}
        self.tick, self.done = 0, 0

    def others(self, name):
        size = self.grid.size[name]
        return [lax.rem(self.digit[name] + j, size) for j in range(1, size)]

    def send(self, source, place, name):
        copies = []
        for target in self.others(name):
            slot = len(self.started)
            copy = pltpu.make_async_remote_copy(
                src_ref=source,
                dst_ref=place,
                send_sem=self.send_sem.at[slot],
                recv_sem=self.recv_sem.at[slot],
                device_id=self.grid.peer(self.index, self.digit, name, target),
                device_id_type=MESH,
            )
            copy.start()
            self.started.append(copy)
            copies.append(copy)
        return copies

    def stage(self, unit, number):
        if not 0 <= unit < len(self.plan):
            return
        for piece in range(len(self.plan[unit][1])):
            self.step(unit, piece, number)

    def step(self, unit, piece, number):
        array, parts = self.plan[unit]
        column, columns, first, second = parts[piece]
        digit = self.digit
        window = pl.ds(column, columns)
        full = self.fulls[array]
        key = (unit, piece)

        def at(**fixed):
            place = tuple(fixed.get(name, slice(None)) for name in self.grid.order)
            return full.at[place + (slice(None), window)]

        if number == 0:
            place = at(**digit)
            source = self.shards[array].at[:, window]
            copy = pltpu.make_async_copy(source, place, self.own_sem.at[len(self.own)])
            copy.start()
            self.own[key] = copy
            self.pending[key] = self.send(source, place, "z")
            return
        for copy in self.pending[key]:
            copy.wait_recv()
        if number == 1:
            self.own[key].wait()
            fixed, name = {n: digit[n] for n in ("x", "y", "c")}, first
        elif number == 2:
            fixed, name = {n: digit[n] for n in (second, "c")}, second
        elif number == 3:
            fixed, name = {"c": digit["c"]}, "c"
        else:
            self.pending[key] = []
            return
        place = at(**fixed)
        self.pending[key] = self.send(place, place, name)

    def open(self, ahead):
        self.ahead = ahead
        for piece in range(ahead):
            self.stage(piece, 0)

    def pump(self, count=1):
        for _ in range(count):
            tick = self.tick
            self.tick += 1
            for number in (1, 2, 3):
                self.stage(tick - (number - 1), number)
            self.stage(tick + self.ahead, 0)

    def ready(self, piece):
        while self.tick < piece + 3:
            self.pump()
        while self.done <= piece:
            self.stage(self.done, 4)
            self.done += 1

    def close(self):
        for copy in self.started:
            copy.wait_send()


def gather_plan(arrays):
    plan, starts = [], []
    for array, (columns, step) in enumerate(arrays):
        starts.append(len(plan))
        for column, size in pieces(columns, step):
            half = size // 2
            if half % LANES:
                plan.append((array, [(column, size, "x", "y")]))
            else:
                plan.append((array, [(column, half, "x", "y"), (column + half, half, "y", "x")]))
    return plan, starts


def span(unit):
    return unit[1][0][0], sum(part[1] for part in unit[1])


def column_of(row, length):
    at = lax.broadcasted_iota(jnp.int32, (LANES, LANES), 0)
    lane = lax.broadcasted_iota(jnp.int32, (LANES, LANES), 1)
    spread = jnp.where(at == lane, jnp.broadcast_to(row, (LANES, LANES)), 0.0)
    return jnp.broadcast_to(jnp.sum(spread, axis=1, keepdims=True), (LANES, LANES))


def forward_kernel(grid, length, plan, starts, *refs):
    (
        x_ref, up_ref, att_entry_ref, ffn_entry_ref, start_ref, *shards
    ) = refs[:14]
    fulls = refs[14:23]
    (
        result_ref, table_ref, mixed_ref, r_ref, k_ref, v_ref, gate_ref, wkv_ref, attended_ref, begin_ref,
        middle_ref, mixed2_ref, hidden_ref, d_carried_ref, d_recv_ref, prev_ref,
    ) = refs[23:39]
    (
        normed_ref, wide_ref, tall_ref, small_ref, edge_ref, arrive_ref, recv_ref,
        own_ref, got_ref, out_ref, fade_ref,
        own_sem, send_sem, recv_sem, load_sem, edge_send, edge_recv, send_a, recv_a, send_b, recv_b,
    ) = refs[39:]
    index, digit = grid.place()
    me = index["seq"]
    tokens, width = x_ref.shape
    segments = tokens // length
    pairs, rows = width // LANES, width // grid.seq
    batch_roles = [n for n in grid.order if grid.axis[n] == "batch"]
    gather = Gather(grid, index, digit, shards, fulls, plan, own_sem, send_sem, recv_sem)
    peers = [grid.peer(index, digit, n, t) for n in batch_roles for t in gather.others(n)]
    peers += [(lax.rem(me + j, grid.seq), index["batch"]) for j in range(1, grid.seq)]
    greet(peers)
    gather.open(3)

    def first_piece(array):
        return starts[array]

    def load(array, piece, buffer, slot):
        gather.ready(piece)
        column, columns = span(plan[piece])
        source = fulls[array].at[(slice(None),) * 5 + (pl.ds(column, columns),)]
        target = buffer.at[(slot,) + (slice(None),) * 5 + (pl.ds(0, columns),)]
        copy = pltpu.make_async_copy(source, target, load_sem.at[slot])
        copy.start()
        return copy

    def weight(buffer, slot, window):
        value = buffer[(slot,) + (slice(None),) * 5 + (window,)]
        return value.reshape((-1, value.shape[-1]))

    def tile(n, step=256):
        return pl.ds(pl.multiple_of(n * step, step), step)

    gather.ready(0)
    copy = pltpu.make_async_copy(fulls[0], small_ref, load_sem.at[0])
    copy.start()
    copy.wait()
    ranks = grid.seq * grid.batch
    small = small_ref[...].astype(F32).reshape((ranks, 16, LANES))
    per = ranks // pairs
    for p in range(pairs):
        total = small[p * per]
        for j in range(1, per):
            total = total + small[p * per + j]
        table_ref[:, p * LANES : (p + 1) * LANES] = total
    gather.pump()

    def shift_rows(segment, source_ref, slot, body):
        step = 64

        def run(i, carry):
            at = pl.ds(pl.multiple_of(segment * length + i * step, step), step)
            current = source_ref[at, :]
            row = lax.broadcasted_iota(jnp.int32, (step, 1), 0)
            previous = jnp.where(row == 0, carry, pltpu.roll(current, 1, 0))
            body(at, current, previous)
            return current[step - 1 : step, :]

        lax.fori_loop(0, length // step, run, prev_ref[slot, segment : segment + 1, :])

    def swap_edges(entry_ref, slot):
        edge_ref[...] = jnp.zeros_like(edge_ref)
        for q in range(segments):
            last = (q + 1) * length
            edge_ref[q : q + 1, :] = normed_ref[last - 8 : last, :][7:8, :]
        copy = pltpu.make_async_remote_copy(
            src_ref=edge_ref,
            dst_ref=arrive_ref.at[slot],
            send_sem=edge_send.at[slot],
            recv_sem=edge_recv.at[slot],
            device_id=(lax.rem(me + 1, grid.seq), index["batch"]),
            device_id_type=MESH,
        )
        copy.start()
        copy.wait()
        first = jnp.where(me == 0, 1.0, 0.0)
        prev_ref[slot] = arrive_ref[slot] * (1.0 - first)
        prev_ref[slot, 0:segments, :] += entry_ref[...].astype(F32) * first

    def norm(source_ref, gain, bias):
        step = 64

        def run(i, carry):
            at = pl.ds(pl.multiple_of(i * step, step), step)
            value = source_ref[at, :].astype(F32)
            center = value - jnp.mean(value, axis=-1, keepdims=True)
            spread = jnp.mean(center * center, axis=-1, keepdims=True)
            normed_ref[at, :] = center * lax.rsqrt(spread + 1e-05) * table_ref[gain : gain + 1, :] + table_ref[bias : bias + 1, :]
            return carry

        lax.fori_loop(0, tokens // step, run, 0)

    norm(x_ref, 0, 1)
    swap_edges(att_entry_ref, 0)

    def mix_one(at, current, previous):
        for c in range(4):
            blend = table_ref[2 + c : 3 + c, :]
            mixed_ref[c, at, :] = (current * blend + previous * (1.0 - blend)).astype(BF16)

    for q in range(segments):
        shift_rows(q, normed_ref, 0, mix_one)

    def project_to(array, slot, left, target_ref):
        copy = load(array, first_piece(array), wide_ref, slot)
        copy.wait()

        def run(n, carry):
            value = dot(left[...], weight(wide_ref, slot, tile(n)), 1, 0)
            target_ref[:, tile(n)] = value.astype(target_ref.dtype)
            return carry

        lax.fori_loop(0, width // 256, run, 0)

    project_to(1, 0, mixed_ref.at[1], k_ref)
    project_to(2, 1, mixed_ref.at[2], v_ref)
    ones, ones16 = block_ones(F32), block_ones(BF16)
    group = lax.div(me * rows, LANES)
    own_log = table_ref[6:7, pl.ds(pl.multiple_of(group * LANES, LANES), LANES)]
    fade_ref[...] = column_of(jnp.exp(-length * jnp.exp(own_log)), length)

    def columns(p):
        return pl.ds(pl.multiple_of(p * LANES, LANES), LANES)

    def rate_of(p):
        return jnp.exp(table_ref[6:7, columns(p)])

    def own_states(p, carry):
        _, _, end = decays(rate_of(p), length)
        both = []
        for q in range(segments):
            token = pl.ds(q * length, length)
            k_end = k_ref[token, columns(p)].astype(F32) * end
            both.append(dot2(k_end, v_ref[token, columns(p)], 0, 0, "own"))
        own_ref[columns(p), :] = fold(both[0], both[1], ones).astype(BF16)
        return carry

    lax.fori_loop(0, pairs, own_states, 0)
    first = exchange(grid, index, own_ref, got_ref, rows, send_a, recv_a)
    project_to(3, 0, mixed_ref.at[0], r_ref)
    project_to(4, 1, mixed_ref.at[3], gate_ref)
    for copy in first:
        copy.wait_recv()
    state = start_ref[...]
    fade = fade_ref[pl.ds(pl.multiple_of(lax.rem(me * rows, LANES), rows), rows), :]
    for block in range(grid.seq):
        at = pl.ds(block * rows, rows)
        out_ref[at, :] = state.astype(BF16)
        state = fade * state + got_ref[at, :].astype(F32)
    second = exchange(grid, index, out_ref, begin_ref, rows, send_b, recv_b)
    gather.pump()

    later = lax.broadcasted_iota(jnp.int32, (length, length), 0) > lax.broadcasted_iota(
        jnp.int32, (length, length), 1
    )
    for copy in second:
        copy.wait_recv()

    def inside(p, carry):
        down, up, _ = decays(rate_of(p), length)
        pick = half_masks(length)
        begin = begin_ref[columns(p), :].astype(F32)
        for q in range(segments):
            token = pl.ds(q * length, length)
            r = r_ref[token, columns(p)].astype(F32)
            k = k_ref[token, columns(p)].astype(F32)
            v = v_ref[token, columns(p)]
            r_down = r * down
            k_up = k * up
            halves = []
            for h in range(2):
                r_head = jnp.where(pick == (h == 0), r_down, 0.0)
                scores = jnp.where(later, dot3(r_head, k_up, 1, 1, "score"), 0.0)
                halves.append(dot2(scores, v, 1, 0, "inner"))
            inner = jnp.where(pick, halves[0], halves[1])
            self_part = head_sum(r * table_ref[7:8, columns(p)] * k, ones16)
            inner = inner + self_part * v.astype(F32)
            state16 = unfold(begin, q, ones).astype(BF16)
            y = (inner + dot2(r_down, state16, 1, 0, "cross")).astype(BF16)
            wkv_ref[token, columns(p)] = y
            center = y.astype(F32) - dot(y, ones16, 1, 0) * (1.0 / SUBSPACE_EXTENT)
            spread = head_sum(center * center, ones16) * (1.0 / SUBSPACE_EXTENT)
            z = center * lax.rsqrt(spread + 0.00064)
            normalized = z * table_ref[8:9, columns(p)] + table_ref[9:10, columns(p)]
            g = gate_ref[token, columns(p)]
            attended_ref[token, columns(p)] = (normalized * g / (1.0 + jnp.exp(-g))).astype(BF16)
        return carry

    for quarter in range(4):
        lax.fori_loop(quarter * pairs // 4, (quarter + 1) * pairs // 4, inside, 0)
        gather.pump()

    copy = load(5, first_piece(5), wide_ref, 0)
    copy.wait()

    def out_project(n, carry):
        value = dot(attended_ref[...], weight(wide_ref, 0, tile(n)), 1, 0)
        middle_ref[:, tile(n)] = x_ref[:, tile(n)].astype(F32) + value
        return carry

    lax.fori_loop(0, width // 256, out_project, 0)
    norm(middle_ref, 10, 11)
    swap_edges(ffn_entry_ref, 1)

    def mix_two(at, current, previous):
        for c in range(2):
            blend = table_ref[12 + c : 13 + c, :]
            mixed2_ref[c, at, :] = (current * blend + previous * (1.0 - blend)).astype(BF16)

    for q in range(segments):
        shift_rows(q, normed_ref, 1, mix_two)
    copy = load(6, first_piece(6), wide_ref, 1)
    copy.wait()

    def receive(n, carry):
        value = dot(mixed2_ref[1], weight(wide_ref, 1, tile(n)), 1, 0)
        recv = 1.0 / (1.0 + jnp.exp(-value))
        recv_ref[:, tile(n)] = recv
        d_carried_ref[:, tile(n)] = (recv * up_ref[:, tile(n)].astype(F32)).astype(BF16)
        return carry

    lax.fori_loop(0, width // 256, receive, 0)

    for piece in range(starts[7], starts[8]):
        slot = (piece - starts[7]) % 2
        column, size = span(plan[piece])
        copy = load(7, piece, wide_ref, slot)
        copy.wait()

        def key(n, carry):
            value = jnp.maximum(dot(mixed2_ref[0], weight(wide_ref, slot, tile(n)), 1, 0), 0.0)
            hidden_ref[:, pl.ds(pl.multiple_of(column + n * 256, 256), 256)] = (value * value).astype(BF16)
            return carry

        lax.fori_loop(0, size // 256, key, 0)
    for piece in range(starts[8], len(plan)):
        slot = (piece - starts[8]) % 2
        column, size = span(plan[piece])
        copy = load(8, piece, tall_ref, slot)
        copy.wait()
        window = pl.ds(column, size)

        def carry_out(m, carry):
            at = tile(m, 256)
            carried = dot(hidden_ref[at, :], weight(tall_ref, slot, pl.ds(0, size)), 1, 0)
            recv = recv_ref[at, window]
            result_ref[at, window] = (middle_ref[at, window] + recv * carried).astype(BF16)
            upstream = up_ref[at, window].astype(F32)
            d_recv_ref[at, window] = (recv * (1.0 - recv) * carried * upstream).astype(BF16)
            return carry

        lax.fori_loop(0, tokens // 256, carry_out, 0)

    for copy in first + second:
        copy.wait_send()
    gather.close()


def forward(grid, x, upstream, att_entry, ffn_entry, start, shards, length):
    tokens, width = x.shape
    steps = [LANES] + [CHUNK] * 7 + [TALL]
    plan, starts = gather_plan([(s.shape[1], step) for s, step in zip(shards, steps)])
    total = sum(len(unit[1]) for unit in plan)
    hidden = shards[7].shape[1]
    vmem = pl.BlockSpec(memory_space=pltpu.VMEM)
    anywhere = pl.BlockSpec(memory_space=pl.ANY)
    flat = jax.ShapeDtypeStruct((tokens, width), BF16)
    flat32 = jax.ShapeDtypeStruct((tokens, width), F32)
    state = pltpu.VMEM((width, LANES), BF16)
    sems = pltpu.SemaphoreType.DMA((grid.seq - 1,))
    count = total * sum(size - 1 for size in grid.shape)
    return pl.pallas_call(
        functools.partial(forward_kernel, grid, length, plan, starts),
        out_shape=[jax.ShapeDtypeStruct(grid.shape + s.shape, s.dtype) for s in shards]
        + [
            flat, jax.ShapeDtypeStruct((16, width), F32), jax.ShapeDtypeStruct((4, tokens, width), BF16),
            flat, flat, flat, flat32, flat, flat, jax.ShapeDtypeStruct((width, LANES), BF16),
            flat32, jax.ShapeDtypeStruct((2, tokens, width), BF16), jax.ShapeDtypeStruct((tokens, hidden), BF16),
            flat, flat, jax.ShapeDtypeStruct((2, 8, width), F32),
        ],
        in_specs=[vmem] * 5 + [anywhere] * 9,
        out_specs=[anywhere] * 9 + [vmem] * 16,
        scratch_shapes=[
            pltpu.VMEM((tokens, width), F32),
            pltpu.VMEM((2,) + grid.shape + (shards[1].shape[0], CHUNK), BF16),
            pltpu.VMEM((2,) + grid.shape + (shards[8].shape[0], TALL), BF16),
            pltpu.VMEM(grid.shape + shards[0].shape, BF16),
            pltpu.VMEM((8, width), F32),
            pltpu.VMEM((2, 8, width), F32),
            pltpu.VMEM((tokens, width), F32),
            state, state, state,
            pltpu.VMEM((LANES, LANES), F32),
            pltpu.SemaphoreType.DMA((total,)),
            pltpu.SemaphoreType.DMA((count,)),
            pltpu.SemaphoreType.DMA((count,)),
            pltpu.SemaphoreType.DMA((2,)),
            pltpu.SemaphoreType.DMA((2,)),
            pltpu.SemaphoreType.DMA((2,)),
            sems, sems, sems, sems,
        ],
        compiler_params=pltpu.CompilerParams(
            collective_id=0, has_side_effects=True, vmem_limit_bytes=VMEM_LIMIT
        ),
    )(x, upstream, att_entry, ffn_entry, start, *shards)


STAGES = ("c", "first", "second", "z")
GAPS = (1, 2, 2, 2)


class Piece:
    def __init__(self, array, column, columns, tile, first, kind):
        self.array, self.column, self.columns = array, column, columns
        self.first, self.second = (first, "y" if first == "x" else "x")
        self.tile, self.kind = (tile, columns), kind
        self.group = (tile, columns, first, jnp.dtype(kind).name)


def scatter_plan(arrays):
    units, of_array, counts = [], [], {}
    for array, (tile, columns, step, kind) in enumerate(arrays):
        mine = []
        at = 0
        while at < columns:
            unit = []
            for first in ("x", "y"):
                if at < columns:
                    piece = Piece(array, at, step, tile, first, kind)
                    piece.place = counts.get(piece.group, 0)
                    counts[piece.group] = piece.place + 1
                    unit.append(piece)
                    at += step
            mine.append(len(units))
            units.append(unit)
        of_array.append(mine)
    return units, of_array, counts


def stage_shapes(grid, group):
    tile, columns, first, _ = group
    second = "y" if first == "x" else "x"
    end = (tile, columns)
    return [
        grid.sizes("c") + end,
        (grid.size[first] - 1,) + grid.sizes("c" + first) + end,
        (grid.size[second] - 1,) + grid.sizes("cxy") + end,
        (grid.size["z"] - 1,) + end,
    ]


class Scatter:
    def __init__(self, grid, index, digit, units, keeps, gives, landings, loads, outs, send_sem, recv_sem, load_sem):
        self.grid, self.index, self.digit, self.units = grid, index, digit, units
        self.keeps, self.gives, self.landings, self.loads, self.outs = keeps, gives, landings, loads, outs
        self.send_sem, self.recv_sem, self.load_sem = send_sem, recv_sem, load_sem
        self.started, self.pending, self.giving = [], {}, {}
        self.stage, self.when, self.now = {}, {}, 0

    def copy(self, source, target, name, digit):
        slot = len(self.started)
        copy = pltpu.make_async_remote_copy(
            src_ref=source,
            dst_ref=target,
            send_sem=self.send_sem.at[slot],
            recv_sem=self.recv_sem.at[slot],
            device_id=self.grid.peer(self.index, self.digit, name, digit),
            device_id_type=MESH,
        )
        copy.start()
        self.started.append([copy, True])
        return copy

    def open(self, unit, number):
        piece = self.units[unit][number]
        if piece.group in self.giving:
            entry = self.giving.pop(piece.group)
            entry[0].wait_send()
            entry[1] = False
        return self.keeps[unit, number], self.gives[piece.group]

    def give(self, unit):
        for number, piece in enumerate(self.units[unit]):
            target = lax.rem(self.digit["c"] + 1, 2)
            copy = self.copy(self.gives[piece.group], self.landings[piece.group][0].at[piece.place], "c", target)
            self.giving[piece.group] = self.started[-1]
            self.pending[unit, number] = [copy]
        self.stage[unit], self.when[unit] = 0, self.now

    def load(self, unit, number):
        piece, stage = self.units[unit][number], self.stage[unit]
        for copy in self.pending[unit, number]:
            copy.wait_recv()
        copy = pltpu.make_async_copy(
            self.landings[piece.group][stage].at[piece.place],
            self.loads[piece.group][stage],
            self.load_sem.at[2 * stage + number],
        )
        copy.start()
        return copy

    def add(self, unit, number, copy):
        piece, stage = self.units[unit][number], self.stage[unit]
        keep, got = self.keeps[unit, number], self.loads[piece.group][stage]
        names = [n for n in self.grid.order if n != "c"]
        fixed = ((), (piece.first,), (piece.first, piece.second), ("x", "y", "z"))[stage]
        free = [n for n in names if n not in fixed]
        copy.wait()
        terms = 1 if stage == 0 else got.shape[0]
        steps = 1
        for n in free:
            steps *= self.grid.size[n]

        def body(i, carry):
            at, rest = {n: self.digit[n] for n in fixed}, i
            for n in reversed(free):
                at[n] = lax.rem(rest, self.grid.size[n])
                rest = lax.div(rest, self.grid.size[n])
            where, inner = tuple(at[n] for n in names), tuple(at[n] for n in free)
            value = keep[where].astype(F32)
            for j in range(terms):
                value = value + got[inner if stage == 0 else (j,) + inner].astype(F32)
            if stage == 3:
                self.outs[piece.array][:, piece.column : piece.column + piece.columns] = value
            else:
                keep[where] = value.astype(keep.dtype)
            return carry

        if steps == 1:
            body(0, 0)
        else:
            lax.fori_loop(0, steps, body, 0)
        if stage == 3:
            return
        name = (piece.first, piece.second, "z")[stage]
        held = {n: self.digit[n] for n in fixed}
        copies = []
        for j in range(1, self.grid.size[name]):
            target = lax.rem(self.digit[name] + j, self.grid.size[name])
            source = self.grid.at(keep, "c", **held, **{name: target})
            copies.append(self.copy(source, self.landings[piece.group][stage + 1].at[piece.place, j - 1], name, target))
        self.pending[unit, number] = copies

    def tick(self, gaps=GAPS):
        work = []
        for stage in (3, 2, 1, 0):
            waiting = [u for u in sorted(self.stage) if self.stage[u] == stage]
            if waiting and self.now - self.when[waiting[0]] >= gaps[stage]:
                work.append(waiting[0])
        copies = {}
        for unit in work:
            for number in range(len(self.units[unit])):
                copies[unit, number] = self.load(unit, number)
        for unit in work:
            for number in range(len(self.units[unit])):
                self.add(unit, number, copies[unit, number])
            self.stage[unit] += 1
            self.when[unit] = self.now
            if self.stage[unit] == 4:
                del self.stage[unit]
        self.now += 1

    def close(self):
        while self.stage:
            self.tick((1, 1, 1, 1))
        for copy, waiting in self.started:
            if waiting:
                copy.wait_send()


def backward_kernel(grid, length, units, of_array, groups, *refs):
    it = iter(refs)

    def take(count):
        return [next(it) for _ in range(count)]

    (table_ref, prev_ref, begin_ref) = take(3)
    (
        x_hbm, up_hbm, mixed_hbm, r_hbm, k_hbm, v_hbm, gate_hbm, wkv_hbm, attended_hbm, middle_hbm, mixed2_hbm,
        hidden_hbm, d_carried_hbm, d_recv_hbm,
    ) = take(14)
    w_k, w_v, w_r, w_g, w_o, f_r, f_k, f_v = take(8)
    (d_input_ref,) = take(1)
    outs = take(len(of_array))
    landings = {group: take(4) for group in groups}
    keeps = {(u, n): next(it) for u, unit in enumerate(units) for n in range(len(unit))}
    gives = {group: next(it) for group in groups}
    loads = {group: take(4) for group in groups}
    (
        hid, dc, dr, m2, dkey, wide, tall, dn, db, mid, nrm, up, dmid, rr, kk, vv, wk, dgate,
        own_ref, got_ref, out_ref, end_ref, fade_ref, acc, edge_ref, arrive_ref,
        send_sem, recv_sem, load_sem, in_sem, wide_sem, edge_send, edge_recv, send_a, recv_a, send_b, recv_b,
    ) = it
    index, digit = grid.place()
    me = index["seq"]
    tokens, width = dc.shape
    segments = tokens // length
    pairs, rows = width // LANES, width // grid.seq
    n0 = grid.shape[0]
    c_at = grid.order.index("c") - 1
    scatter = Scatter(grid, index, digit, units, keeps, gives, landings, loads, outs, send_sem, recv_sem, load_sem)
    batch_roles = [n for n in grid.order if grid.axis[n] == "batch"]
    peers = [
        grid.peer(index, digit, n, lax.rem(digit[n] + j, grid.size[n])) for n in batch_roles for j in range(1, grid.size[n])
    ]
    peers += [(lax.rem(me + j, grid.seq), index["batch"]) for j in range(1, grid.seq)]

    fetched = {}

    def fetch(name, source, target, slot):
        copy = pltpu.make_async_copy(source, target, in_sem.at[slot])
        copy.start()
        fetched[name] = copy

    def have(*names):
        for name in names:
            fetched.pop(name).wait()

    fetch("hid", hidden_hbm, hid, 0)
    fetch("dc", d_carried_hbm, dc, 1)
    fetch("tall", f_v.at[0], tall, 2)
    fetch("m2", mixed2_hbm, m2, 3)
    fetch("dr", d_recv_hbm, dr, 4)
    fetch("mid", middle_hbm, mid, 5)
    fetch("up", up_hbm, up, 6)
    fetch("att", attended_hbm, dgate, 7)
    fetch("rr", r_hbm, rr, 8)
    fetch("kk", k_hbm, kk, 9)
    fetch("vv", v_hbm, vv, 10)
    fetch("wk", wkv_hbm, wk, 11)
    acc[...] = jnp.zeros_like(acc)
    greet(peers)

    everything = (slice(None),) * 5

    def weight_load(array, column, columns, slot):
        copy = pltpu.make_async_copy(
            array.at[everything + (pl.ds(column, columns),)],
            wide.at[(slot,) + everything + (pl.ds(0, columns),)],
            wide_sem.at[slot],
        )
        copy.start()
        return copy

    def weight(slot, columns):
        return wide[(slot,) + everything + (pl.ds(0, columns),)].reshape((-1, columns))

    def tile(n, step):
        return pl.ds(pl.multiple_of(n * step, step), step)

    def gradient(unit, left_ref, right_ref):
        parts = units[unit]
        targets = [scatter.open(unit, number) for number in range(len(parts))]
        span, narrow = left_ref.shape[1] // n0, parts[0].columns < 256
        for batch in [list(range(len(parts)))] if narrow else [[number] for number in range(len(parts))]:
            first = parts[batch[0]]
            width_all = sum(parts[number].columns for number in batch)

            def run(y, carry, batch=batch, first=first, width_all=width_all):
                total = dot(left_ref[:, tile(y, span)], right_ref[:, first.column : first.column + width_all], 0, 0)
                is_zero = digit["c"] == 0
                for number in batch:
                    keep, give = targets[number]
                    at = parts[number].column - first.column
                    value = total[:, at : at + parts[number].columns].reshape(grid.shape[1:] + parts[number].tile)
                    zero = value[(slice(None),) * c_at + (0,)]
                    one = value[(slice(None),) * c_at + (1,)]
                    keep[y] = jnp.where(is_zero, zero, one).astype(keep.dtype)
                    give[y] = jnp.where(is_zero, one, zero).astype(give.dtype)
                return carry

            lax.fori_loop(0, n0, run, 0)
        scatter.give(unit)

    U = dict(zip(("fv", "fr", "fk", "o", "g", "r", "k", "v", "small"), of_array))

    have("hid", "dc")
    for unit in U["fv"]:
        gradient(unit, hid, dc)
        scatter.tick()
    span = hid.shape[1] // n0
    loading = weight_load(f_r, 0, width, 0)
    for y in range(n0):
        have("tall")

        def key(m, carry, y=y):
            at = tile(m, 128)
            window = slice(y * span, (y + 1) * span)
            d_hidden = dot(dc[at, :], tall[...].reshape((span, width)), 1, 1)
            dkey[at, window] = (2.0 * jnp.sqrt(hid[at, window].astype(F32)) * d_hidden).astype(BF16)
            return carry

        lax.fori_loop(0, tokens // 128, key, 0)
        if y + 1 < n0:
            fetch("tall", f_v.at[y + 1], tall, 2)
    have("m2", "dr")
    gradient(U["fr"][0], m2.at[1], dr)
    fetch("mx0", mixed_hbm.at[0], hid.at[:, pl.ds(0, width)], 0)
    fetch("mx1", mixed_hbm.at[1], hid.at[:, pl.ds(width, width)], 1)
    fetch("mx2", mixed_hbm.at[2], hid.at[:, pl.ds(2 * width, width)], 2)
    scatter.tick()
    loading.wait()
    chunks = pieces(hid.shape[1], CHUNK)
    loading = weight_load(f_k, *chunks[0], 1)

    def through_recv(m, carry):
        at = tile(m, 256)
        db[at, :] = dot(dr[at, :], weight(0, width), 1, 1)
        return carry

    lax.fori_loop(0, tokens // 256, through_recv, 0)
    for number, unit in enumerate(U["fk"]):
        gradient(unit, m2.at[0], dkey)
        column, columns = chunks[number]
        slot = (number + 1) % 2
        loading.wait()
        if number + 1 < len(chunks):
            loading = weight_load(f_k, *chunks[number + 1], 1 - slot)

        def through_key(m, carry, number=number, column=column, columns=columns, slot=slot):
            at = tile(m, 256)
            value = dot(dkey[at, column : column + columns], weight(slot, columns), 1, 1)
            dn[at, :] = value if number == 0 else dn[at, :] + value
            return carry

        lax.fori_loop(0, tokens // 256, through_key, 0)
        scatter.tick()
    fetch("mx3", mixed_hbm.at[3], m2.at[0], 3)
    loading = weight_load(w_o, 0, width, 0)

    step = 64

    def fold_rows(value):
        return jnp.sum(value.reshape((step // 8, 8, width)), axis=0)

    def norm(source_ref, gain, bias):
        def run(i, carry):
            at = tile(i, step)
            value = source_ref[at, :].astype(F32)
            center = value - jnp.mean(value, axis=-1, keepdims=True)
            spread = jnp.mean(center * center, axis=-1, keepdims=True)
            nrm[at, :] = center * lax.rsqrt(spread + 1e-05) * table_ref[gain : gain + 1, :] + table_ref[bias : bias + 1, :]
            return carry

        lax.fori_loop(0, tokens // step, run, 0)

    def swap_edges(slot):
        edge_ref[...] = jnp.zeros_like(edge_ref)
        for q in range(segments):
            edge_ref[q : q + 1, :] = db[q * length : q * length + 8, :][0:1, :]
        copy = pltpu.make_async_remote_copy(
            src_ref=edge_ref,
            dst_ref=arrive_ref.at[slot],
            send_sem=edge_send.at[slot],
            recv_sem=edge_recv.at[slot],
            device_id=(lax.rem(me + grid.seq - 1, grid.seq), index["batch"]),
            device_id_type=MESH,
        )
        copy.start()
        return copy

    def norm_back(source_ref, gain, bias, slot, base_ref, put):
        keep_next = jnp.where(me == grid.seq - 1, 0.0, 1.0)
        for q in range(segments):
            count = length // step

            def run(i, carry, q=q):
                at = tile(q * count + count - 1 - i, step)
                value = source_ref[at, :].astype(F32)
                center = value - jnp.mean(value, axis=-1, keepdims=True)
                spread = jnp.mean(center * center, axis=-1, keepdims=True)
                scale = lax.rsqrt(spread + 1e-05)
                z = center * scale
                before = db[at, :]
                row = lax.broadcasted_iota(jnp.int32, (step, 1), 0)
                d_normed = dn[at, :] + jnp.where(row == step - 1, carry, pltpu.roll(before, step - 1, 0))
                acc[gain] += fold_rows(z * d_normed)
                acc[bias] += fold_rows(d_normed)
                e = d_normed * table_ref[gain : gain + 1, :]
                back = (e - jnp.mean(e, axis=-1, keepdims=True) - z * jnp.mean(e * z, axis=-1, keepdims=True)) * scale
                put(at, base_ref[at, :].astype(F32) + back)
                return before[0:1, :]

            lax.fori_loop(0, count, run, arrive_ref[slot, q : q + 1, :] * keep_next)

    have("mid")
    norm(mid, 10, 11)
    for q in range(segments):

        def blend_two(i, carry, q=q):
            at = tile(q * (length // step) + i, step)
            current = nrm[at, :]
            row = lax.broadcasted_iota(jnp.int32, (step, 1), 0)
            difference = current - jnp.where(row == 0, carry, pltpu.roll(current, 1, 0))
            first, second = dn[at, :], db[at, :]
            acc[12] += fold_rows(difference * first)
            acc[13] += fold_rows(difference * second)
            a, b = table_ref[12:13, :], table_ref[13:14, :]
            dn[at, :] = first * a + second * b
            db[at, :] = first * (1.0 - a) + second * (1.0 - b)
            return current[step - 1 : step, :]

        lax.fori_loop(0, length // step, blend_two, prev_ref[1, q : q + 1, :])
    moving = swap_edges(0)
    scatter.tick()
    have("up")
    moving.wait()

    def put_middle(at, value):
        dmid[at, :] = value
        dr[at, :] = value.astype(BF16)

    norm_back(mid, 10, 11, 0, up, put_middle)
    fetch("mid", gate_hbm, mid, 5)
    fetch("up", x_hbm, up, 6)
    have("att")
    gradient(U["o"][0], dgate, dr)
    loading.wait()

    def through_out(m, carry):
        at = tile(m, 256)
        nrm[at, :] = dot(dr[at, :], weight(0, width), 1, 1)
        return carry

    lax.fori_loop(0, tokens // 256, through_out, 0)
    scatter.tick()

    ones, ones16 = block_ones(F32), block_ones(BF16)
    share = 1.0 / SUBSPACE_EXTENT

    def columns(p, base=0):
        return pl.ds(pl.multiple_of(base + p * LANES, LANES), LANES)

    def rate_of(p):
        return jnp.exp(table_ref[6:7, columns(p)])

    group = lax.div(me * rows, LANES)
    own_log = table_ref[6:7, pl.ds(pl.multiple_of(group * LANES, LANES), LANES)]
    fade_ref[...] = column_of(jnp.exp(-length * jnp.exp(own_log)), length)
    have("wk", "mid", "rr")

    def own_states(p, carry):
        down, _, _ = decays(rate_of(p), length)
        both = []
        gain_sum, bias_sum = jnp.zeros((1, LANES), F32), jnp.zeros((1, LANES), F32)
        for q in range(segments):
            token = pl.ds(q * length, length)
            y = wk[token, columns(p)]
            center = y.astype(F32) - dot(y, ones16, 1, 0) * share
            spread = head_sum(center * center, ones16) * share
            scale = lax.rsqrt(spread + 0.00064)
            z = center * scale
            gain = table_ref[8:9, columns(p)]
            normalized = z * gain + table_ref[9:10, columns(p)]
            g = mid[token, columns(p)]
            s = 1.0 / (1.0 + jnp.exp(-g))
            d_att = nrm[token, columns(p)]
            dgate[token, columns(p)] = (d_att * normalized * s * (1.0 + g * (1.0 - s))).astype(BF16)
            d_norm = d_att * g * s
            gain_sum = gain_sum + jnp.sum(d_norm * z, axis=0, keepdims=True)
            bias_sum = bias_sum + jnp.sum(d_norm, axis=0, keepdims=True)
            e = d_norm * gain
            dy = ((e - head_sum(e, ones16) * share - z * (head_sum(e * z, ones16) * share)) * scale).astype(BF16)
            dc[token, columns(p)] = dy
            both.append(dot2(rr[token, columns(p)].astype(F32) * down, dy, 0, 0, "own"))
        acc[8, 0:1, columns(p)] = gain_sum
        acc[9, 0:1, columns(p)] = bias_sum
        own_ref[columns(p), :] = fold(both[0], both[1], ones).astype(BF16)
        return carry

    lax.fori_loop(0, pairs, own_states, 0)
    first = exchange(grid, index, own_ref, got_ref, rows, send_a, recv_a)
    have("mx3")
    gradient(U["g"][0], m2.at[0], dgate)
    scatter.tick()
    for copy in first:
        copy.wait_recv()
    fade = fade_ref[pl.ds(pl.multiple_of(lax.rem(me * rows, LANES), rows), rows), :]
    state = jnp.zeros_like(fade)
    for block in reversed(range(grid.seq)):
        at = pl.ds(block * rows, rows)
        out_ref[at, :] = state.astype(BF16)
        state = fade * state + got_ref[at, :].astype(F32)
    second = exchange(grid, index, out_ref, end_ref, rows, send_b, recv_b)
    have("up")
    norm(up, 0, 1)
    have("kk", "vv")
    for copy in second:
        copy.wait_recv()
    later = lax.broadcasted_iota(jnp.int32, (length, length), 0) > lax.broadcasted_iota(
        jnp.int32, (length, length), 1
    )
    time = lax.broadcasted_iota(jnp.int32, (length, LANES), 0).astype(F32)

    def inside(p, carry):
        rate = rate_of(p)
        reward = table_ref[7:8, columns(p)]
        down, up_, end = decays(rate, length)
        pick = half_masks(length)
        begins, ends = begin_ref[columns(p), :].astype(F32), end_ref[columns(p), :].astype(F32)
        reward_sum, rate_sum = jnp.zeros((1, LANES), F32), jnp.zeros((1, LANES), F32)
        for q in range(segments):
            token = pl.ds(q * length, length)
            r = rr[token, columns(p)].astype(F32)
            k = kk[token, columns(p)].astype(F32)
            v = vv[token, columns(p)]
            dy = dc[token, columns(p)]
            begin, finish = unfold(begins, q, ones), unfold(ends, q, ones)
            begin16, finish16 = begin.astype(BF16), finish.astype(BF16)
            r_down = (r * down).astype(BF16)
            k_up = (k * up_).astype(BF16)
            k_end = k * end
            zero = jnp.zeros_like(r_down)
            d_r, d_k, d_v = [], [], []
            for h in range(2):
                here = pick == (h == 0)
                scores = jnp.where(later, dot(jnp.where(here, r_down, zero), k_up, 1, 1), 0.0)
                d_scores = jnp.where(later, dot(jnp.where(here, dy, zero), v, 1, 1), 0.0).astype(BF16)
                d_r.append(dot(d_scores, k_up, 1, 0))
                d_k.append(dot(d_scores, r_down, 0, 0))
                d_v.append(dot2(scores, dy, 0, 0, "inner"))
            from_r = jnp.where(pick, d_r[0], d_r[1]) + dot(dy, begin16, 1, 1)
            from_k = jnp.where(pick, d_k[0], d_k[1])
            from_end = dot(v, finish16, 1, 1)
            v32, dy32 = v.astype(F32), dy.astype(F32)
            v_dy = head_sum(v32 * dy32, ones16)
            self_part = head_sum(r * reward * k, ones16)
            dkey[token, columns(p)] = (from_r * down + reward * k * v_dy).astype(BF16)
            dkey[token, columns(p, width)] = (from_k * up_ + from_end * end + reward * r * v_dy).astype(BF16)
            dkey[token, columns(p, 2 * width)] = (
                jnp.where(pick, d_v[0], d_v[1]) + dot2(k_end, finish16, 1, 0, "cross") + self_part * dy32
            ).astype(BF16)
            reward_sum = reward_sum + jnp.sum(r * k * v_dy, axis=0, keepdims=True)
            terms = (
                (time + 1.0) * k_up.astype(F32) * from_k
                - time * r_down.astype(F32) * from_r
                - (length - 1.0 - time) * k_end * from_end
            )
            through = lax.dot_general(
                jnp.ones((8, LANES), F32), begin * finish, (((1,), (1,)), ((), ())),
                precision=lax.Precision.HIGHEST, preferred_element_type=F32,
            )[0:1, :]
            rate_sum = rate_sum + jnp.sum(terms, axis=0, keepdims=True) - length * jnp.exp(-rate * length) * through
        acc[7, 0:1, columns(p)] = reward_sum
        acc[6, 0:1, columns(p)] = rate_sum * rate
        return carry

    for quarter in range(4):
        lax.fori_loop(quarter * pairs // 4, (quarter + 1) * pairs // 4, inside, 0)
        scatter.tick()
    have("mx0", "mx1", "mx2")
    weights = (w_r, w_k, w_v, w_g)
    grads = [dkey.at[:, pl.ds(c * width, width)] for c in range(3)] + [dgate]

    def load_rows(y):
        copies = []
        for c in range(4):
            copy = pltpu.make_async_copy(weights[c].at[y], wide.at[c // n0, c % n0], in_sem.at[8 + c])
            copy.start()
            copies.append(copy)
        return copies

    loading = load_rows(0)
    for c, name in enumerate("rkv"):
        gradient(U[name][0], hid.at[:, pl.ds(c * width, width)], grads[c])
    scatter.tick()
    span = width // n0
    for y in range(n0):
        for copy in loading:
            copy.wait()
        window = slice(y * span, (y + 1) * span)

        def through_mix(m, carry, y=y, window=window):
            at = tile(m, 128)
            current = nrm[at, window]
            above = nrm[pl.ds(pl.multiple_of(jnp.maximum(m * 128 - 8, 0), 8), 8), window][7:8, :]
            segment = lax.div(m, length // 128)
            given = prev_ref[0, 0:1, window]
            for q in range(1, segments):
                given = jnp.where(segment == q, prev_ref[0, q : q + 1, window], given)
            carried = jnp.where(lax.rem(m, length // 128) == 0, given, above)
            row = lax.broadcasted_iota(jnp.int32, (128, 1), 0)
            difference = current - jnp.where(row == 0, carried, pltpu.roll(current, 1, 0))
            here, before = None, None
            for c in range(4):
                value = dot(grads[c][at, :], wide[c // n0, c % n0].reshape((span, width)), 1, 1)
                acc[2 + c, :, window] += jnp.sum((difference * value).reshape((16, 8, span)), axis=0)
                blend = table_ref[2 + c : 3 + c, window]
                here = blend * value if c == 0 else here + blend * value
                before = (1.0 - blend) * value if c == 0 else before + (1.0 - blend) * value
            dn[at, window] = here
            db[at, window] = before
            return carry

        lax.fori_loop(0, tokens // 128, through_mix, 0)
        if y + 1 < n0:
            loading = load_rows(y + 1)
        scatter.tick()
    moving = swap_edges(1)
    scatter.tick()
    moving.wait()

    def put_input(at, value):
        d_input_ref[at, :] = value.astype(BF16)

    norm_back(up, 0, 1, 1, dmid, put_input)

    sums = [jnp.sum(acc[i], axis=0, keepdims=True) for i in range(14)]
    for i in range(14):
        edge_ref[0:1, :] = sums[i]
        nrm[i : i + 1, :] = edge_ref[0:1, :]
    nrm[14:16, :] = jnp.zeros((2, width), F32)
    keep, give = scatter.open(U["small"][0], 0)
    per = grid.seq * grid.batch // pairs
    names = [n for n in grid.order if n != "c"]

    def spread(i, carry):
        at, rest = {}, i
        for n in reversed(names):
            at[n] = lax.rem(rest, grid.size[n])
            rest = lax.div(rest, grid.size[n])
        for target, core in ((keep, digit["c"]), (give, 1 - digit["c"])):
            spot = dict(at, c=core)
            rank = 0
            for n in grid.order:
                rank = rank * grid.size[n] + spot[n]
            target[tuple(at[n] for n in names)] = nrm[0:16, columns(lax.div(rank, per))]
        return carry

    steps = 1
    for n in names:
        steps *= grid.size[n]
    lax.fori_loop(0, steps, spread, 0)
    scatter.give(U["small"][0])
    for copy in first + second:
        copy.wait_send()
    scatter.close()


def backward(grid, length, table, prev, begin, stored, weights):
    tokens, width = stored[0].shape
    hidden = stored[11].shape[1]
    blk, tall = weights[0].shape[4], weights[7].shape[4]
    arrays = [
        (tall, width, LANES, BF16), (blk, width, 512, BF16), (blk, hidden, 512, BF16), (blk, width, 512, BF16),
        (blk, width, 512, BF16), (blk, width, 512, BF16), (blk, width, 512, BF16), (blk, width, 512, BF16),
        (16, LANES, LANES, F32),
    ]
    units, of_array, counts = scatter_plan(arrays)
    groups = list(counts)
    kinds = {group: jnp.dtype(group[3]) for group in groups}
    shapes = {group: stage_shapes(grid, group) for group in groups}
    vmem = pl.BlockSpec(memory_space=pltpu.VMEM)
    anywhere = pl.BlockSpec(memory_space=pl.ANY)
    flat16, flat32 = pltpu.VMEM((tokens, width), BF16), pltpu.VMEM((tokens, width), F32)
    state = pltpu.VMEM((width, LANES), BF16)
    sems = pltpu.SemaphoreType.DMA((grid.seq - 1,))
    dma = pltpu.SemaphoreType.DMA
    count = sum(len(unit) for unit in units) * sum(size - 1 for size in grid.shape)
    landing = [
        jax.ShapeDtypeStruct((counts[group],) + shape, kinds[group]) for group in groups for shape in shapes[group]
    ]
    outs = pl.pallas_call(
        functools.partial(backward_kernel, grid, length, units, of_array, groups),
        out_shape=[jax.ShapeDtypeStruct((tokens, width), BF16)]
        + [jax.ShapeDtypeStruct((a[0], a[1]), F32) for a in arrays]
        + landing,
        in_specs=[vmem] * 3 + [anywhere] * 22,
        out_specs=[vmem] * (1 + len(arrays)) + [anywhere] * len(landing),
        scratch_shapes=[pltpu.VMEM(grid.sizes("c") + p.tile, p.kind) for unit in units for p in unit]
        + [pltpu.VMEM(shapes[group][0], kinds[group]) for group in groups]
        + [pltpu.VMEM(shape, kinds[group]) for group in groups for shape in shapes[group]]
        + [
            pltpu.VMEM((tokens, hidden), BF16), flat16, flat16, pltpu.VMEM((2, tokens, width), BF16),
            pltpu.VMEM((tokens, hidden), BF16),
            pltpu.VMEM((2,) + grid.shape + (blk, CHUNK), BF16),
            pltpu.VMEM(grid.shape[1:] + (tall, width), BF16),
            flat32, flat32, flat32, flat32, flat16, flat32, flat16, flat16, flat16, flat16, flat16,
            state, state, state, state,
            pltpu.VMEM((LANES, LANES), F32),
            pltpu.VMEM((14, 8, width), F32),
            pltpu.VMEM((8, width), F32),
            pltpu.VMEM((2, 8, width), F32),
            dma((count,)), dma((count,)), dma((8,)), dma((12,)), dma((2,)), dma((2,)), dma((2,)),
            sems, sems, sems, sems,
        ],
        compiler_params=pltpu.CompilerParams(
            collective_id=1, has_side_effects=True, vmem_limit_bytes=VMEM_LIMIT
        ),
    )(table, prev, begin, *stored, *weights)
    return outs[0], outs[1 : 1 + len(arrays)]


def local(grid, *args):
    (
        incoming, att_entry, ffn_entry, memory, upstream,
        ln1_gain, ln1_bias, att_mix, w_recept, w_key, w_value, w_gate, decay_log, reward,
        gn_gain, gn_bias, w_out, ln2_gain, ln2_bias, ffn_mix, f_key, f_value, f_recept,
    ) = args
    segments, length, width = incoming.shape
    tokens = segments * length
    ranks = grid.seq * grid.batch
    share = width // ranks

    per = LANES // share
    rank = lax.axis_index(("seq", "batch"))
    small = jnp.stack(
        [ln1_gain, ln1_bias] + [att_mix[:, c] for c in range(4)] + [decay_log, reward, gn_gain, gn_bias, ln2_gain, ln2_bias]
        + [ffn_mix[:, c] for c in range(2)]
    )
    small = jnp.tile(jnp.pad(small, ((0, 2), (0, 0))), (1, per))
    lane = lax.broadcasted_iota(jnp.int32, small.shape, 1)
    small = jnp.where(lane // share == rank % per, small, jnp.zeros_like(small))
    rows = width // grid.seq
    row = lax.axis_index("seq") * rows
    start = memory.transpose(1, 2, 0, 3).reshape(width, segments * SUBSPACE_EXTENT)
    start = lax.dynamic_slice_in_dim(start, row, rows, 0)
    shards = [small, w_key, w_value, w_recept, w_gate, w_out, f_recept, f_key, f_value]
    outs = forward(
        grid, incoming.reshape(tokens, width), upstream.reshape(tokens, width), att_entry, ffn_entry, start, shards, length
    )
    (
        result, table, mixed, r, k, v, gate_pre, wkv, attended, begin, middle, mixed2, hidden, d_carried, d_recv, prev,
    ) = outs[9:]
    stored = [
        incoming.reshape(tokens, width), upstream.reshape(tokens, width), mixed, r, k, v, gate_pre, wkv, attended, middle,
        mixed2, hidden, d_carried, d_recv,
    ]
    d_input, (s_fv, s_fr, s_fk, s_o, s_g, s_r, s_k, s_v, s_small) = backward(
        grid, length, table, prev, begin, stored, outs[1:9]
    )
    s = lax.dynamic_slice_in_dim(s_small, (rank % per) * share, share, 1)
    shape = incoming.shape
    return (
        result.reshape(shape), d_input.reshape(shape),
        s[0], s[1], s[2:6].T, s_r, s_k, s_v, s_g, s[6], s[7], s[8], s[9], s_o, s[10], s[11], s[12:14].T,
        s_fk, s_fv, s_fr,
    )


def solution(mesh):
    grid = Grid(mesh.shape["seq"], mesh.shape["batch"])
    both, rows = P(("seq", "batch")), P(("seq", "batch"), None)
    tokens, entry = P("batch", "seq", None), P("batch", None)
    return jax.shard_map(
        functools.partial(local, grid),
        mesh=mesh,
        in_specs=(
            tokens, entry, entry, P("batch", None, None, None), tokens,
            both, both, rows, rows, rows, rows, rows, both, both, both, both, rows, both, both, rows, rows, rows, rows,
        ),
        out_specs=(
            tokens, tokens, both, both, rows, rows, rows, rows, rows, both, both, both, both, rows, both, both, rows,
            rows, rows, rows,
        ),
        check_vma=False,
    )
```

```python
import functools

import jax
import jax.numpy as jnp
from jax import lax
from jax.experimental import pallas as pl
from jax.experimental.pallas import tpu as pltpu
from jax.sharding import PartitionSpec as P

WKV_PARTITIONS = 16
SUBSPACE_EXTENT = 64
LANES = 128
MESH = pl.DeviceIdType.MESH
F32 = jnp.float32
BF16 = jnp.bfloat16
VMEM_LIMIT = 63 * 1024 * 1024


class Grid:
    def __init__(self, seq, batch):
        self.seq, self.batch = seq, batch
        if seq == 8 and batch == 4:
            digits = [("y", "seq", 4, 2), ("x", "seq", 2, 2), ("c", "seq", 1, 2), ("z", "batch", 1, 4)]
        elif seq == 16 and batch == 8:
            digits = [("y", "seq", 4, 4), ("x", "seq", 1, 4), ("z", "batch", 2, 4), ("c", "batch", 1, 2)]
        else:
            raise ValueError("unknown mesh")
        self.order = [name for name, *_ in digits]
        self.axis = {name: axis for name, axis, *_ in digits}
        self.stride = {name: stride for name, _, stride, _ in digits}
        self.size = {name: size for name, *_, size in digits}
        self.shape = tuple(self.size[name] for name in self.order)

    def place(self):
        index = {"seq": lax.axis_index("seq"), "batch": lax.axis_index("batch")}
        return index, {
            name: (index[self.axis[name]] // self.stride[name]) % self.size[name] for name in self.order
        }

    def peer(self, index, digit, name, target):
        where = dict(index)
        axis = self.axis[name]
        where[axis] = index[axis] + (target - digit[name]) * self.stride[name]
        return (where["seq"], where["batch"])

    def at(self, ref, gone="", **fixed):
        return ref.at[tuple(fixed.get(name, slice(None)) for name in self.order if name not in gone)]

    def sizes(self, gone=""):
        return tuple(self.size[name] for name in self.order if name not in gone)


def greet(peers):
    barrier = pltpu.get_barrier_semaphore()
    for peer in peers:
        pl.semaphore_signal(barrier, inc=1, device_id=peer, device_id_type=MESH)
    pl.semaphore_wait(barrier, len(peers))


def dot(a, b, da, db):
    return lax.dot_general(a, b, (((da,), (db,)), ((), ())), preferred_element_type=F32)


PRECISE = dict(score=0, inner=1, cross=1, own=1, back=0)


def parts_of(value):
    high = value.astype(BF16)
    return high, (value - high.astype(F32)).astype(BF16)


def dot2(a, b, da, db, name):
    if not PRECISE[name]:
        return dot(a.astype(BF16), b, da, db)
    high, low = parts_of(a)
    return dot(high, b, da, db) + dot(low, b, da, db)


def dot3(a, b, da, db, name):
    if not PRECISE[name]:
        return dot(a.astype(BF16), b.astype(BF16), da, db)
    a_high, a_low = parts_of(a)
    b_high, b_low = parts_of(b)
    return dot(a_high, b_high, da, db) + (dot(a_low, b_high, da, db) + dot(a_high, b_low, da, db))


def half_masks(rows):
    lane = lax.broadcasted_iota(jnp.int32, (rows, LANES), 1)
    return lane < SUBSPACE_EXTENT


def block_ones(kind):
    row = lax.broadcasted_iota(jnp.int32, (LANES, LANES), 0) // SUBSPACE_EXTENT
    lane = lax.broadcasted_iota(jnp.int32, (LANES, LANES), 1) // SUBSPACE_EXTENT
    return (row == lane).astype(kind)


def head_sum(value, ones):
    high = value.astype(BF16)
    low = (value - high.astype(F32)).astype(BF16)
    return dot(high, ones, 1, 0) + dot(low, ones, 1, 0)


def decays(rate, length):
    step = lax.broadcasted_iota(jnp.int32, (length, LANES), 0).astype(F32)
    return jnp.exp(-rate * step), jnp.exp(rate * (step + 1.0)), jnp.exp(-rate * (length - 1.0 - step))


def fold(first, second, ones):
    pick = half_masks(LANES)
    a, b = first * ones, second * ones
    a = a + pltpu.roll(a, SUBSPACE_EXTENT, 1)
    b = b + pltpu.roll(b, SUBSPACE_EXTENT, 1)
    return jnp.where(pick, a, b)


def unfold(both, segment, ones):
    pick = half_masks(LANES)
    turned = pltpu.roll(both, SUBSPACE_EXTENT, 1)
    full = jnp.where(pick, both, turned) if segment == 0 else jnp.where(pick, turned, both)
    return full * ones


def exchange(grid, index, source, slots, rows, send_sem, recv_sem):
    me, copies = index["seq"], []
    for j in range(1, grid.seq):
        target = lax.rem(me + j, grid.seq)
        copy = pltpu.make_async_remote_copy(
            src_ref=source.at[pl.ds(pl.multiple_of(target * rows, 16), rows)],
            dst_ref=slots.at[pl.ds(pl.multiple_of(me * rows, 16), rows)],
            send_sem=send_sem.at[j - 1],
            recv_sem=recv_sem.at[j - 1],
            device_id=(target, index["batch"]),
            device_id_type=MESH,
        )
        copy.start()
        copies.append(copy)
    here = pl.ds(pl.multiple_of(me * rows, 16), rows)
    slots[here, :] = source[here, :]
    return copies


CHUNK = 1024
TALL = 256
LAGS = (0, 1, 3)
AHEAD = 4
PUMPS = (
    1, 1, 1, 0, 0, 2, 0, 0, 0, 1, 0, 1, 0, 0, 0, 1, 0, 0, 0, 1, 0, 1, 0, 0, 0, 0, 1, 0, 0, 1, 0, 0, 0, 0, 0, 0, 1, 1, 0, 0, 0,
    1, 0, 1, 0, 0, 1, 0, 0, 0,
)


def pieces(columns, step):
    return [(at, min(step, columns - at)) for at in range(0, columns, step)]


class Gather:
    def __init__(self, grid, index, digit, shards, fulls, plan, own_sem, send_sem, recv_sem):
        self.grid, self.index, self.digit = grid, index, digit
        self.shards, self.fulls, self.plan = shards, fulls, plan
        self.own_sem, self.send_sem, self.recv_sem = own_sem, send_sem, recv_sem
        self.started, self.pending, self.own = [], {}, {}
        self.tick, self.done, self.places = 0, 0, 0

    def others(self, name):
        size = self.grid.size[name]
        return [lax.rem(self.digit[name] + j, size) for j in range(1, size)]

    def send(self, source, place, name):
        copies = []
        for target in self.others(name):
            slot = len(self.started)
            copy = pltpu.make_async_remote_copy(
                src_ref=source,
                dst_ref=place,
                send_sem=self.send_sem.at[slot],
                recv_sem=self.recv_sem.at[slot],
                device_id=self.grid.peer(self.index, self.digit, name, target),
                device_id_type=MESH,
            )
            copy.start()
            self.started.append(copy)
            copies.append(copy)
        return copies

    def stage(self, unit, number):
        if not 0 <= unit < len(self.plan):
            return
        for piece in range(len(self.plan[unit][1])):
            self.step(unit, piece, number)

    def step(self, unit, piece, number):
        array, parts = self.plan[unit]
        column, columns, first, second = parts[piece]
        digit = self.digit
        window = pl.ds(column, columns)
        full = self.fulls[array]
        key = (unit, piece)

        def at(**fixed):
            place = tuple(fixed.get(name, slice(None)) for name in self.grid.order)
            return full.at[place + (slice(None), window)]

        if number == 0:
            place = at(**digit)
            source = self.shards[array].at[:, window]
            copy = pltpu.make_async_copy(source, place, self.own_sem.at[len(self.own)])
            copy.start()
            self.own[key] = copy
            self.pending[key] = self.send(source, place, "z")
            return
        for copy in self.pending[key]:
            copy.wait_recv()
        if number == 1:
            self.own[key].wait()
            fixed, name = {n: digit[n] for n in ("x", "y", "c")}, first
        elif number == 2:
            fixed, name = {n: digit[n] for n in (second, "c")}, second
        elif number == 3:
            fixed, name = {"c": digit["c"]}, "c"
        else:
            self.pending[key] = []
            return
        place = at(**fixed)
        self.pending[key] = self.send(place, place, name)

    def open(self, ahead):
        self.ahead = ahead
        for piece in range(ahead):
            self.stage(piece, 0)

    def pump(self, count=1):
        for _ in range(count):
            tick = self.tick
            self.tick += 1
            for number in (1, 2, 3):
                self.stage(tick - LAGS[number - 1], number)
            self.stage(tick + self.ahead, 0)

    def point(self):
        count = PUMPS[self.places]
        self.places += 1
        self.pump(count if self.tick < len(self.plan) + LAGS[2] + 1 else 0)

    def ready(self, piece):
        while self.tick < piece + LAGS[2] + 1:
            self.pump()
        while self.done <= piece:
            self.stage(self.done, 4)
            self.done += 1

    def close(self):
        for copy in self.started:
            copy.wait_send()


def gather_plan(arrays):
    plan, starts = [], []
    for array, (columns, step) in enumerate(arrays):
        starts.append(len(plan))
        for column, size in pieces(columns, step):
            half = size // 2
            if half % LANES:
                plan.append((array, [(column, size, "x", "y")]))
            else:
                plan.append((array, [(column, half, "x", "y"), (column + half, half, "y", "x")]))
    return plan, starts


def span(unit):
    return unit[1][0][0], sum(part[1] for part in unit[1])


def column_of(row, length):
    at = lax.broadcasted_iota(jnp.int32, (LANES, LANES), 0)
    lane = lax.broadcasted_iota(jnp.int32, (LANES, LANES), 1)
    spread = jnp.where(at == lane, jnp.broadcast_to(row, (LANES, LANES)), 0.0)
    return jnp.broadcast_to(jnp.sum(spread, axis=1, keepdims=True), (LANES, LANES))


def forward_kernel(grid, length, plan, starts, *refs):
    (
        x_ref, up_ref, att_entry_ref, ffn_entry_ref, start_ref, *shards
    ) = refs[:14]
    fulls = refs[14:23]
    result_ref, table_ref, begin_ref, prev_ref = refs[23:27]
    kept = refs[27:39]
    (
        mixed_ref, r_ref, k_ref, v_ref, gate_ref, wkv_ref, attended_ref, middle_ref, mixed2_ref, hidden_ref,
        d_carried_ref, d_recv_ref,
    ) = places = refs[39:51]
    (
        normed_ref, wide_ref, tall_ref, small_ref, edge_ref, arrive_ref, recv_ref,
        own_ref, got_ref, out_ref, fade_ref,
        own_sem, send_sem, recv_sem, load_sem, save_sem, edge_send, edge_recv, send_a, recv_a, send_b, recv_b,
    ) = refs[51:]
    saved = []

    def save(*names):
        for name in names:
            at = [place is name for place in places].index(True)
            copy = pltpu.make_async_copy(name, kept[at], save_sem.at[at])
            copy.start()
            saved.append(copy)

    index, digit = grid.place()
    me = index["seq"]
    tokens, width = x_ref.shape
    segments = tokens // length
    pairs, rows = width // LANES, width // grid.seq
    batch_roles = [n for n in grid.order if grid.axis[n] == "batch"]
    gather = Gather(grid, index, digit, shards, fulls, plan, own_sem, send_sem, recv_sem)
    peers = [grid.peer(index, digit, n, t) for n in batch_roles for t in gather.others(n)]
    peers += [(lax.rem(me + j, grid.seq), index["batch"]) for j in range(1, grid.seq)]
    greet(peers)
    gather.open(AHEAD)
    gather.point()

    def first_piece(array):
        return starts[array]

    def load(piece, buffer, slot):
        gather.ready(piece)
        array = plan[piece][0]
        column, columns = span(plan[piece])
        source = fulls[array].at[(slice(None),) * 5 + (pl.ds(column, columns),)]
        target = buffer.at[(slot,) + (slice(None),) * 5 + (pl.ds(0, columns),)]
        copy = pltpu.make_async_copy(source, target, load_sem.at[slot])
        copy.start()
        gather.point()
        copy.wait()

    def weight(buffer, slot, window):
        value = buffer[(slot,) + (slice(None),) * 5 + (window,)]
        return value.reshape((-1, value.shape[-1]))

    def tile(n, step=256):
        return pl.ds(pl.multiple_of(n * step, step), step)

    def norm(source_ref):
        step = 64

        def run(i, carry):
            at = pl.ds(pl.multiple_of(i * step, step), step)
            value = source_ref[at, :].astype(F32)
            center = value - jnp.mean(value, axis=-1, keepdims=True)
            spread = jnp.mean(center * center, axis=-1, keepdims=True)
            normed_ref[at, :] = center * lax.rsqrt(spread + 1e-05)
            return carry

        lax.fori_loop(0, tokens // step, run, 0)

    norm(x_ref)
    gather.point()

    gather.ready(0)
    copy = pltpu.make_async_copy(fulls[0], small_ref, load_sem.at[0])
    copy.start()
    copy.wait()
    ranks = grid.seq * grid.batch
    small = small_ref[...].astype(F32).reshape((ranks, 16, LANES))
    per = ranks // pairs
    for p in range(pairs):
        total = small[p * per]
        for j in range(1, per):
            total = total + small[p * per + j]
        table_ref[:, p * LANES : (p + 1) * LANES] = total
    gather.point()

    def shift_rows(segment, gain, bias, slot, body):
        step = 64

        def run(i, carry):
            at = pl.ds(pl.multiple_of(segment * length + i * step, step), step)
            current = normed_ref[at, :] * table_ref[gain : gain + 1, :] + table_ref[bias : bias + 1, :]
            row = lax.broadcasted_iota(jnp.int32, (step, 1), 0)
            previous = jnp.where(row == 0, carry, pltpu.roll(current, 1, 0))
            body(at, current, previous)
            return current[step - 1 : step, :]

        lax.fori_loop(0, length // step, run, prev_ref[slot, segment : segment + 1, :])

    def swap_edges(entry_ref, gain, bias, slot):
        edge_ref[...] = jnp.zeros_like(edge_ref)
        for q in range(segments):
            last = (q + 1) * length
            row = normed_ref[last - 8 : last, :][7:8, :]
            edge_ref[q : q + 1, :] = row * table_ref[gain : gain + 1, :] + table_ref[bias : bias + 1, :]
        copy = pltpu.make_async_remote_copy(
            src_ref=edge_ref,
            dst_ref=arrive_ref.at[slot],
            send_sem=edge_send.at[slot],
            recv_sem=edge_recv.at[slot],
            device_id=(lax.rem(me + 1, grid.seq), index["batch"]),
            device_id_type=MESH,
        )
        copy.start()
        gather.point()
        copy.wait()
        first = jnp.where(me == 0, 1.0, 0.0)
        prev_ref[slot] = arrive_ref[slot] * (1.0 - first)
        prev_ref[slot, 0:segments, :] += entry_ref[...].astype(F32) * first

    swap_edges(att_entry_ref, 0, 1, 0)

    def mix_one(at, current, previous):
        for c in range(4):
            blend = table_ref[2 + c : 3 + c, :]
            mixed_ref[c, at, :] = (current * blend + previous * (1.0 - blend)).astype(BF16)

    for q in range(segments):
        shift_rows(q, 0, 1, 0, mix_one)
        gather.point()
    save(mixed_ref)

    def project_to(array, slot, left, target_ref):
        for number, piece in enumerate(range(starts[array], starts[array + 1])):
            column, size = span(plan[piece])
            here = (slot + number) % 2
            load(piece, wide_ref, here)

            def run(n, carry, column=column, here=here):
                value = dot(left[...], weight(wide_ref, here, tile(n)), 1, 0)
                target_ref[:, pl.ds(pl.multiple_of(column + n * 256, 256), 256)] = value.astype(target_ref.dtype)
                return carry

            lax.fori_loop(0, size // 256, run, 0)
            gather.point()

    project_to(1, 0, mixed_ref.at[1], k_ref)
    project_to(2, 1, mixed_ref.at[2], v_ref)
    save(k_ref, v_ref)
    ones, ones16 = block_ones(F32), block_ones(BF16)
    group = lax.div(me * rows, LANES)
    own_log = table_ref[6:7, pl.ds(pl.multiple_of(group * LANES, LANES), LANES)]
    fade_ref[...] = column_of(jnp.exp(-length * jnp.exp(own_log)), length)

    def columns(p):
        return pl.ds(pl.multiple_of(p * LANES, LANES), LANES)

    def rate_of(p):
        return jnp.exp(table_ref[6:7, columns(p)])

    def own_states(p, carry):
        _, _, end = decays(rate_of(p), length)
        both = []
        for q in range(segments):
            token = pl.ds(q * length, length)
            k_end = k_ref[token, columns(p)].astype(F32) * end
            both.append(dot2(k_end, v_ref[token, columns(p)], 0, 0, "own"))
        own_ref[columns(p), :] = fold(both[0], both[1], ones).astype(BF16)
        return carry

    lax.fori_loop(0, pairs, own_states, 0)
    first = exchange(grid, index, own_ref, got_ref, rows, send_a, recv_a)
    gather.point()
    project_to(3, 0, mixed_ref.at[0], r_ref)
    project_to(4, 1, mixed_ref.at[3], gate_ref)
    save(r_ref, gate_ref)
    for copy in first:
        copy.wait_recv()
    state = start_ref[...]
    fade = fade_ref[pl.ds(pl.multiple_of(lax.rem(me * rows, LANES), rows), rows), :]
    for block in range(grid.seq):
        at = pl.ds(block * rows, rows)
        out_ref[at, :] = state.astype(BF16)
        state = fade * state + got_ref[at, :].astype(F32)
    second = exchange(grid, index, out_ref, begin_ref, rows, send_b, recv_b)
    gather.point()

    later = lax.broadcasted_iota(jnp.int32, (length, length), 0) > lax.broadcasted_iota(
        jnp.int32, (length, length), 1
    )
    for copy in second:
        copy.wait_recv()

    def inside(p, carry):
        down, up, _ = decays(rate_of(p), length)
        pick = half_masks(length)
        begin = begin_ref[columns(p), :].astype(F32)
        for q in range(segments):
            token = pl.ds(q * length, length)
            r = r_ref[token, columns(p)].astype(F32)
            k = k_ref[token, columns(p)].astype(F32)
            v = v_ref[token, columns(p)]
            r_down = r * down
            k_up = k * up
            halves = []
            for h in range(2):
                r_head = jnp.where(pick == (h == 0), r_down, 0.0)
                scores = jnp.where(later, dot3(r_head, k_up, 1, 1, "score"), 0.0)
                halves.append(dot2(scores, v, 1, 0, "inner"))
            inner = jnp.where(pick, halves[0], halves[1])
            self_part = head_sum(r * table_ref[7:8, columns(p)] * k, ones16)
            inner = inner + self_part * v.astype(F32)
            state16 = unfold(begin, q, ones).astype(BF16)
            y = (inner + dot2(r_down, state16, 1, 0, "cross")).astype(BF16)
            wkv_ref[token, columns(p)] = y
            center = y.astype(F32) - dot(y, ones16, 1, 0) * (1.0 / SUBSPACE_EXTENT)
            spread = head_sum(center * center, ones16) * (1.0 / SUBSPACE_EXTENT)
            z = center * lax.rsqrt(spread + 0.00064)
            normalized = z * table_ref[8:9, columns(p)] + table_ref[9:10, columns(p)]
            g = gate_ref[token, columns(p)]
            attended_ref[token, columns(p)] = (normalized * g / (1.0 + jnp.exp(-g))).astype(BF16)
        return carry

    for p in range(pairs):
        lax.fori_loop(p, p + 1, inside, 0)
        gather.point()
    save(wkv_ref, attended_ref)

    load(first_piece(5), wide_ref, 0)

    def out_project(n, carry):
        value = dot(attended_ref[...], weight(wide_ref, 0, tile(n)), 1, 0)
        middle_ref[:, tile(n)] = x_ref[:, tile(n)].astype(F32) + value
        return carry

    lax.fori_loop(0, width // 256, out_project, 0)
    save(middle_ref)
    gather.point()
    norm(middle_ref)
    gather.point()
    swap_edges(ffn_entry_ref, 10, 11, 1)

    def mix_two(at, current, previous):
        for c in range(2):
            blend = table_ref[12 + c : 13 + c, :]
            mixed2_ref[c, at, :] = (current * blend + previous * (1.0 - blend)).astype(BF16)

    for q in range(segments):
        shift_rows(q, 10, 11, 1, mix_two)
        gather.point()
    save(mixed2_ref)
    load(first_piece(6), wide_ref, 1)

    def receive(n, carry):
        value = dot(mixed2_ref[1], weight(wide_ref, 1, tile(n)), 1, 0)
        recv = 1.0 / (1.0 + jnp.exp(-value))
        recv_ref[:, tile(n)] = recv
        d_carried_ref[:, tile(n)] = (recv * up_ref[:, tile(n)].astype(F32)).astype(BF16)
        return carry

    lax.fori_loop(0, width // 256, receive, 0)
    save(d_carried_ref)
    gather.point()

    for piece in range(starts[7], starts[8]):
        slot = (piece - starts[7]) % 2
        column, size = span(plan[piece])
        load(piece, wide_ref, slot)

        def key(n, carry):
            value = jnp.maximum(dot(mixed2_ref[0], weight(wide_ref, slot, tile(n)), 1, 0), 0.0)
            hidden_ref[:, pl.ds(pl.multiple_of(column + n * 256, 256), 256)] = (value * value).astype(BF16)
            return carry

        lax.fori_loop(0, size // 256, key, 0)
        gather.point()
    save(hidden_ref)
    for piece in range(starts[8], len(plan)):
        slot = (piece - starts[8]) % 2
        column, size = span(plan[piece])
        load(piece, tall_ref, slot)
        window = pl.ds(column, size)

        def carry_out(m, carry):
            at = tile(m, 256)
            carried = dot(hidden_ref[at, :], weight(tall_ref, slot, pl.ds(0, size)), 1, 0)
            recv = recv_ref[at, window]
            result_ref[at, window] = (middle_ref[at, window] + recv * carried).astype(BF16)
            upstream = up_ref[at, window].astype(F32)
            d_recv_ref[at, window] = (recv * (1.0 - recv) * carried * upstream).astype(BF16)
            return carry

        lax.fori_loop(0, tokens // 256, carry_out, 0)
        gather.point()

    save(d_recv_ref)
    for copy in first + second:
        copy.wait_send()
    gather.close()
    for copy in saved:
        copy.wait()


def forward(grid, x, upstream, att_entry, ffn_entry, start, shards, length):
    tokens, width = x.shape
    steps = [LANES, CHUNK // 2] + [CHUNK] * 6 + [TALL]
    plan, starts = gather_plan([(s.shape[1], step) for s, step in zip(shards, steps)])
    total = sum(len(unit[1]) for unit in plan)
    hidden = shards[7].shape[1]
    vmem = pl.BlockSpec(memory_space=pltpu.VMEM)
    anywhere = pl.BlockSpec(memory_space=pl.ANY)
    flat = jax.ShapeDtypeStruct((tokens, width), BF16)
    state = pltpu.VMEM((width, LANES), BF16)
    sems = pltpu.SemaphoreType.DMA((grid.seq - 1,))
    count = total * sum(size - 1 for size in grid.shape)
    kept = [
        ((4, tokens, width), BF16), ((tokens, width), BF16), ((tokens, width), BF16), ((tokens, width), BF16),
        ((tokens, width), F32), ((tokens, width), BF16), ((tokens, width), BF16), ((tokens, width), F32),
        ((2, tokens, width), BF16), ((tokens, hidden), BF16), ((tokens, width), BF16), ((tokens, width), BF16),
    ]
    return pl.pallas_call(
        functools.partial(forward_kernel, grid, length, plan, starts),
        out_shape=[jax.ShapeDtypeStruct(grid.shape + s.shape, s.dtype) for s in shards]
        + [
            flat, jax.ShapeDtypeStruct((16, width), F32), jax.ShapeDtypeStruct((width, LANES), BF16),
            jax.ShapeDtypeStruct((2, 8, width), F32),
        ]
        + [jax.ShapeDtypeStruct(*entry) for entry in kept],
        in_specs=[vmem] * 5 + [anywhere] * 9,
        out_specs=[anywhere] * 9 + [vmem] * 4 + [anywhere] * len(kept),
        scratch_shapes=[pltpu.VMEM(*entry) for entry in kept] + [
            pltpu.VMEM((tokens, width), F32),
            pltpu.VMEM((2,) + grid.shape + (shards[1].shape[0], CHUNK), BF16),
            pltpu.VMEM((2,) + grid.shape + (shards[8].shape[0], TALL), BF16),
            pltpu.VMEM(grid.shape + shards[0].shape, BF16),
            pltpu.VMEM((8, width), F32),
            pltpu.VMEM((2, 8, width), F32),
            pltpu.VMEM((tokens, width), F32),
            state, state, state,
            pltpu.VMEM((LANES, LANES), F32),
            pltpu.SemaphoreType.DMA((total,)),
            pltpu.SemaphoreType.DMA((count,)),
            pltpu.SemaphoreType.DMA((count,)),
            pltpu.SemaphoreType.DMA((2,)),
            pltpu.SemaphoreType.DMA((len(kept),)),
            pltpu.SemaphoreType.DMA((2,)),
            pltpu.SemaphoreType.DMA((2,)),
            sems, sems, sems, sems,
        ],
        compiler_params=pltpu.CompilerParams(
            collective_id=0, has_side_effects=True, vmem_limit_bytes=VMEM_LIMIT
        ),
    )(x, upstream, att_entry, ffn_entry, start, *shards)


STAGES = ("c", "first", "second", "z")
GAPS = (1, 2, 2, 2)
SLOTS = (1, 1, 1, 1)
TICKS = (0, 0, 1, 1, 1, 1, 0, 0, 1, 1, 0, 0, 0, 1, 0, 0, 0, 0, 0, 1, 0, 0, 1, 0, 0, 0, 0, 0, 1, 1, 0, 0, 0, 1, 0, 0, 1, 1, 0, 0, 1, 1, 2, 0, 1, 1, 1, 2)


class Piece:
    def __init__(self, array, column, columns, tile, first, kind):
        self.array, self.column, self.columns = array, column, columns
        self.first, self.second = (first, "y" if first == "x" else "x")
        self.tile, self.kind = (tile, columns), kind
        self.group = (tile, columns, first, jnp.dtype(kind).name)


def scatter_plan(arrays):
    units, of_array, counts = [], [], {}
    for array, (tile, columns, step, kind) in enumerate(arrays):
        mine = []
        at = 0
        while at < columns:
            unit = []
            for first in ("x", "y"):
                if at < columns:
                    piece = Piece(array, at, step, tile, first, kind)
                    piece.place = counts.get(piece.group, 0)
                    counts[piece.group] = piece.place + 1
                    unit.append(piece)
                    at += step
            mine.append(len(units))
            units.append(unit)
        of_array.append(mine)
    return units, of_array, counts


def stage_shapes(grid, group):
    tile, columns, first, _ = group
    second = "y" if first == "x" else "x"
    end = (tile, columns)
    return [
        grid.sizes("c") + end,
        (grid.size[first] - 1,) + grid.sizes("c" + first) + end,
        (grid.size[second] - 1,) + grid.sizes("cxy") + end,
        (grid.size["z"] - 1,) + end,
    ]


class Scatter:
    def __init__(self, grid, index, digit, units, keeps, gives, landings, loads, outs, send_sem, recv_sem, load_sem):
        self.grid, self.index, self.digit, self.units = grid, index, digit, units
        self.keeps, self.gives, self.landings, self.loads, self.outs = keeps, gives, landings, loads, outs
        self.send_sem, self.recv_sem, self.load_sem = send_sem, recv_sem, load_sem
        self.started, self.pending, self.giving = [], {}, {}
        self.stage, self.when, self.now, self.reading, self.places = {}, {}, 0, [], 0

    def copy(self, source, target, name, digit):
        slot = len(self.started)
        copy = pltpu.make_async_remote_copy(
            src_ref=source,
            dst_ref=target,
            send_sem=self.send_sem.at[slot],
            recv_sem=self.recv_sem.at[slot],
            device_id=self.grid.peer(self.index, self.digit, name, digit),
            device_id_type=MESH,
        )
        copy.start()
        self.started.append([copy, True])
        return copy

    def open(self, unit, number):
        piece = self.units[unit][number]
        if piece.group in self.giving:
            entry = self.giving.pop(piece.group)
            entry[0].wait_send()
            entry[1] = False
        return self.keeps[unit, number], self.gives[piece.group]

    def give(self, unit):
        for number, piece in enumerate(self.units[unit]):
            target = lax.rem(self.digit["c"] + 1, 2)
            copy = self.copy(self.gives[piece.group], self.landings[piece.group][0].at[piece.place], "c", target)
            self.giving[piece.group] = self.started[-1]
            self.pending[unit, number] = [copy]
        self.stage[unit], self.when[unit] = 0, self.now

    def load(self, unit, number, slot):
        piece, stage = self.units[unit][number], self.stage[unit]
        for copy in self.pending[unit, number]:
            copy.wait_recv()
        copy = pltpu.make_async_copy(
            self.landings[piece.group][stage].at[piece.place],
            self.loads[piece.group][stage].at[slot],
            self.load_sem.at[2 * (sum(SLOTS[:stage]) + slot) + number],
        )
        copy.start()
        return copy

    def add(self, unit, number, slot, copy):
        piece, stage = self.units[unit][number], self.stage[unit]
        keep, got = self.keeps[unit, number], self.loads[piece.group][stage].at[slot]
        names = [n for n in self.grid.order if n != "c"]
        fixed = ((), (piece.first,), (piece.first, piece.second), ("x", "y", "z"))[stage]
        free = [n for n in names if n not in fixed]
        copy.wait()
        terms = 1 if stage == 0 else got.shape[0]
        steps = 1
        for n in free:
            steps *= self.grid.size[n]

        def body(i, carry):
            at, rest = {n: self.digit[n] for n in fixed}, i
            for n in reversed(free):
                at[n] = lax.rem(rest, self.grid.size[n])
                rest = lax.div(rest, self.grid.size[n])
            where, inner = tuple(at[n] for n in names), tuple(at[n] for n in free)
            value = keep[where].astype(F32)
            for j in range(terms):
                value = value + got[inner if stage == 0 else (j,) + inner].astype(F32)
            if stage == 3:
                self.outs[piece.array][:, piece.column : piece.column + piece.columns] = value
            else:
                keep[where] = value.astype(keep.dtype)
            return carry

        if steps == 1:
            body(0, 0)
        else:
            lax.fori_loop(0, steps, body, 0)
        if stage == 3:
            return
        name = (piece.first, piece.second, "z")[stage]
        held = {n: self.digit[n] for n in fixed}
        copies = []
        for j in range(1, self.grid.size[name]):
            target = lax.rem(self.digit[name] + j, self.grid.size[name])
            source = self.grid.at(keep, "c", **held, **{name: target})
            copies.append(self.copy(source, self.landings[piece.group][stage + 1].at[piece.place, j - 1], name, target))
        self.pending[unit, number] = copies

    def finish(self):
        for unit, slot, copies in self.reading:
            for number, copy in enumerate(copies):
                self.add(unit, number, slot, copy)
            self.stage[unit] += 1
            self.when[unit] = self.now
            if self.stage[unit] == 4:
                del self.stage[unit]
        self.reading = []

    def tick(self, stages=(3, 2, 1, 0), gaps=GAPS):
        self.now += 1
        self.finish()
        for stage in stages:
            waiting = [u for u in sorted(self.stage) if self.stage[u] == stage and self.now - self.when[u] >= gaps[stage]]
            for slot, unit in enumerate(waiting[: SLOTS[stage]]):
                copies = [self.load(unit, number, slot) for number in range(len(self.units[unit]))]
                self.reading.append((unit, slot, copies))

    def point(self):
        count = TICKS[self.places]
        self.places += 1
        for _ in range(count):
            self.tick()

    def close(self):
        while self.stage:
            self.tick(gaps=(1, 1, 1, 1))
            self.finish()
        for copy, waiting in self.started:
            if waiting:
                copy.wait_send()


def backward_kernel(grid, length, units, of_array, groups, *refs):
    it = iter(refs)

    def take(count):
        return [next(it) for _ in range(count)]

    (table_ref, prev_ref, begin_ref) = take(3)
    (
        x_hbm, up_hbm, mixed_hbm, r_hbm, k_hbm, v_hbm, gate_hbm, wkv_hbm, attended_hbm, middle_hbm, mixed2_hbm,
        hidden_hbm, d_carried_hbm, d_recv_hbm,
    ) = take(14)
    w_k, w_v, w_r, w_g, w_o, f_r, f_k, f_v = take(8)
    (d_input_ref,) = take(1)
    outs = take(len(of_array))
    landings = {group: take(4) for group in groups}
    keeps = {(u, n): next(it) for u, unit in enumerate(units) for n in range(len(unit))}
    gives = {group: next(it) for group in groups}
    loads = {group: take(4) for group in groups}
    (
        hid, dc, dr, m2, dkey, wide, tall, dn, db, mid, nrm, up, dmid, rr, kk, vv, wk, dgate,
        own_ref, got_ref, out_ref, end_ref, fade_ref, acc, edge_ref, arrive_ref,
        send_sem, recv_sem, load_sem, in_sem, wide_sem, edge_send, edge_recv, send_a, recv_a, send_b, recv_b,
    ) = it
    index, digit = grid.place()
    me = index["seq"]
    tokens, width = dc.shape
    segments = tokens // length
    pairs, rows = width // LANES, width // grid.seq
    n0 = grid.shape[0]
    c_at = grid.order.index("c") - 1
    scatter = Scatter(grid, index, digit, units, keeps, gives, landings, loads, outs, send_sem, recv_sem, load_sem)
    batch_roles = [n for n in grid.order if grid.axis[n] == "batch"]
    peers = [
        grid.peer(index, digit, n, lax.rem(digit[n] + j, grid.size[n])) for n in batch_roles for j in range(1, grid.size[n])
    ]
    peers += [(lax.rem(me + j, grid.seq), index["batch"]) for j in range(1, grid.seq)]

    fetched = {}

    def fetch(name, source, target, slot):
        copy = pltpu.make_async_copy(source, target, in_sem.at[slot])
        copy.start()
        fetched[name] = copy

    def have(*names):
        for name in names:
            fetched.pop(name).wait()

    fetch("hid", hidden_hbm, hid, 0)
    fetch("dc", d_carried_hbm, dc, 1)
    fetch("tall", f_v.at[0], tall, 2)
    fetch("m2", mixed2_hbm, m2, 3)
    fetch("dr", d_recv_hbm, dr, 4)
    fetch("mid", middle_hbm, mid, 5)
    fetch("up", up_hbm, up, 6)
    fetch("att", attended_hbm, dgate, 7)
    fetch("rr", r_hbm, rr, 8)
    fetch("kk", k_hbm, kk, 9)
    fetch("vv", v_hbm, vv, 10)
    fetch("wk", wkv_hbm, wk, 11)
    acc[...] = jnp.zeros_like(acc)
    greet(peers)

    everything = (slice(None),) * 5

    def weight_load(array, column, columns, slot):
        copy = pltpu.make_async_copy(
            array.at[everything + (pl.ds(column, columns),)],
            wide.at[(slot,) + everything + (pl.ds(0, columns),)],
            wide_sem.at[slot],
        )
        copy.start()
        return copy

    def weight(slot, columns):
        return wide[(slot,) + everything + (pl.ds(0, columns),)].reshape((-1, columns))

    def tile(n, step):
        return pl.ds(pl.multiple_of(n * step, step), step)

    def gradient(unit, left_ref, right_ref):
        parts = units[unit]
        targets = [scatter.open(unit, number) for number in range(len(parts))]
        span, narrow = left_ref.shape[1] // n0, parts[0].columns < 256
        for batch in [list(range(len(parts)))] if narrow else [[number] for number in range(len(parts))]:
            first = parts[batch[0]]
            width_all = sum(parts[number].columns for number in batch)

            def run(y, carry, batch=batch, first=first, width_all=width_all):
                total = dot(left_ref[:, tile(y, span)], right_ref[:, first.column : first.column + width_all], 0, 0)
                is_zero = digit["c"] == 0
                for number in batch:
                    keep, give = targets[number]
                    at = parts[number].column - first.column
                    value = total[:, at : at + parts[number].columns].reshape(grid.shape[1:] + parts[number].tile)
                    zero = value[(slice(None),) * c_at + (0,)]
                    one = value[(slice(None),) * c_at + (1,)]
                    keep[y] = jnp.where(is_zero, zero, one).astype(keep.dtype)
                    give[y] = jnp.where(is_zero, one, zero).astype(give.dtype)
                return carry

            lax.fori_loop(0, n0, run, 0)
        scatter.give(unit)

    U = dict(zip(("fv", "fr", "fk", "o", "g", "r", "k", "v", "small"), of_array))

    have("hid", "dc")
    for unit in U["fv"]:
        gradient(unit, hid, dc)
        scatter.point()
    span = hid.shape[1] // n0
    loading = weight_load(f_r, 0, width, 0)
    for y in range(n0):
        have("tall")

        def key(m, carry, y=y):
            at = tile(m, 128)
            window = slice(y * span, (y + 1) * span)
            d_hidden = dot(dc[at, :], tall[...].reshape((span, width)), 1, 1)
            dkey[at, window] = (2.0 * jnp.sqrt(hid[at, window].astype(F32)) * d_hidden).astype(BF16)
            return carry

        lax.fori_loop(0, tokens // 128, key, 0)
        if y + 1 < n0:
            fetch("tall", f_v.at[y + 1], tall, 2)
        if y < 2:
            scatter.point()
    have("m2", "dr")
    gradient(U["fr"][0], m2.at[1], dr)
    fetch("mx0", mixed_hbm.at[0], hid.at[:, pl.ds(0, width)], 0)
    fetch("mx1", mixed_hbm.at[1], hid.at[:, pl.ds(width, width)], 1)
    fetch("mx2", mixed_hbm.at[2], hid.at[:, pl.ds(2 * width, width)], 2)
    scatter.point()
    loading.wait()
    chunks = pieces(hid.shape[1], CHUNK)
    loading = weight_load(f_k, *chunks[0], 1)

    def through_recv(m, carry):
        at = tile(m, 256)
        db[at, :] = dot(dr[at, :], weight(0, width), 1, 1)
        return carry

    lax.fori_loop(0, tokens // 256, through_recv, 0)
    scatter.point()
    for number, unit in enumerate(U["fk"]):
        gradient(unit, m2.at[0], dkey)
        scatter.point()
        column, columns = chunks[number]
        slot = (number + 1) % 2
        loading.wait()
        if number + 1 < len(chunks):
            loading = weight_load(f_k, *chunks[number + 1], 1 - slot)

        def through_key(m, carry, number=number, column=column, columns=columns, slot=slot):
            at = tile(m, 256)
            value = dot(dkey[at, column : column + columns], weight(slot, columns), 1, 1)
            dn[at, :] = value if number == 0 else dn[at, :] + value
            return carry

        lax.fori_loop(0, tokens // 256, through_key, 0)
        scatter.point()
    fetch("mx3", mixed_hbm.at[3], m2.at[0], 3)
    loading = weight_load(w_o, 0, width, 0)

    step = 64

    def fold_rows(value):
        return jnp.sum(value.reshape((step // 8, 8, width)), axis=0)

    def norm(source_ref, gain, bias):
        def run(i, carry):
            at = tile(i, step)
            value = source_ref[at, :].astype(F32)
            center = value - jnp.mean(value, axis=-1, keepdims=True)
            spread = jnp.mean(center * center, axis=-1, keepdims=True)
            nrm[at, :] = center * lax.rsqrt(spread + 1e-05) * table_ref[gain : gain + 1, :] + table_ref[bias : bias + 1, :]
            return carry

        lax.fori_loop(0, tokens // step, run, 0)

    def swap_edges(slot):
        edge_ref[...] = jnp.zeros_like(edge_ref)
        for q in range(segments):
            edge_ref[q : q + 1, :] = db[q * length : q * length + 8, :][0:1, :]
        copy = pltpu.make_async_remote_copy(
            src_ref=edge_ref,
            dst_ref=arrive_ref.at[slot],
            send_sem=edge_send.at[slot],
            recv_sem=edge_recv.at[slot],
            device_id=(lax.rem(me + grid.seq - 1, grid.seq), index["batch"]),
            device_id_type=MESH,
        )
        copy.start()
        return copy

    def norm_back(source_ref, gain, bias, slot, base_ref, put):
        keep_next = jnp.where(me == grid.seq - 1, 0.0, 1.0)
        for q in range(segments):
            count = length // step

            def run(i, carry, q=q):
                at = tile(q * count + count - 1 - i, step)
                value = source_ref[at, :].astype(F32)
                center = value - jnp.mean(value, axis=-1, keepdims=True)
                spread = jnp.mean(center * center, axis=-1, keepdims=True)
                scale = lax.rsqrt(spread + 1e-05)
                z = center * scale
                before = db[at, :]
                row = lax.broadcasted_iota(jnp.int32, (step, 1), 0)
                d_normed = dn[at, :] + jnp.where(row == step - 1, carry, pltpu.roll(before, step - 1, 0))
                acc[gain] += fold_rows(z * d_normed)
                acc[bias] += fold_rows(d_normed)
                e = d_normed * table_ref[gain : gain + 1, :]
                back = (e - jnp.mean(e, axis=-1, keepdims=True) - z * jnp.mean(e * z, axis=-1, keepdims=True)) * scale
                put(at, base_ref[at, :].astype(F32) + back)
                return before[0:1, :]

            lax.fori_loop(0, count, run, arrive_ref[slot, q : q + 1, :] * keep_next)
            scatter.point()

    have("mid")
    norm(mid, 10, 11)
    scatter.point()
    for q in range(segments):

        def blend_two(i, carry, q=q):
            at = tile(q * (length // step) + i, step)
            current = nrm[at, :]
            row = lax.broadcasted_iota(jnp.int32, (step, 1), 0)
            difference = current - jnp.where(row == 0, carry, pltpu.roll(current, 1, 0))
            first, second = dn[at, :], db[at, :]
            acc[12] += fold_rows(difference * first)
            acc[13] += fold_rows(difference * second)
            a, b = table_ref[12:13, :], table_ref[13:14, :]
            dn[at, :] = first * a + second * b
            db[at, :] = first * (1.0 - a) + second * (1.0 - b)
            return current[step - 1 : step, :]

        lax.fori_loop(0, length // step, blend_two, prev_ref[1, q : q + 1, :])
        scatter.point()
    moving = swap_edges(0)
    scatter.point()
    have("up")
    moving.wait()

    def put_middle(at, value):
        dmid[at, :] = value
        dr[at, :] = value.astype(BF16)

    norm_back(mid, 10, 11, 0, up, put_middle)
    fetch("mid", gate_hbm, mid, 5)
    fetch("up", x_hbm, up, 6)
    have("att")
    gradient(U["o"][0], dgate, dr)
    scatter.point()
    loading.wait()

    def through_out(m, carry):
        at = tile(m, 256)
        nrm[at, :] = dot(dr[at, :], weight(0, width), 1, 1)
        return carry

    lax.fori_loop(0, tokens // 256, through_out, 0)
    scatter.point()

    ones, ones16 = block_ones(F32), block_ones(BF16)
    share = 1.0 / SUBSPACE_EXTENT

    def columns(p, base=0):
        return pl.ds(pl.multiple_of(base + p * LANES, LANES), LANES)

    def rate_of(p):
        return jnp.exp(table_ref[6:7, columns(p)])

    group = lax.div(me * rows, LANES)
    own_log = table_ref[6:7, pl.ds(pl.multiple_of(group * LANES, LANES), LANES)]
    fade_ref[...] = column_of(jnp.exp(-length * jnp.exp(own_log)), length)
    have("wk", "mid", "rr")

    def own_states(p, carry):
        down, _, _ = decays(rate_of(p), length)
        both = []
        gain_sum, bias_sum = jnp.zeros((1, LANES), F32), jnp.zeros((1, LANES), F32)
        for q in range(segments):
            token = pl.ds(q * length, length)
            y = wk[token, columns(p)]
            center = y.astype(F32) - dot(y, ones16, 1, 0) * share
            spread = head_sum(center * center, ones16) * share
            scale = lax.rsqrt(spread + 0.00064)
            z = center * scale
            gain = table_ref[8:9, columns(p)]
            normalized = z * gain + table_ref[9:10, columns(p)]
            g = mid[token, columns(p)]
            s = 1.0 / (1.0 + jnp.exp(-g))
            d_att = nrm[token, columns(p)]
            dgate[token, columns(p)] = (d_att * normalized * s * (1.0 + g * (1.0 - s))).astype(BF16)
            d_norm = d_att * g * s
            gain_sum = gain_sum + jnp.sum(d_norm * z, axis=0, keepdims=True)
            bias_sum = bias_sum + jnp.sum(d_norm, axis=0, keepdims=True)
            e = d_norm * gain
            dy = ((e - head_sum(e, ones16) * share - z * (head_sum(e * z, ones16) * share)) * scale).astype(BF16)
            dc[token, columns(p)] = dy
            both.append(dot2(rr[token, columns(p)].astype(F32) * down, dy, 0, 0, "own"))
        acc[8, 0:1, columns(p)] = gain_sum
        acc[9, 0:1, columns(p)] = bias_sum
        own_ref[columns(p), :] = fold(both[0], both[1], ones).astype(BF16)
        return carry

    for quarter in range(4):
        lax.fori_loop(quarter * pairs // 4, (quarter + 1) * pairs // 4, own_states, 0)
        scatter.point()
    first = exchange(grid, index, own_ref, got_ref, rows, send_a, recv_a)
    have("mx3")
    gradient(U["g"][0], m2.at[0], dgate)
    scatter.point()
    for copy in first:
        copy.wait_recv()
    fade = fade_ref[pl.ds(pl.multiple_of(lax.rem(me * rows, LANES), rows), rows), :]
    state = jnp.zeros_like(fade)
    for block in reversed(range(grid.seq)):
        at = pl.ds(block * rows, rows)
        out_ref[at, :] = state.astype(BF16)
        state = fade * state + got_ref[at, :].astype(F32)
    second = exchange(grid, index, out_ref, end_ref, rows, send_b, recv_b)
    scatter.point()
    have("up")
    norm(up, 0, 1)
    scatter.point()
    have("kk", "vv")
    for copy in second:
        copy.wait_recv()
    later = lax.broadcasted_iota(jnp.int32, (length, length), 0) > lax.broadcasted_iota(
        jnp.int32, (length, length), 1
    )
    time = lax.broadcasted_iota(jnp.int32, (length, LANES), 0).astype(F32)

    def inside(p, carry):
        rate = rate_of(p)
        reward = table_ref[7:8, columns(p)]
        down, up_, end = decays(rate, length)
        pick = half_masks(length)
        begins, ends = begin_ref[columns(p), :].astype(F32), end_ref[columns(p), :].astype(F32)
        reward_sum, rate_sum = jnp.zeros((1, LANES), F32), jnp.zeros((1, LANES), F32)
        for q in range(segments):
            token = pl.ds(q * length, length)
            r = rr[token, columns(p)].astype(F32)
            k = kk[token, columns(p)].astype(F32)
            v = vv[token, columns(p)]
            dy = dc[token, columns(p)]
            begin, finish = unfold(begins, q, ones), unfold(ends, q, ones)
            begin16, finish16 = begin.astype(BF16), finish.astype(BF16)
            r_down = (r * down).astype(BF16)
            k_up = (k * up_).astype(BF16)
            k_end = k * end
            zero = jnp.zeros_like(r_down)
            d_r, d_k, d_v = [], [], []
            for h in range(2):
                here = pick == (h == 0)
                scores = jnp.where(later, dot(jnp.where(here, r_down, zero), k_up, 1, 1), 0.0)
                d_scores = jnp.where(later, dot(jnp.where(here, dy, zero), v, 1, 1), 0.0).astype(BF16)
                d_r.append(dot(d_scores, k_up, 1, 0))
                d_k.append(dot(d_scores, r_down, 0, 0))
                d_v.append(dot2(scores, dy, 0, 0, "inner"))
            from_r = jnp.where(pick, d_r[0], d_r[1]) + dot(dy, begin16, 1, 1)
            from_k = jnp.where(pick, d_k[0], d_k[1])
            from_end = dot(v, finish16, 1, 1)
            v32, dy32 = v.astype(F32), dy.astype(F32)
            v_dy = head_sum(v32 * dy32, ones16)
            self_part = head_sum(r * reward * k, ones16)
            dkey[token, columns(p)] = (from_r * down + reward * k * v_dy).astype(BF16)
            dkey[token, columns(p, width)] = (from_k * up_ + from_end * end + reward * r * v_dy).astype(BF16)
            dkey[token, columns(p, 2 * width)] = (
                jnp.where(pick, d_v[0], d_v[1]) + dot2(k_end, finish16, 1, 0, "cross") + self_part * dy32
            ).astype(BF16)
            reward_sum = reward_sum + jnp.sum(r * k * v_dy, axis=0, keepdims=True)
            terms = (
                (time + 1.0) * k_up.astype(F32) * from_k
                - time * r_down.astype(F32) * from_r
                - (length - 1.0 - time) * k_end * from_end
            )
            through = lax.dot_general(
                jnp.ones((8, LANES), F32), begin * finish, (((1,), (1,)), ((), ())),
                precision=lax.Precision.HIGHEST, preferred_element_type=F32,
            )[0:1, :]
            rate_sum = rate_sum + jnp.sum(terms, axis=0, keepdims=True) - length * jnp.exp(-rate * length) * through
        acc[7, 0:1, columns(p)] = reward_sum
        acc[6, 0:1, columns(p)] = rate_sum * rate
        return carry

    for p in range(pairs):
        lax.fori_loop(p, p + 1, inside, 0)
        scatter.point()
    have("mx0", "mx1", "mx2")
    weights = (w_r, w_k, w_v, w_g)
    grads = [dkey.at[:, pl.ds(c * width, width)] for c in range(3)] + [dgate]

    def load_rows(y):
        copies = []
        for c in range(4):
            copy = pltpu.make_async_copy(weights[c].at[y], wide.at[c // n0, c % n0], in_sem.at[8 + c])
            copy.start()
            copies.append(copy)
        return copies

    loading = load_rows(0)
    for c, name in enumerate("rkv"):
        gradient(U[name][0], hid.at[:, pl.ds(c * width, width)], grads[c])
        scatter.point()
    span = width // n0
    for y in range(n0):
        for copy in loading:
            copy.wait()
        window = slice(y * span, (y + 1) * span)

        def through_mix(m, carry, y=y, window=window):
            at = tile(m, 128)
            current = nrm[at, window]
            above = nrm[pl.ds(pl.multiple_of(jnp.maximum(m * 128 - 8, 0), 8), 8), window][7:8, :]
            segment = lax.div(m, length // 128)
            given = prev_ref[0, 0:1, window]
            for q in range(1, segments):
                given = jnp.where(segment == q, prev_ref[0, q : q + 1, window], given)
            carried = jnp.where(lax.rem(m, length // 128) == 0, given, above)
            row = lax.broadcasted_iota(jnp.int32, (128, 1), 0)
            difference = current - jnp.where(row == 0, carried, pltpu.roll(current, 1, 0))
            here, before = None, None
            for c in range(4):
                value = dot(grads[c][at, :], wide[c // n0, c % n0].reshape((span, width)), 1, 1)
                acc[2 + c, :, window] += jnp.sum((difference * value).reshape((16, 8, span)), axis=0)
                blend = table_ref[2 + c : 3 + c, window]
                here = blend * value if c == 0 else here + blend * value
                before = (1.0 - blend) * value if c == 0 else before + (1.0 - blend) * value
            dn[at, window] = here
            db[at, window] = before
            return carry

        lax.fori_loop(0, tokens // 128, through_mix, 0)
        if y + 1 < n0:
            loading = load_rows(y + 1)
        if y < 2:
            scatter.point()
    moving = swap_edges(1)
    scatter.point()
    moving.wait()

    def put_input(at, value):
        dr[at, :] = value.astype(BF16)

    norm_back(up, 0, 1, 1, dmid, put_input)
    fetch("result", dr, d_input_ref, 4)

    sums = [jnp.sum(acc[i], axis=0, keepdims=True) for i in range(14)]
    for i in range(14):
        edge_ref[0:1, :] = sums[i]
        nrm[i : i + 1, :] = edge_ref[0:1, :]
    nrm[14:16, :] = jnp.zeros((2, width), F32)
    keep, give = scatter.open(U["small"][0], 0)
    per = grid.seq * grid.batch // pairs
    names = [n for n in grid.order if n != "c"]

    def spread(i, carry):
        at, rest = {}, i
        for n in reversed(names):
            at[n] = lax.rem(rest, grid.size[n])
            rest = lax.div(rest, grid.size[n])
        for target, core in ((keep, digit["c"]), (give, 1 - digit["c"])):
            spot = dict(at, c=core)
            rank = 0
            for n in grid.order:
                rank = rank * grid.size[n] + spot[n]
            target[tuple(at[n] for n in names)] = nrm[0:16, columns(lax.div(rank, per))]
        return carry

    steps = 1
    for n in names:
        steps *= grid.size[n]
    lax.fori_loop(0, steps, spread, 0)
    scatter.give(U["small"][0])
    scatter.point()
    for copy in first + second:
        copy.wait_send()
    scatter.close()
    have("result")


def backward(grid, length, table, prev, begin, stored, weights):
    tokens, width = stored[0].shape
    hidden = stored[11].shape[1]
    blk, tall = weights[0].shape[4], weights[7].shape[4]
    arrays = [
        (tall, width, LANES, BF16), (blk, width, 512, BF16), (blk, hidden, 512, BF16), (blk, width, 512, BF16),
        (blk, width, 512, BF16), (blk, width, 512, BF16), (blk, width, 512, BF16), (blk, width, 512, BF16),
        (16, LANES, LANES, F32),
    ]
    units, of_array, counts = scatter_plan(arrays)
    groups = list(counts)
    kinds = {group: jnp.dtype(group[3]) for group in groups}
    shapes = {group: stage_shapes(grid, group) for group in groups}
    vmem = pl.BlockSpec(memory_space=pltpu.VMEM)
    anywhere = pl.BlockSpec(memory_space=pl.ANY)
    flat16, flat32 = pltpu.VMEM((tokens, width), BF16), pltpu.VMEM((tokens, width), F32)
    state = pltpu.VMEM((width, LANES), BF16)
    sems = pltpu.SemaphoreType.DMA((grid.seq - 1,))
    dma = pltpu.SemaphoreType.DMA
    count = sum(len(unit) for unit in units) * sum(size - 1 for size in grid.shape)
    landing = [
        jax.ShapeDtypeStruct((counts[group],) + shape, kinds[group]) for group in groups for shape in shapes[group]
    ]
    outs = pl.pallas_call(
        functools.partial(backward_kernel, grid, length, units, of_array, groups),
        out_shape=[jax.ShapeDtypeStruct((tokens, width), BF16)]
        + [jax.ShapeDtypeStruct((a[0], a[1]), F32) for a in arrays]
        + landing,
        in_specs=[vmem] * 3 + [anywhere] * 22,
        out_specs=[anywhere] + [vmem] * len(arrays) + [anywhere] * len(landing),
        scratch_shapes=[pltpu.VMEM(grid.sizes("c") + p.tile, p.kind) for unit in units for p in unit]
        + [pltpu.VMEM(shapes[group][0], kinds[group]) for group in groups]
        + [pltpu.VMEM((slots,) + shape, kinds[group]) for group in groups for slots, shape in zip(SLOTS, shapes[group])]
        + [
            pltpu.VMEM((tokens, hidden), BF16), flat16, flat16, pltpu.VMEM((2, tokens, width), BF16),
            pltpu.VMEM((tokens, hidden), BF16),
            pltpu.VMEM((2,) + grid.shape + (blk, CHUNK), BF16),
            pltpu.VMEM(grid.shape[1:] + (tall, width), BF16),
            flat32, flat32, flat32, flat32, flat16, flat32, flat16, flat16, flat16, flat16, flat16,
            state, state, state, state,
            pltpu.VMEM((LANES, LANES), F32),
            pltpu.VMEM((14, 8, width), F32),
            pltpu.VMEM((8, width), F32),
            pltpu.VMEM((2, 8, width), F32),
            dma((count,)), dma((count,)), dma((2 * sum(SLOTS),)), dma((12,)), dma((2,)), dma((2,)), dma((2,)),
            sems, sems, sems, sems,
        ],
        compiler_params=pltpu.CompilerParams(
            collective_id=1, has_side_effects=True, vmem_limit_bytes=VMEM_LIMIT
        ),
    )(table, prev, begin, *stored, *weights)
    return outs[0], outs[1 : 1 + len(arrays)]


def local(grid, *args):
    (
        incoming, att_entry, ffn_entry, memory, upstream,
        ln1_gain, ln1_bias, att_mix, w_recept, w_key, w_value, w_gate, decay_log, reward,
        gn_gain, gn_bias, w_out, ln2_gain, ln2_bias, ffn_mix, f_key, f_value, f_recept,
    ) = args
    segments, length, width = incoming.shape
    tokens = segments * length
    ranks = grid.seq * grid.batch
    share = width // ranks

    per = LANES // share
    rank = lax.axis_index(("seq", "batch"))
    small = jnp.stack(
        [ln1_gain, ln1_bias] + [att_mix[:, c] for c in range(4)] + [decay_log, reward, gn_gain, gn_bias, ln2_gain, ln2_bias]
        + [ffn_mix[:, c] for c in range(2)]
    )
    small = jnp.tile(jnp.pad(small, ((0, 2), (0, 0))), (1, per))
    lane = lax.broadcasted_iota(jnp.int32, small.shape, 1)
    small = jnp.where(lane // share == rank % per, small, jnp.zeros_like(small))
    rows = width // grid.seq
    row = lax.axis_index("seq") * rows
    start = memory.transpose(1, 2, 0, 3).reshape(width, segments * SUBSPACE_EXTENT)
    start = lax.dynamic_slice_in_dim(start, row, rows, 0)
    shards = [small, w_key, w_value, w_recept, w_gate, w_out, f_recept, f_key, f_value]
    outs = forward(
        grid, incoming.reshape(tokens, width), upstream.reshape(tokens, width), att_entry, ffn_entry, start, shards, length
    )
    (
        result, table, begin, prev, mixed, r, k, v, gate_pre, wkv, attended, middle, mixed2, hidden, d_carried, d_recv,
    ) = outs[9:]
    stored = [
        incoming.reshape(tokens, width), upstream.reshape(tokens, width), mixed, r, k, v, gate_pre, wkv, attended, middle,
        mixed2, hidden, d_carried, d_recv,
    ]
    d_input, (s_fv, s_fr, s_fk, s_o, s_g, s_r, s_k, s_v, s_small) = backward(
        grid, length, table, prev, begin, stored, outs[1:9]
    )
    s = lax.dynamic_slice_in_dim(s_small, (rank % per) * share, share, 1)
    shape = incoming.shape
    return (
        result.reshape(shape), d_input.reshape(shape),
        s[0], s[1], s[2:6].T, s_r, s_k, s_v, s_g, s[6], s[7], s[8], s[9], s_o, s[10], s[11], s[12:14].T,
        s_fk, s_fv, s_fr,
    )


def solution(mesh):
    grid = Grid(mesh.shape["seq"], mesh.shape["batch"])
    both, rows = P(("seq", "batch")), P(("seq", "batch"), None)
    tokens, entry = P("batch", "seq", None), P("batch", None)
    return jax.shard_map(
        functools.partial(local, grid),
        mesh=mesh,
        in_specs=(
            tokens, entry, entry, P("batch", None, None, None), tokens,
            both, both, rows, rows, rows, rows, rows, both, both, both, both, rows, both, both, rows, rows, rows, rows,
        ),
        out_specs=(
            tokens, tokens, both, both, rows, rows, rows, rows, rows, both, both, both, both, rows, both, both, rows,
            rows, rows, rows,
        ),
        check_vma=False,
    )
```

```python
import functools

import jax
import jax.numpy as jnp
from jax import lax
from jax.experimental import pallas as pl
from jax.experimental.pallas import tpu as pltpu
from jax.sharding import PartitionSpec as P

WKV_PARTITIONS = 16
SUBSPACE_EXTENT = 64
LANES = 128
MESH = pl.DeviceIdType.MESH
F32 = jnp.float32
BF16 = jnp.bfloat16
VMEM_LIMIT = 63 * 1024 * 1024


class Grid:
    def __init__(self, seq, batch):
        self.seq, self.batch = seq, batch
        if seq == 8 and batch == 4:
            digits = [("y", "seq", 4, 2), ("x", "seq", 2, 2), ("c", "seq", 1, 2), ("z", "batch", 1, 4)]
        elif seq == 16 and batch == 8:
            digits = [("y", "seq", 4, 4), ("x", "seq", 1, 4), ("z", "batch", 2, 4), ("c", "batch", 1, 2)]
        else:
            raise ValueError("unknown mesh")
        self.order = [name for name, *_ in digits]
        self.axis = {name: axis for name, axis, *_ in digits}
        self.stride = {name: stride for name, _, stride, _ in digits}
        self.size = {name: size for name, *_, size in digits}
        self.shape = tuple(self.size[name] for name in self.order)

    def place(self):
        index = {"seq": lax.axis_index("seq"), "batch": lax.axis_index("batch")}
        return index, {
            name: (index[self.axis[name]] // self.stride[name]) % self.size[name] for name in self.order
        }

    def peer(self, index, digit, name, target):
        where = dict(index)
        axis = self.axis[name]
        where[axis] = index[axis] + (target - digit[name]) * self.stride[name]
        return (where["seq"], where["batch"])

    def at(self, ref, gone="", **fixed):
        return ref.at[tuple(fixed.get(name, slice(None)) for name in self.order if name not in gone)]

    def sizes(self, gone=""):
        return tuple(self.size[name] for name in self.order if name not in gone)


def greet(peers):
    barrier = pltpu.get_barrier_semaphore()
    for peer in peers:
        pl.semaphore_signal(barrier, inc=1, device_id=peer, device_id_type=MESH)
    pl.semaphore_wait(barrier, len(peers))


def dot(a, b, da, db):
    return lax.dot_general(a, b, (((da,), (db,)), ((), ())), preferred_element_type=F32)


PRECISE = dict(score=0, inner=1, cross=1, own=1, back=0)


def parts_of(value):
    high = value.astype(BF16)
    return high, (value - high.astype(F32)).astype(BF16)


def dot2(a, b, da, db, name):
    if not PRECISE[name]:
        return dot(a.astype(BF16), b, da, db)
    high, low = parts_of(a)
    return dot(high, b, da, db) + dot(low, b, da, db)


def dot3(a, b, da, db, name):
    if not PRECISE[name]:
        return dot(a.astype(BF16), b.astype(BF16), da, db)
    a_high, a_low = parts_of(a)
    b_high, b_low = parts_of(b)
    return dot(a_high, b_high, da, db) + (dot(a_low, b_high, da, db) + dot(a_high, b_low, da, db))


def half_masks(rows):
    lane = lax.broadcasted_iota(jnp.int32, (rows, LANES), 1)
    return lane < SUBSPACE_EXTENT


def block_ones(kind):
    row = lax.broadcasted_iota(jnp.int32, (LANES, LANES), 0) // SUBSPACE_EXTENT
    lane = lax.broadcasted_iota(jnp.int32, (LANES, LANES), 1) // SUBSPACE_EXTENT
    return (row == lane).astype(kind)


def head_sum(value, ones):
    high = value.astype(BF16)
    low = (value - high.astype(F32)).astype(BF16)
    return dot(high, ones, 1, 0) + dot(low, ones, 1, 0)


def decays(rate, length):
    step = lax.broadcasted_iota(jnp.int32, (length, LANES), 0).astype(F32)
    return jnp.exp(-rate * step), jnp.exp(rate * (step + 1.0)), jnp.exp(-rate * (length - 1.0 - step))


def fold(first, second, ones):
    pick = half_masks(LANES)
    a, b = first * ones, second * ones
    a = a + pltpu.roll(a, SUBSPACE_EXTENT, 1)
    b = b + pltpu.roll(b, SUBSPACE_EXTENT, 1)
    return jnp.where(pick, a, b)


def unfold(both, segment, ones):
    pick = half_masks(LANES)
    turned = pltpu.roll(both, SUBSPACE_EXTENT, 1)
    full = jnp.where(pick, both, turned) if segment == 0 else jnp.where(pick, turned, both)
    return full * ones


def exchange(grid, index, source, slots, rows, send_sem, recv_sem):
    me, copies = index["seq"], []
    for j in range(1, grid.seq):
        target = lax.rem(me + j, grid.seq)
        copy = pltpu.make_async_remote_copy(
            src_ref=source.at[pl.ds(pl.multiple_of(target * rows, 16), rows)],
            dst_ref=slots.at[pl.ds(pl.multiple_of(me * rows, 16), rows)],
            send_sem=send_sem.at[j - 1],
            recv_sem=recv_sem.at[j - 1],
            device_id=(target, index["batch"]),
            device_id_type=MESH,
        )
        copy.start()
        copies.append(copy)
    here = pl.ds(pl.multiple_of(me * rows, 16), rows)
    slots[here, :] = source[here, :]
    return copies


CHUNK = 1024
TALL = 256
LAGS = (0, 1, 3)
AHEAD = 4
PUMPS = (
    0, 0, 1, 0, 0, 0, 2, 0, 0, 0, 0, 0, 1, 0, 0, 0, 0, 1, 0, 1, 0, 0, 1, 0, 0, 0, 0, 1, 1, 0, 0, 0, 1, 0, 1, 1, 0, 0, 0, 0,
    1, 0, 0, 0, 1, 0, 0, 0, 0, 0,
)


def pieces(columns, step):
    return [(at, min(step, columns - at)) for at in range(0, columns, step)]


class Gather:
    def __init__(self, grid, index, digit, shards, fulls, plan, own_sem, send_sem, recv_sem):
        self.grid, self.index, self.digit = grid, index, digit
        self.shards, self.fulls, self.plan = shards, fulls, plan
        self.own_sem, self.send_sem, self.recv_sem = own_sem, send_sem, recv_sem
        self.started, self.pending, self.own = [], {}, {}
        self.tick, self.done, self.places = 0, 0, 0

    def others(self, name):
        size = self.grid.size[name]
        return [lax.rem(self.digit[name] + j, size) for j in range(1, size)]

    def send(self, source, place, name):
        copies = []
        for target in self.others(name):
            slot = len(self.started)
            copy = pltpu.make_async_remote_copy(
                src_ref=source,
                dst_ref=place,
                send_sem=self.send_sem.at[slot],
                recv_sem=self.recv_sem.at[slot],
                device_id=self.grid.peer(self.index, self.digit, name, target),
                device_id_type=MESH,
            )
            copy.start()
            self.started.append(copy)
            copies.append(copy)
        return copies

    def stage(self, unit, number):
        if not 0 <= unit < len(self.plan):
            return
        for piece in range(len(self.plan[unit][1])):
            self.step(unit, piece, number)

    def step(self, unit, piece, number):
        array, parts = self.plan[unit]
        column, columns, first, second = parts[piece]
        digit = self.digit
        window = pl.ds(column, columns)
        full = self.fulls[array]
        key = (unit, piece)

        def at(**fixed):
            place = tuple(fixed.get(name, slice(None)) for name in self.grid.order)
            return full.at[place + (slice(None), window)]

        if number == 0:
            place = at(**digit)
            source = self.shards[array].at[:, window]
            copy = pltpu.make_async_copy(source, place, self.own_sem.at[len(self.own)])
            copy.start()
            self.own[key] = copy
            self.pending[key] = self.send(source, place, "z")
            return
        for copy in self.pending[key]:
            copy.wait_recv()
        if number == 1:
            self.own[key].wait()
            fixed, name = {n: digit[n] for n in ("x", "y", "c")}, first
        elif number == 2:
            fixed, name = {n: digit[n] for n in (second, "c")}, second
        elif number == 3:
            fixed, name = {"c": digit["c"]}, "c"
        else:
            self.pending[key] = []
            return
        place = at(**fixed)
        self.pending[key] = self.send(place, place, name)

    def open(self, ahead):
        self.ahead = ahead
        for piece in range(ahead):
            self.stage(piece, 0)

    def pump(self, count=1):
        for _ in range(count):
            tick = self.tick
            self.tick += 1
            for number in (1, 2, 3):
                self.stage(tick - LAGS[number - 1], number)
            self.stage(tick + self.ahead, 0)

    def point(self):
        count = PUMPS[self.places]
        self.places += 1
        self.pump(count if self.tick < len(self.plan) + LAGS[2] + 1 else 0)

    def ready(self, piece):
        while self.tick < piece + LAGS[2] + 1:
            self.pump()
        while self.done <= piece:
            self.stage(self.done, 4)
            self.done += 1

    def close(self):
        for copy in self.started:
            copy.wait_send()


def gather_plan(arrays):
    plan, starts = [], []
    for array, (columns, step) in enumerate(arrays):
        starts.append(len(plan))
        for column, size in pieces(columns, step):
            half = size // 2
            if half % LANES:
                plan.append((array, [(column, size, "x", "y")]))
            else:
                plan.append((array, [(column, half, "x", "y"), (column + half, half, "y", "x")]))
    return plan, starts


def span(unit):
    return unit[1][0][0], sum(part[1] for part in unit[1])


def column_of(row, length):
    at = lax.broadcasted_iota(jnp.int32, (LANES, LANES), 0)
    lane = lax.broadcasted_iota(jnp.int32, (LANES, LANES), 1)
    spread = jnp.where(at == lane, jnp.broadcast_to(row, (LANES, LANES)), 0.0)
    return jnp.broadcast_to(jnp.sum(spread, axis=1, keepdims=True), (LANES, LANES))


def forward_kernel(grid, length, plan, starts, *refs):
    (
        x_ref, up_ref, att_entry_ref, ffn_entry_ref, start_ref, *shards
    ) = refs[:14]
    stored = refs[14:23]
    result_ref, table_ref, begin_ref, prev_ref = refs[23:27]
    kept = refs[27:39]
    (
        mixed_ref, r_ref, k_ref, v_ref, gate_ref, wkv_ref, attended_ref, middle_ref, mixed2_ref, hidden_ref,
        d_carried_ref, d_recv_ref,
    ) = places = refs[39:51]
    (
        normed_ref, edge_ref, arrive_ref, recv_ref,
        own_ref, got_ref, out_ref, fade_ref,
        own_sem, send_sem, recv_sem, store_sem, save_sem, edge_send, edge_recv, send_a, recv_a, send_b, recv_b,
    ) = refs[60:]
    fulls = refs[51:60]
    saved = []

    def save(*names):
        for name in names:
            at = [place is name for place in places].index(True)
            copy = pltpu.make_async_copy(name, kept[at], save_sem.at[at])
            copy.start()
            saved.append(copy)

    index, digit = grid.place()
    me = index["seq"]
    tokens, width = x_ref.shape
    segments = tokens // length
    pairs, rows = width // LANES, width // grid.seq
    batch_roles = [n for n in grid.order if grid.axis[n] == "batch"]
    gather = Gather(grid, index, digit, shards, fulls, plan, own_sem, send_sem, recv_sem)
    peers = [grid.peer(index, digit, n, t) for n in batch_roles for t in gather.others(n)]
    peers += [(lax.rem(me + j, grid.seq), index["batch"]) for j in range(1, grid.seq)]
    greet(peers)
    gather.open(AHEAD)
    gather.point()

    def first_piece(array):
        return starts[array]

    def await_unit(unit):
        gather.ready(unit)
        array = plan[unit][0]
        column, columns = span(plan[unit])
        window = (slice(None),) * 5 + (pl.ds(column, columns),)
        copy = pltpu.make_async_copy(fulls[array].at[window], stored[array].at[window], store_sem.at[unit])
        copy.start()
        saved.append(copy)
        gather.point()

    def weight(array, window):
        value = fulls[array][(slice(None),) * 5 + (window,)]
        return value.reshape((-1, value.shape[-1]))

    def tile(n, step=256):
        return pl.ds(pl.multiple_of(n * step, step), step)

    def norm(source_ref):
        step = 64

        def run(i, carry):
            at = pl.ds(pl.multiple_of(i * step, step), step)
            value = source_ref[at, :].astype(F32)
            center = value - jnp.mean(value, axis=-1, keepdims=True)
            spread = jnp.mean(center * center, axis=-1, keepdims=True)
            normed_ref[at, :] = center * lax.rsqrt(spread + 1e-05)
            return carry

        lax.fori_loop(0, tokens // step, run, 0)

    norm(x_ref)
    gather.point()

    gather.ready(0)
    ranks = grid.seq * grid.batch
    small = fulls[0][...].astype(F32).reshape((ranks, 16, LANES))
    per = ranks // pairs
    for p in range(pairs):
        total = small[p * per]
        for j in range(1, per):
            total = total + small[p * per + j]
        table_ref[:, p * LANES : (p + 1) * LANES] = total
    gather.point()

    def shift_rows(segment, gain, bias, slot, body):
        step = 64

        def run(i, carry):
            at = pl.ds(pl.multiple_of(segment * length + i * step, step), step)
            current = normed_ref[at, :] * table_ref[gain : gain + 1, :] + table_ref[bias : bias + 1, :]
            row = lax.broadcasted_iota(jnp.int32, (step, 1), 0)
            previous = jnp.where(row == 0, carry, pltpu.roll(current, 1, 0))
            body(at, current, previous)
            return current[step - 1 : step, :]

        lax.fori_loop(0, length // step, run, prev_ref[slot, segment : segment + 1, :])

    def swap_edges(entry_ref, gain, bias, slot):
        edge_ref[...] = jnp.zeros_like(edge_ref)
        for q in range(segments):
            last = (q + 1) * length
            row = normed_ref[last - 8 : last, :][7:8, :]
            edge_ref[q : q + 1, :] = row * table_ref[gain : gain + 1, :] + table_ref[bias : bias + 1, :]
        copy = pltpu.make_async_remote_copy(
            src_ref=edge_ref,
            dst_ref=arrive_ref.at[slot],
            send_sem=edge_send.at[slot],
            recv_sem=edge_recv.at[slot],
            device_id=(lax.rem(me + 1, grid.seq), index["batch"]),
            device_id_type=MESH,
        )
        copy.start()
        gather.point()
        copy.wait()
        first = jnp.where(me == 0, 1.0, 0.0)
        prev_ref[slot] = arrive_ref[slot] * (1.0 - first)
        prev_ref[slot, 0:segments, :] += entry_ref[...].astype(F32) * first

    swap_edges(att_entry_ref, 0, 1, 0)

    def mix_one(at, current, previous):
        for c in range(4):
            blend = table_ref[2 + c : 3 + c, :]
            mixed_ref[c, at, :] = (current * blend + previous * (1.0 - blend)).astype(BF16)

    for q in range(segments):
        shift_rows(q, 0, 1, 0, mix_one)
        gather.point()
    save(mixed_ref)

    def shifted_tile(column, n):
        return pl.ds(pl.multiple_of(column + n * 256, 256), 256)

    def project_to(array, left, target_ref):
        for unit in range(starts[array], starts[array + 1]):
            await_unit(unit)
            column, size = span(plan[unit])

            def run(n, carry, column=column):
                window = shifted_tile(column, n)
                target_ref[:, window] = dot(left[...], weight(array, window), 1, 0).astype(target_ref.dtype)
                return carry

            lax.fori_loop(0, size // 256, run, 0)
            gather.point()

    project_to(1, mixed_ref.at[1], k_ref)
    project_to(2, mixed_ref.at[2], v_ref)
    save(k_ref, v_ref)
    ones, ones16 = block_ones(F32), block_ones(BF16)
    group = lax.div(me * rows, LANES)
    own_log = table_ref[6:7, pl.ds(pl.multiple_of(group * LANES, LANES), LANES)]
    fade_ref[...] = column_of(jnp.exp(-length * jnp.exp(own_log)), length)

    def columns(p):
        return pl.ds(pl.multiple_of(p * LANES, LANES), LANES)

    def rate_of(p):
        return jnp.exp(table_ref[6:7, columns(p)])

    def own_states(p, carry):
        _, _, end = decays(rate_of(p), length)
        both = []
        for q in range(segments):
            token = pl.ds(q * length, length)
            k_end = k_ref[token, columns(p)].astype(F32) * end
            both.append(dot2(k_end, v_ref[token, columns(p)], 0, 0, "own"))
        own_ref[columns(p), :] = fold(both[0], both[1], ones).astype(BF16)
        return carry

    lax.fori_loop(0, pairs, own_states, 0)
    first = exchange(grid, index, own_ref, got_ref, rows, send_a, recv_a)
    gather.point()
    project_to(3, mixed_ref.at[0], r_ref)
    project_to(4, mixed_ref.at[3], gate_ref)
    save(r_ref, gate_ref)
    for copy in first:
        copy.wait_recv()
    state = start_ref[...]
    fade = fade_ref[pl.ds(pl.multiple_of(lax.rem(me * rows, LANES), rows), rows), :]
    for block in range(grid.seq):
        at = pl.ds(block * rows, rows)
        out_ref[at, :] = state.astype(BF16)
        state = fade * state + got_ref[at, :].astype(F32)
    second = exchange(grid, index, out_ref, begin_ref, rows, send_b, recv_b)
    gather.point()

    later = lax.broadcasted_iota(jnp.int32, (length, length), 0) > lax.broadcasted_iota(
        jnp.int32, (length, length), 1
    )
    for copy in second:
        copy.wait_recv()

    def inside(p, carry):
        down, up, _ = decays(rate_of(p), length)
        pick = half_masks(length)
        begin = begin_ref[columns(p), :].astype(F32)
        for q in range(segments):
            token = pl.ds(q * length, length)
            r = r_ref[token, columns(p)].astype(F32)
            k = k_ref[token, columns(p)].astype(F32)
            v = v_ref[token, columns(p)]
            r_down = r * down
            k_up = k * up
            halves = []
            for h in range(2):
                r_head = jnp.where(pick == (h == 0), r_down, 0.0)
                scores = jnp.where(later, dot3(r_head, k_up, 1, 1, "score"), 0.0)
                halves.append(dot2(scores, v, 1, 0, "inner"))
            inner = jnp.where(pick, halves[0], halves[1])
            self_part = head_sum(r * table_ref[7:8, columns(p)] * k, ones16)
            inner = inner + self_part * v.astype(F32)
            state16 = unfold(begin, q, ones).astype(BF16)
            y = (inner + dot2(r_down, state16, 1, 0, "cross")).astype(BF16)
            wkv_ref[token, columns(p)] = y
            center = y.astype(F32) - dot(y, ones16, 1, 0) * (1.0 / SUBSPACE_EXTENT)
            spread = head_sum(center * center, ones16) * (1.0 / SUBSPACE_EXTENT)
            z = center * lax.rsqrt(spread + 0.00064)
            normalized = z * table_ref[8:9, columns(p)] + table_ref[9:10, columns(p)]
            g = gate_ref[token, columns(p)]
            attended_ref[token, columns(p)] = (normalized * g / (1.0 + jnp.exp(-g))).astype(BF16)
        return carry

    for p in range(pairs):
        lax.fori_loop(p, p + 1, inside, 0)
        gather.point()
    save(wkv_ref, attended_ref)

    await_unit(first_piece(5))

    def out_project(n, carry):
        value = dot(attended_ref[...], weight(5, tile(n)), 1, 0)
        middle_ref[:, tile(n)] = x_ref[:, tile(n)].astype(F32) + value
        return carry

    lax.fori_loop(0, width // 256, out_project, 0)
    save(middle_ref)
    gather.point()
    norm(middle_ref)
    gather.point()
    swap_edges(ffn_entry_ref, 10, 11, 1)

    def mix_two(at, current, previous):
        for c in range(2):
            blend = table_ref[12 + c : 13 + c, :]
            mixed2_ref[c, at, :] = (current * blend + previous * (1.0 - blend)).astype(BF16)

    for q in range(segments):
        shift_rows(q, 10, 11, 1, mix_two)
        gather.point()
    save(mixed2_ref)
    await_unit(first_piece(6))

    def receive(n, carry):
        value = dot(mixed2_ref[1], weight(6, tile(n)), 1, 0)
        recv = 1.0 / (1.0 + jnp.exp(-value))
        recv_ref[:, tile(n)] = recv
        d_carried_ref[:, tile(n)] = (recv * up_ref[:, tile(n)].astype(F32)).astype(BF16)
        return carry

    lax.fori_loop(0, width // 256, receive, 0)
    save(d_carried_ref)
    gather.point()

    for piece in range(starts[7], starts[8]):
        column, size = span(plan[piece])
        await_unit(piece)

        def key(n, carry, column=column):
            window = shifted_tile(column, n)
            value = jnp.maximum(dot(mixed2_ref[0], weight(7, window), 1, 0), 0.0)
            hidden_ref[:, window] = (value * value).astype(BF16)
            return carry

        lax.fori_loop(0, size // 256, key, 0)
        gather.point()
    save(hidden_ref)
    for piece in range(starts[8], len(plan)):
        column, size = span(plan[piece])
        await_unit(piece)
        window = pl.ds(column, size)

        def carry_out(m, carry):
            at = tile(m, 256)
            carried = dot(hidden_ref[at, :], weight(8, window), 1, 0)
            recv = recv_ref[at, window]
            result_ref[at, window] = (middle_ref[at, window] + recv * carried).astype(BF16)
            upstream = up_ref[at, window].astype(F32)
            d_recv_ref[at, window] = (recv * (1.0 - recv) * carried * upstream).astype(BF16)
            return carry

        lax.fori_loop(0, tokens // 256, carry_out, 0)
        gather.point()

    save(d_recv_ref)
    for copy in first + second:
        copy.wait_send()
    gather.close()
    for copy in saved:
        copy.wait()


def forward(grid, x, upstream, att_entry, ffn_entry, start, shards, length):
    tokens, width = x.shape
    steps = [LANES, CHUNK // 2] + [CHUNK] * 6 + [TALL]
    plan, starts = gather_plan([(s.shape[1], step) for s, step in zip(shards, steps)])
    total = sum(len(unit[1]) for unit in plan)
    hidden = shards[7].shape[1]
    vmem = pl.BlockSpec(memory_space=pltpu.VMEM)
    anywhere = pl.BlockSpec(memory_space=pl.ANY)
    flat = jax.ShapeDtypeStruct((tokens, width), BF16)
    state = pltpu.VMEM((width, LANES), BF16)
    sems = pltpu.SemaphoreType.DMA((grid.seq - 1,))
    count = total * sum(size - 1 for size in grid.shape)
    kept = [
        ((4, tokens, width), BF16), ((tokens, width), BF16), ((tokens, width), BF16), ((tokens, width), BF16),
        ((tokens, width), F32), ((tokens, width), BF16), ((tokens, width), BF16), ((tokens, width), F32),
        ((2, tokens, width), BF16), ((tokens, hidden), BF16), ((tokens, width), BF16), ((tokens, width), BF16),
    ]
    return pl.pallas_call(
        functools.partial(forward_kernel, grid, length, plan, starts),
        out_shape=[jax.ShapeDtypeStruct(grid.shape + s.shape, s.dtype) for s in shards]
        + [
            flat, jax.ShapeDtypeStruct((16, width), F32), jax.ShapeDtypeStruct((width, LANES), BF16),
            jax.ShapeDtypeStruct((2, 8, width), F32),
        ]
        + [jax.ShapeDtypeStruct(*entry) for entry in kept],
        in_specs=[vmem] * 5 + [anywhere] * 9,
        out_specs=[anywhere] * 9 + [vmem] * 4 + [anywhere] * len(kept),
        scratch_shapes=[pltpu.VMEM(*entry) for entry in kept]
        + [pltpu.VMEM(grid.shape + s.shape, s.dtype) for s in shards]
        + [
            pltpu.VMEM((tokens, width), F32),
            pltpu.VMEM((8, width), F32),
            pltpu.VMEM((2, 8, width), F32),
            pltpu.VMEM((tokens, width), F32),
            state, state, state,
            pltpu.VMEM((LANES, LANES), F32),
            pltpu.SemaphoreType.DMA((total,)),
            pltpu.SemaphoreType.DMA((count,)),
            pltpu.SemaphoreType.DMA((count,)),
            pltpu.SemaphoreType.DMA((len(plan),)),
            pltpu.SemaphoreType.DMA((len(kept),)),
            pltpu.SemaphoreType.DMA((2,)),
            pltpu.SemaphoreType.DMA((2,)),
            sems, sems, sems, sems,
        ],
        compiler_params=pltpu.CompilerParams(
            collective_id=0, has_side_effects=True, vmem_limit_bytes=VMEM_LIMIT
        ),
    )(x, upstream, att_entry, ffn_entry, start, *shards)


STAGES = ("c", "first", "second", "z")
GAPS = (1, 2, 2, 2)
ALL = (3, 2, 1, 0)
SLOTS = (1, 1, 1, 1)
TICKS = (
    0, 0, 1, 4, 3, 1, 3, 0, 0, 0, 1, 0, 0, 0, 0, 0, 1, 0, 0, 1, 0, 0, 0, 0, 1, 0, 0, 0, 1, 4, 3, 0, 4, 4, 0, 3, 0, 1, 0, 0,
    2, 4, 4, 3, 2, 0, 0, 0,
)


class Piece:
    def __init__(self, array, column, columns, tile, first, kind):
        self.array, self.column, self.columns = array, column, columns
        self.first, self.second = (first, "y" if first == "x" else "x")
        self.tile, self.kind = (tile, columns), kind
        self.group = (tile, columns, first, jnp.dtype(kind).name)


def scatter_plan(arrays):
    units, of_array, counts = [], [], {}
    for array, (tile, columns, step, kind) in enumerate(arrays):
        mine = []
        at = 0
        while at < columns:
            unit = []
            for first in ("x", "y"):
                if at < columns:
                    piece = Piece(array, at, step, tile, first, kind)
                    piece.place = counts.get(piece.group, 0)
                    counts[piece.group] = piece.place + 1
                    unit.append(piece)
                    at += step
            mine.append(len(units))
            units.append(unit)
        of_array.append(mine)
    return units, of_array, counts


def stage_shapes(grid, group):
    tile, columns, first, _ = group
    second = "y" if first == "x" else "x"
    end = (tile, columns)
    return [
        grid.sizes("c") + end,
        (grid.size[first] - 1,) + grid.sizes("c" + first) + end,
        (grid.size[second] - 1,) + grid.sizes("cxy") + end,
        (grid.size["z"] - 1,) + end,
    ]


class Scatter:
    def __init__(self, grid, index, digit, units, keeps, gives, landings, loads, outs, send_sem, recv_sem, load_sem):
        self.grid, self.index, self.digit, self.units = grid, index, digit, units
        self.keeps, self.gives, self.landings, self.loads, self.outs = keeps, gives, landings, loads, outs
        self.send_sem, self.recv_sem, self.load_sem = send_sem, recv_sem, load_sem
        self.started, self.pending, self.giving = [], {}, {}
        self.stage, self.when, self.now, self.reading, self.places = {}, {}, 0, [], 0

    def copy(self, source, target, name, digit):
        slot = len(self.started)
        copy = pltpu.make_async_remote_copy(
            src_ref=source,
            dst_ref=target,
            send_sem=self.send_sem.at[slot],
            recv_sem=self.recv_sem.at[slot],
            device_id=self.grid.peer(self.index, self.digit, name, digit),
            device_id_type=MESH,
        )
        copy.start()
        self.started.append([copy, True])
        return copy

    def open(self, unit, number):
        piece = self.units[unit][number]
        if piece.group in self.giving:
            entry = self.giving.pop(piece.group)
            entry[0].wait_send()
            entry[1] = False
        return self.keeps[unit, number], self.gives[piece.group]

    def give(self, unit):
        for number, piece in enumerate(self.units[unit]):
            target = lax.rem(self.digit["c"] + 1, 2)
            copy = self.copy(self.gives[piece.group], self.landings[piece.group][0].at[piece.place], "c", target)
            self.giving[piece.group] = self.started[-1]
            self.pending[unit, number] = [copy]
        self.stage[unit], self.when[unit] = 0, self.now

    def load(self, unit, number, slot):
        piece, stage = self.units[unit][number], self.stage[unit]
        for copy in self.pending[unit, number]:
            copy.wait_recv()
        copy = pltpu.make_async_copy(
            self.landings[piece.group][stage].at[piece.place],
            self.loads[piece.group][stage].at[slot],
            self.load_sem.at[2 * (sum(SLOTS[:stage]) + slot) + number],
        )
        copy.start()
        return copy

    def add(self, unit, number, slot, copy):
        piece, stage = self.units[unit][number], self.stage[unit]
        keep, got = self.keeps[unit, number], self.loads[piece.group][stage].at[slot]
        names = [n for n in self.grid.order if n != "c"]
        fixed = ((), (piece.first,), (piece.first, piece.second), ("x", "y", "z"))[stage]
        free = [n for n in names if n not in fixed]
        copy.wait()
        terms = 1 if stage == 0 else got.shape[0]
        steps = 1
        for n in free:
            steps *= self.grid.size[n]

        def body(i, carry):
            at, rest = {n: self.digit[n] for n in fixed}, i
            for n in reversed(free):
                at[n] = lax.rem(rest, self.grid.size[n])
                rest = lax.div(rest, self.grid.size[n])
            where, inner = tuple(at[n] for n in names), tuple(at[n] for n in free)
            value = keep[where].astype(F32)
            for j in range(terms):
                value = value + got[inner if stage == 0 else (j,) + inner].astype(F32)
            if stage == 3:
                self.outs[piece.array][:, piece.column : piece.column + piece.columns] = value
            else:
                keep[where] = value.astype(keep.dtype)
            return carry

        if steps == 1:
            body(0, 0)
        else:
            lax.fori_loop(0, steps, body, 0)
        if stage == 3:
            return
        name = (piece.first, piece.second, "z")[stage]
        held = {n: self.digit[n] for n in fixed}
        copies = []
        for j in range(1, self.grid.size[name]):
            target = lax.rem(self.digit[name] + j, self.grid.size[name])
            source = self.grid.at(keep, "c", **held, **{name: target})
            copies.append(self.copy(source, self.landings[piece.group][stage + 1].at[piece.place, j - 1], name, target))
        self.pending[unit, number] = copies

    def finish(self):
        for unit, slot, copies in self.reading:
            for number, copy in enumerate(copies):
                self.add(unit, number, slot, copy)
            self.stage[unit] += 1
            self.when[unit] = self.now
            if self.stage[unit] == 4:
                del self.stage[unit]
        self.reading = []

    def tick(self, stages, gaps=GAPS):
        self.now += 1
        self.finish()
        for stage in stages:
            waiting = [u for u in sorted(self.stage) if self.stage[u] == stage and self.now - self.when[u] >= gaps[stage]]
            for slot, unit in enumerate(waiting[: SLOTS[stage]]):
                copies = [self.load(unit, number, slot) for number in range(len(self.units[unit]))]
                self.reading.append((unit, slot, copies))

    def point(self):
        kind = TICKS[self.places]
        self.places += 1
        for stages in ((), (ALL,), (ALL, ALL), ((0,),), (ALL[:3],))[kind]:
            self.tick(stages)

    def close(self):
        while self.stage:
            self.tick((0, 1, 2, 3), gaps=(1, 1, 1, 1))
            self.finish()
        for copy, waiting in self.started:
            if waiting:
                copy.wait_send()


def backward_kernel(grid, length, units, of_array, groups, *refs):
    it = iter(refs)

    def take(count):
        return [next(it) for _ in range(count)]

    (table_ref, prev_ref, begin_ref) = take(3)
    (
        x_hbm, up_hbm, mixed_hbm, r_hbm, k_hbm, v_hbm, gate_hbm, wkv_hbm, attended_hbm, middle_hbm, mixed2_hbm,
        hidden_hbm, d_carried_hbm, d_recv_hbm,
    ) = take(14)
    w_k, w_v, w_r, w_g, w_o, f_r, f_k, f_v = take(8)
    (d_input_ref,) = take(1)
    outs = take(len(of_array))
    landings = {group: take(4) for group in groups}
    keeps = {(u, n): next(it) for u, unit in enumerate(units) for n in range(len(unit))}
    gives = {group: next(it) for group in groups}
    loads = {group: take(4) for group in groups}
    (
        hid, dc, dr, m2, dkey, wide, tall, dn, db, mid, nrm, up, dmid, rr, kk, vv, wk, dgate,
        own_ref, got_ref, out_ref, end_ref, fade_ref, acc, edge_ref, arrive_ref,
        send_sem, recv_sem, load_sem, in_sem, wide_sem, edge_send, edge_recv, send_a, recv_a, send_b, recv_b,
    ) = it
    index, digit = grid.place()
    me = index["seq"]
    tokens, width = dc.shape
    segments = tokens // length
    pairs, rows = width // LANES, width // grid.seq
    n0 = grid.shape[0]
    c_at = grid.order.index("c") - 1
    scatter = Scatter(grid, index, digit, units, keeps, gives, landings, loads, outs, send_sem, recv_sem, load_sem)
    batch_roles = [n for n in grid.order if grid.axis[n] == "batch"]
    peers = [
        grid.peer(index, digit, n, lax.rem(digit[n] + j, grid.size[n])) for n in batch_roles for j in range(1, grid.size[n])
    ]
    peers += [(lax.rem(me + j, grid.seq), index["batch"]) for j in range(1, grid.seq)]

    fetched = {}

    def fetch(name, source, target, slot):
        copy = pltpu.make_async_copy(source, target, in_sem.at[slot])
        copy.start()
        fetched[name] = copy

    def have(*names):
        for name in names:
            fetched.pop(name).wait()

    fetch("hid", hidden_hbm, hid, 0)
    fetch("dc", d_carried_hbm, dc, 1)
    fetch("tall", f_v.at[0], tall, 2)
    fetch("m2", mixed2_hbm, m2, 3)
    fetch("dr", d_recv_hbm, dr, 4)
    fetch("mid", middle_hbm, mid, 5)
    fetch("up", up_hbm, up, 6)
    fetch("att", attended_hbm, dgate, 7)
    fetch("rr", r_hbm, rr, 8)
    fetch("kk", k_hbm, kk, 9)
    fetch("vv", v_hbm, vv, 10)
    fetch("wk", wkv_hbm, wk, 11)
    acc[...] = jnp.zeros_like(acc)
    greet(peers)

    everything = (slice(None),) * 5

    def weight_load(array, column, columns, slot):
        copy = pltpu.make_async_copy(
            array.at[everything + (pl.ds(column, columns),)],
            wide.at[(slot,) + everything + (pl.ds(0, columns),)],
            wide_sem.at[slot],
        )
        copy.start()
        return copy

    def weight(slot, columns):
        return wide[(slot,) + everything + (pl.ds(0, columns),)].reshape((-1, columns))

    def tile(n, step):
        return pl.ds(pl.multiple_of(n * step, step), step)

    def gradient(unit, left_ref, right_ref):
        parts = units[unit]
        targets = [scatter.open(unit, number) for number in range(len(parts))]
        span, narrow = left_ref.shape[1] // n0, parts[0].columns < 256
        for batch in [list(range(len(parts)))] if narrow else [[number] for number in range(len(parts))]:
            first = parts[batch[0]]
            width_all = sum(parts[number].columns for number in batch)

            def run(y, carry, batch=batch, first=first, width_all=width_all):
                total = dot(left_ref[:, tile(y, span)], right_ref[:, first.column : first.column + width_all], 0, 0)
                is_zero = digit["c"] == 0
                for number in batch:
                    keep, give = targets[number]
                    at = parts[number].column - first.column
                    value = total[:, at : at + parts[number].columns].reshape(grid.shape[1:] + parts[number].tile)
                    zero = value[(slice(None),) * c_at + (0,)]
                    one = value[(slice(None),) * c_at + (1,)]
                    keep[y] = jnp.where(is_zero, zero, one).astype(keep.dtype)
                    give[y] = jnp.where(is_zero, one, zero).astype(give.dtype)
                return carry

            lax.fori_loop(0, n0, run, 0)
        scatter.give(unit)

    U = dict(zip(("fv", "fr", "fk", "o", "g", "r", "k", "v", "small"), of_array))

    have("hid", "dc")
    for unit in U["fv"]:
        gradient(unit, hid, dc)
        scatter.point()
    span = hid.shape[1] // n0
    loading = weight_load(f_r, 0, width, 0)
    for y in range(n0):
        have("tall")

        def key(m, carry, y=y):
            at = tile(m, 128)
            window = slice(y * span, (y + 1) * span)
            d_hidden = dot(dc[at, :], tall[...].reshape((span, width)), 1, 1)
            dkey[at, window] = (2.0 * jnp.sqrt(hid[at, window].astype(F32)) * d_hidden).astype(BF16)
            return carry

        lax.fori_loop(0, tokens // 128, key, 0)
        if y + 1 < n0:
            fetch("tall", f_v.at[y + 1], tall, 2)
        if y < 2:
            scatter.point()
    have("m2", "dr")
    gradient(U["fr"][0], m2.at[1], dr)
    fetch("mx0", mixed_hbm.at[0], hid.at[:, pl.ds(0, width)], 0)
    fetch("mx1", mixed_hbm.at[1], hid.at[:, pl.ds(width, width)], 1)
    fetch("mx2", mixed_hbm.at[2], hid.at[:, pl.ds(2 * width, width)], 2)
    scatter.point()
    loading.wait()
    chunks = pieces(hid.shape[1], CHUNK)
    loading = weight_load(f_k, *chunks[0], 1)

    def through_recv(m, carry):
        at = tile(m, 256)
        db[at, :] = dot(dr[at, :], weight(0, width), 1, 1)
        return carry

    lax.fori_loop(0, tokens // 256, through_recv, 0)
    scatter.point()
    for number, unit in enumerate(U["fk"]):
        gradient(unit, m2.at[0], dkey)
        scatter.point()
        column, columns = chunks[number]
        slot = (number + 1) % 2
        loading.wait()
        if number + 1 < len(chunks):
            loading = weight_load(f_k, *chunks[number + 1], 1 - slot)

        def through_key(m, carry, number=number, column=column, columns=columns, slot=slot):
            at = tile(m, 256)
            value = dot(dkey[at, column : column + columns], weight(slot, columns), 1, 1)
            dn[at, :] = value if number == 0 else dn[at, :] + value
            return carry

        lax.fori_loop(0, tokens // 256, through_key, 0)
        scatter.point()
    fetch("mx3", mixed_hbm.at[3], m2.at[0], 3)
    loading = weight_load(w_o, 0, width, 0)

    step = 64

    def fold_rows(value):
        return jnp.sum(value.reshape((step // 8, 8, width)), axis=0)

    def norm(source_ref, gain, bias):
        def run(i, carry):
            at = tile(i, step)
            value = source_ref[at, :].astype(F32)
            center = value - jnp.mean(value, axis=-1, keepdims=True)
            spread = jnp.mean(center * center, axis=-1, keepdims=True)
            nrm[at, :] = center * lax.rsqrt(spread + 1e-05) * table_ref[gain : gain + 1, :] + table_ref[bias : bias + 1, :]
            return carry

        lax.fori_loop(0, tokens // step, run, 0)

    def swap_edges(slot):
        edge_ref[...] = jnp.zeros_like(edge_ref)
        for q in range(segments):
            edge_ref[q : q + 1, :] = db[q * length : q * length + 8, :][0:1, :]
        copy = pltpu.make_async_remote_copy(
            src_ref=edge_ref,
            dst_ref=arrive_ref.at[slot],
            send_sem=edge_send.at[slot],
            recv_sem=edge_recv.at[slot],
            device_id=(lax.rem(me + grid.seq - 1, grid.seq), index["batch"]),
            device_id_type=MESH,
        )
        copy.start()
        return copy

    def norm_back(source_ref, gain, bias, slot, base_ref, put):
        keep_next = jnp.where(me == grid.seq - 1, 0.0, 1.0)
        for q in range(segments):
            count = length // step

            def run(i, carry, q=q):
                at = tile(q * count + count - 1 - i, step)
                value = source_ref[at, :].astype(F32)
                center = value - jnp.mean(value, axis=-1, keepdims=True)
                spread = jnp.mean(center * center, axis=-1, keepdims=True)
                scale = lax.rsqrt(spread + 1e-05)
                z = center * scale
                before = db[at, :]
                row = lax.broadcasted_iota(jnp.int32, (step, 1), 0)
                d_normed = dn[at, :] + jnp.where(row == step - 1, carry, pltpu.roll(before, step - 1, 0))
                acc[gain] += fold_rows(z * d_normed)
                acc[bias] += fold_rows(d_normed)
                e = d_normed * table_ref[gain : gain + 1, :]
                back = (e - jnp.mean(e, axis=-1, keepdims=True) - z * jnp.mean(e * z, axis=-1, keepdims=True)) * scale
                put(at, base_ref[at, :].astype(F32) + back)
                return before[0:1, :]

            lax.fori_loop(0, count, run, arrive_ref[slot, q : q + 1, :] * keep_next)
            scatter.point()

    have("mid")
    norm(mid, 10, 11)
    scatter.point()
    for q in range(segments):

        def blend_two(i, carry, q=q):
            at = tile(q * (length // step) + i, step)
            current = nrm[at, :]
            row = lax.broadcasted_iota(jnp.int32, (step, 1), 0)
            difference = current - jnp.where(row == 0, carry, pltpu.roll(current, 1, 0))
            first, second = dn[at, :], db[at, :]
            acc[12] += fold_rows(difference * first)
            acc[13] += fold_rows(difference * second)
            a, b = table_ref[12:13, :], table_ref[13:14, :]
            dn[at, :] = first * a + second * b
            db[at, :] = first * (1.0 - a) + second * (1.0 - b)
            return current[step - 1 : step, :]

        lax.fori_loop(0, length // step, blend_two, prev_ref[1, q : q + 1, :])
        scatter.point()
    moving = swap_edges(0)
    scatter.point()
    have("up")
    moving.wait()

    def put_middle(at, value):
        dmid[at, :] = value
        dr[at, :] = value.astype(BF16)

    norm_back(mid, 10, 11, 0, up, put_middle)
    fetch("mid", gate_hbm, mid, 5)
    fetch("up", x_hbm, up, 6)
    have("att")
    gradient(U["o"][0], dgate, dr)
    scatter.point()
    loading.wait()

    def through_out(m, carry):
        at = tile(m, 256)
        nrm[at, :] = dot(dr[at, :], weight(0, width), 1, 1)
        return carry

    lax.fori_loop(0, tokens // 256, through_out, 0)
    scatter.point()

    ones, ones16 = block_ones(F32), block_ones(BF16)
    share = 1.0 / SUBSPACE_EXTENT

    def columns(p, base=0):
        return pl.ds(pl.multiple_of(base + p * LANES, LANES), LANES)

    def rate_of(p):
        return jnp.exp(table_ref[6:7, columns(p)])

    group = lax.div(me * rows, LANES)
    own_log = table_ref[6:7, pl.ds(pl.multiple_of(group * LANES, LANES), LANES)]
    fade_ref[...] = column_of(jnp.exp(-length * jnp.exp(own_log)), length)
    have("wk", "mid", "rr")

    def own_states(p, carry):
        down, _, _ = decays(rate_of(p), length)
        both = []
        gain_sum, bias_sum = jnp.zeros((1, LANES), F32), jnp.zeros((1, LANES), F32)
        for q in range(segments):
            token = pl.ds(q * length, length)
            y = wk[token, columns(p)]
            center = y.astype(F32) - dot(y, ones16, 1, 0) * share
            spread = head_sum(center * center, ones16) * share
            scale = lax.rsqrt(spread + 0.00064)
            z = center * scale
            gain = table_ref[8:9, columns(p)]
            normalized = z * gain + table_ref[9:10, columns(p)]
            g = mid[token, columns(p)]
            s = 1.0 / (1.0 + jnp.exp(-g))
            d_att = nrm[token, columns(p)]
            dgate[token, columns(p)] = (d_att * normalized * s * (1.0 + g * (1.0 - s))).astype(BF16)
            d_norm = d_att * g * s
            gain_sum = gain_sum + jnp.sum(d_norm * z, axis=0, keepdims=True)
            bias_sum = bias_sum + jnp.sum(d_norm, axis=0, keepdims=True)
            e = d_norm * gain
            dy = ((e - head_sum(e, ones16) * share - z * (head_sum(e * z, ones16) * share)) * scale).astype(BF16)
            dc[token, columns(p)] = dy
            both.append(dot2(rr[token, columns(p)].astype(F32) * down, dy, 0, 0, "own"))
        acc[8, 0:1, columns(p)] = gain_sum
        acc[9, 0:1, columns(p)] = bias_sum
        own_ref[columns(p), :] = fold(both[0], both[1], ones).astype(BF16)
        return carry

    for quarter in range(4):
        lax.fori_loop(quarter * pairs // 4, (quarter + 1) * pairs // 4, own_states, 0)
        scatter.point()
    first = exchange(grid, index, own_ref, got_ref, rows, send_a, recv_a)
    have("mx3")
    gradient(U["g"][0], m2.at[0], dgate)
    scatter.point()
    for copy in first:
        copy.wait_recv()
    fade = fade_ref[pl.ds(pl.multiple_of(lax.rem(me * rows, LANES), rows), rows), :]
    state = jnp.zeros_like(fade)
    for block in reversed(range(grid.seq)):
        at = pl.ds(block * rows, rows)
        out_ref[at, :] = state.astype(BF16)
        state = fade * state + got_ref[at, :].astype(F32)
    second = exchange(grid, index, out_ref, end_ref, rows, send_b, recv_b)
    scatter.point()
    have("up")
    norm(up, 0, 1)
    scatter.point()
    have("kk", "vv")
    for copy in second:
        copy.wait_recv()
    later = lax.broadcasted_iota(jnp.int32, (length, length), 0) > lax.broadcasted_iota(
        jnp.int32, (length, length), 1
    )
    time = lax.broadcasted_iota(jnp.int32, (length, LANES), 0).astype(F32)

    def inside(p, carry):
        rate = rate_of(p)
        reward = table_ref[7:8, columns(p)]
        down, up_, end = decays(rate, length)
        pick = half_masks(length)
        begins, ends = begin_ref[columns(p), :].astype(F32), end_ref[columns(p), :].astype(F32)
        reward_sum, rate_sum = jnp.zeros((1, LANES), F32), jnp.zeros((1, LANES), F32)
        for q in range(segments):
            token = pl.ds(q * length, length)
            r = rr[token, columns(p)].astype(F32)
            k = kk[token, columns(p)].astype(F32)
            v = vv[token, columns(p)]
            dy = dc[token, columns(p)]
            begin, finish = unfold(begins, q, ones), unfold(ends, q, ones)
            begin16, finish16 = begin.astype(BF16), finish.astype(BF16)
            r_down = (r * down).astype(BF16)
            k_up = (k * up_).astype(BF16)
            k_end = k * end
            zero = jnp.zeros_like(r_down)
            d_r, d_k, d_v = [], [], []
            for h in range(2):
                here = pick == (h == 0)
                scores = jnp.where(later, dot(jnp.where(here, r_down, zero), k_up, 1, 1), 0.0)
                d_scores = jnp.where(later, dot(jnp.where(here, dy, zero), v, 1, 1), 0.0).astype(BF16)
                d_r.append(dot(d_scores, k_up, 1, 0))
                d_k.append(dot(d_scores, r_down, 0, 0))
                d_v.append(dot2(scores, dy, 0, 0, "inner"))
            from_r = jnp.where(pick, d_r[0], d_r[1]) + dot(dy, begin16, 1, 1)
            from_k = jnp.where(pick, d_k[0], d_k[1])
            from_end = dot(v, finish16, 1, 1)
            v32, dy32 = v.astype(F32), dy.astype(F32)
            v_dy = head_sum(v32 * dy32, ones16)
            self_part = head_sum(r * reward * k, ones16)
            dkey[token, columns(p)] = (from_r * down + reward * k * v_dy).astype(BF16)
            dkey[token, columns(p, width)] = (from_k * up_ + from_end * end + reward * r * v_dy).astype(BF16)
            dkey[token, columns(p, 2 * width)] = (
                jnp.where(pick, d_v[0], d_v[1]) + dot2(k_end, finish16, 1, 0, "cross") + self_part * dy32
            ).astype(BF16)
            reward_sum = reward_sum + jnp.sum(r * k * v_dy, axis=0, keepdims=True)
            terms = (
                (time + 1.0) * k_up.astype(F32) * from_k
                - time * r_down.astype(F32) * from_r
                - (length - 1.0 - time) * k_end * from_end
            )
            through = lax.dot_general(
                jnp.ones((8, LANES), F32), begin * finish, (((1,), (1,)), ((), ())),
                precision=lax.Precision.HIGHEST, preferred_element_type=F32,
            )[0:1, :]
            rate_sum = rate_sum + jnp.sum(terms, axis=0, keepdims=True) - length * jnp.exp(-rate * length) * through
        acc[7, 0:1, columns(p)] = reward_sum
        acc[6, 0:1, columns(p)] = rate_sum * rate
        return carry

    for p in range(pairs):
        lax.fori_loop(p, p + 1, inside, 0)
        scatter.point()
    have("mx0", "mx1", "mx2")
    weights = (w_r, w_k, w_v, w_g)
    grads = [dkey.at[:, pl.ds(c * width, width)] for c in range(3)] + [dgate]

    def load_rows(y):
        copies = []
        for c in range(4):
            copy = pltpu.make_async_copy(weights[c].at[y], wide.at[c // n0, c % n0], in_sem.at[8 + c])
            copy.start()
            copies.append(copy)
        return copies

    loading = load_rows(0)
    for c, name in enumerate("rkv"):
        gradient(U[name][0], hid.at[:, pl.ds(c * width, width)], grads[c])
        scatter.point()
    span = width // n0
    for y in range(n0):
        for copy in loading:
            copy.wait()
        window = slice(y * span, (y + 1) * span)

        def through_mix(m, carry, y=y, window=window):
            at = tile(m, 128)
            current = nrm[at, window]
            above = nrm[pl.ds(pl.multiple_of(jnp.maximum(m * 128 - 8, 0), 8), 8), window][7:8, :]
            segment = lax.div(m, length // 128)
            given = prev_ref[0, 0:1, window]
            for q in range(1, segments):
                given = jnp.where(segment == q, prev_ref[0, q : q + 1, window], given)
            carried = jnp.where(lax.rem(m, length // 128) == 0, given, above)
            row = lax.broadcasted_iota(jnp.int32, (128, 1), 0)
            difference = current - jnp.where(row == 0, carried, pltpu.roll(current, 1, 0))
            here, before = None, None
            for c in range(4):
                value = dot(grads[c][at, :], wide[c // n0, c % n0].reshape((span, width)), 1, 1)
                acc[2 + c, :, window] += jnp.sum((difference * value).reshape((16, 8, span)), axis=0)
                blend = table_ref[2 + c : 3 + c, window]
                here = blend * value if c == 0 else here + blend * value
                before = (1.0 - blend) * value if c == 0 else before + (1.0 - blend) * value
            dn[at, window] = here
            db[at, window] = before
            return carry

        lax.fori_loop(0, tokens // 128, through_mix, 0)
        if y + 1 < n0:
            loading = load_rows(y + 1)
        if y < 2:
            scatter.point()
    moving = swap_edges(1)
    scatter.point()
    moving.wait()

    def put_input(at, value):
        dr[at, :] = value.astype(BF16)

    norm_back(up, 0, 1, 1, dmid, put_input)
    fetch("result", dr, d_input_ref, 4)

    sums = [jnp.sum(acc[i], axis=0, keepdims=True) for i in range(14)]
    for i in range(14):
        edge_ref[0:1, :] = sums[i]
        nrm[i : i + 1, :] = edge_ref[0:1, :]
    nrm[14:16, :] = jnp.zeros((2, width), F32)
    keep, give = scatter.open(U["small"][0], 0)
    per = grid.seq * grid.batch // pairs
    names = [n for n in grid.order if n != "c"]

    def spread(i, carry):
        at, rest = {}, i
        for n in reversed(names):
            at[n] = lax.rem(rest, grid.size[n])
            rest = lax.div(rest, grid.size[n])
        for target, core in ((keep, digit["c"]), (give, 1 - digit["c"])):
            spot = dict(at, c=core)
            rank = 0
            for n in grid.order:
                rank = rank * grid.size[n] + spot[n]
            target[tuple(at[n] for n in names)] = nrm[0:16, columns(lax.div(rank, per))]
        return carry

    steps = 1
    for n in names:
        steps *= grid.size[n]
    lax.fori_loop(0, steps, spread, 0)
    scatter.give(U["small"][0])
    scatter.point()
    for copy in first + second:
        copy.wait_send()
    scatter.close()
    have("result")


def backward(grid, length, table, prev, begin, stored, weights):
    tokens, width = stored[0].shape
    hidden = stored[11].shape[1]
    blk, tall = weights[0].shape[4], weights[7].shape[4]
    arrays = [
        (tall, width, LANES, BF16), (blk, width, 512, BF16), (blk, hidden, 512, BF16), (blk, width, 512, BF16),
        (blk, width, 512, BF16), (blk, width, 512, BF16), (blk, width, 512, BF16), (blk, width, 512, BF16),
        (16, LANES, LANES, F32),
    ]
    units, of_array, counts = scatter_plan(arrays)
    groups = list(counts)
    kinds = {group: jnp.dtype(group[3]) for group in groups}
    shapes = {group: stage_shapes(grid, group) for group in groups}
    vmem = pl.BlockSpec(memory_space=pltpu.VMEM)
    anywhere = pl.BlockSpec(memory_space=pl.ANY)
    flat16, flat32 = pltpu.VMEM((tokens, width), BF16), pltpu.VMEM((tokens, width), F32)
    state = pltpu.VMEM((width, LANES), BF16)
    sems = pltpu.SemaphoreType.DMA((grid.seq - 1,))
    dma = pltpu.SemaphoreType.DMA
    count = sum(len(unit) for unit in units) * sum(size - 1 for size in grid.shape)
    landing = [
        jax.ShapeDtypeStruct((counts[group],) + shape, kinds[group]) for group in groups for shape in shapes[group]
    ]
    outs = pl.pallas_call(
        functools.partial(backward_kernel, grid, length, units, of_array, groups),
        out_shape=[jax.ShapeDtypeStruct((tokens, width), BF16)]
        + [jax.ShapeDtypeStruct((a[0], a[1]), F32) for a in arrays]
        + landing,
        in_specs=[vmem] * 3 + [anywhere] * 22,
        out_specs=[anywhere] + [vmem] * len(arrays) + [anywhere] * len(landing),
        scratch_shapes=[pltpu.VMEM(grid.sizes("c") + p.tile, p.kind) for unit in units for p in unit]
        + [pltpu.VMEM(shapes[group][0], kinds[group]) for group in groups]
        + [pltpu.VMEM((slots,) + shape, kinds[group]) for group in groups for slots, shape in zip(SLOTS, shapes[group])]
        + [
            pltpu.VMEM((tokens, hidden), BF16), flat16, flat16, pltpu.VMEM((2, tokens, width), BF16),
            pltpu.VMEM((tokens, hidden), BF16),
            pltpu.VMEM((2,) + grid.shape + (blk, CHUNK), BF16),
            pltpu.VMEM(grid.shape[1:] + (tall, width), BF16),
            flat32, flat32, flat32, flat32, flat16, flat32, flat16, flat16, flat16, flat16, flat16,
            state, state, state, state,
            pltpu.VMEM((LANES, LANES), F32),
            pltpu.VMEM((14, 8, width), F32),
            pltpu.VMEM((8, width), F32),
            pltpu.VMEM((2, 8, width), F32),
            dma((count,)), dma((count,)), dma((2 * sum(SLOTS),)), dma((12,)), dma((2,)), dma((2,)), dma((2,)),
            sems, sems, sems, sems,
        ],
        compiler_params=pltpu.CompilerParams(
            collective_id=1, has_side_effects=True, vmem_limit_bytes=VMEM_LIMIT
        ),
    )(table, prev, begin, *stored, *weights)
    return outs[0], outs[1 : 1 + len(arrays)]


def local(grid, *args):
    (
        incoming, att_entry, ffn_entry, memory, upstream,
        ln1_gain, ln1_bias, att_mix, w_recept, w_key, w_value, w_gate, decay_log, reward,
        gn_gain, gn_bias, w_out, ln2_gain, ln2_bias, ffn_mix, f_key, f_value, f_recept,
    ) = args
    segments, length, width = incoming.shape
    tokens = segments * length
    ranks = grid.seq * grid.batch
    share = width // ranks

    per = LANES // share
    rank = lax.axis_index(("seq", "batch"))
    small = jnp.stack(
        [ln1_gain, ln1_bias] + [att_mix[:, c] for c in range(4)] + [decay_log, reward, gn_gain, gn_bias, ln2_gain, ln2_bias]
        + [ffn_mix[:, c] for c in range(2)]
    )
    small = jnp.tile(jnp.pad(small, ((0, 2), (0, 0))), (1, per))
    lane = lax.broadcasted_iota(jnp.int32, small.shape, 1)
    small = jnp.where(lane // share == rank % per, small, jnp.zeros_like(small))
    rows = width // grid.seq
    row = lax.axis_index("seq") * rows
    start = memory.transpose(1, 2, 0, 3).reshape(width, segments * SUBSPACE_EXTENT)
    start = lax.dynamic_slice_in_dim(start, row, rows, 0)
    shards = [small, w_key, w_value, w_recept, w_gate, w_out, f_recept, f_key, f_value]
    outs = forward(
        grid, incoming.reshape(tokens, width), upstream.reshape(tokens, width), att_entry, ffn_entry, start, shards, length
    )
    (
        result, table, begin, prev, mixed, r, k, v, gate_pre, wkv, attended, middle, mixed2, hidden, d_carried, d_recv,
    ) = outs[9:]
    stored = [
        incoming.reshape(tokens, width), upstream.reshape(tokens, width), mixed, r, k, v, gate_pre, wkv, attended, middle,
        mixed2, hidden, d_carried, d_recv,
    ]
    d_input, (s_fv, s_fr, s_fk, s_o, s_g, s_r, s_k, s_v, s_small) = backward(
        grid, length, table, prev, begin, stored, outs[1:9]
    )
    s = lax.dynamic_slice_in_dim(s_small, (rank % per) * share, share, 1)
    shape = incoming.shape
    return (
        result.reshape(shape), d_input.reshape(shape),
        s[0], s[1], s[2:6].T, s_r, s_k, s_v, s_g, s[6], s[7], s[8], s[9], s_o, s[10], s[11], s[12:14].T,
        s_fk, s_fv, s_fr,
    )


def solution(mesh):
    grid = Grid(mesh.shape["seq"], mesh.shape["batch"])
    both, rows = P(("seq", "batch")), P(("seq", "batch"), None)
    tokens, entry = P("batch", "seq", None), P("batch", None)
    return jax.shard_map(
        functools.partial(local, grid),
        mesh=mesh,
        in_specs=(
            tokens, entry, entry, P("batch", None, None, None), tokens,
            both, both, rows, rows, rows, rows, rows, both, both, both, both, rows, both, both, rows, rows, rows, rows,
        ),
        out_specs=(
            tokens, tokens, both, both, rows, rows, rows, rows, rows, both, both, both, both, rows, both, both, rows,
            rows, rows, rows,
        ),
        check_vma=False,
    )
```

```python
import functools

import jax
import jax.numpy as jnp
from jax import lax
from jax.experimental import pallas as pl
from jax.experimental.pallas import tpu as pltpu
from jax.sharding import PartitionSpec as P

WKV_PARTITIONS = 16
SUBSPACE_EXTENT = 64
LANES = 128
MESH = pl.DeviceIdType.MESH
F32 = jnp.float32
BF16 = jnp.bfloat16
VMEM_LIMIT = 63 * 1024 * 1024


class Grid:
    def __init__(self, seq, batch):
        self.seq, self.batch = seq, batch
        if seq == 8 and batch == 4:
            digits = [("y", "seq", 4, 2), ("x", "seq", 2, 2), ("c", "seq", 1, 2), ("z", "batch", 1, 4)]
        elif seq == 16 and batch == 8:
            digits = [("y", "seq", 4, 4), ("x", "seq", 1, 4), ("z", "batch", 2, 4), ("c", "batch", 1, 2)]
        else:
            raise ValueError("unknown mesh")
        self.order = [name for name, *_ in digits]
        self.axis = {name: axis for name, axis, *_ in digits}
        self.stride = {name: stride for name, _, stride, _ in digits}
        self.size = {name: size for name, *_, size in digits}
        self.shape = tuple(self.size[name] for name in self.order)

    def place(self):
        index = {"seq": lax.axis_index("seq"), "batch": lax.axis_index("batch")}
        return index, {
            name: (index[self.axis[name]] // self.stride[name]) % self.size[name] for name in self.order
        }

    def peer(self, index, digit, name, target):
        where = dict(index)
        axis = self.axis[name]
        where[axis] = index[axis] + (target - digit[name]) * self.stride[name]
        return (where["seq"], where["batch"])

    def at(self, ref, gone="", **fixed):
        return ref.at[tuple(fixed.get(name, slice(None)) for name in self.order if name not in gone)]

    def sizes(self, gone=""):
        return tuple(self.size[name] for name in self.order if name not in gone)


def greet(peers):
    barrier = pltpu.get_barrier_semaphore()
    for peer in peers:
        pl.semaphore_signal(barrier, inc=1, device_id=peer, device_id_type=MESH)
    pl.semaphore_wait(barrier, len(peers))


def dot(a, b, da, db):
    return lax.dot_general(a, b, (((da,), (db,)), ((), ())), preferred_element_type=F32)


PRECISE = dict(score=0, inner=1, cross=1, own=1, back=0)


def parts_of(value):
    high = value.astype(BF16)
    return high, (value - high.astype(F32)).astype(BF16)


def dot2(a, b, da, db, name):
    if not PRECISE[name]:
        return dot(a.astype(BF16), b, da, db)
    high, low = parts_of(a)
    return dot(high, b, da, db) + dot(low, b, da, db)


def dot3(a, b, da, db, name):
    if not PRECISE[name]:
        return dot(a.astype(BF16), b.astype(BF16), da, db)
    a_high, a_low = parts_of(a)
    b_high, b_low = parts_of(b)
    return dot(a_high, b_high, da, db) + (dot(a_low, b_high, da, db) + dot(a_high, b_low, da, db))


def half_masks(rows):
    lane = lax.broadcasted_iota(jnp.int32, (rows, LANES), 1)
    return lane < SUBSPACE_EXTENT


def block_ones(kind):
    row = lax.broadcasted_iota(jnp.int32, (LANES, LANES), 0) // SUBSPACE_EXTENT
    lane = lax.broadcasted_iota(jnp.int32, (LANES, LANES), 1) // SUBSPACE_EXTENT
    return (row == lane).astype(kind)


def head_sum(value, ones):
    high = value.astype(BF16)
    low = (value - high.astype(F32)).astype(BF16)
    return dot(high, ones, 1, 0) + dot(low, ones, 1, 0)


def decays(rate, length):
    step = lax.broadcasted_iota(jnp.int32, (length, LANES), 0).astype(F32)
    return jnp.exp(-rate * step), jnp.exp(rate * (step + 1.0)), jnp.exp(-rate * (length - 1.0 - step))


def fold(first, second, ones):
    pick = half_masks(LANES)
    a, b = first * ones, second * ones
    a = a + pltpu.roll(a, SUBSPACE_EXTENT, 1)
    b = b + pltpu.roll(b, SUBSPACE_EXTENT, 1)
    return jnp.where(pick, a, b)


def unfold(both, segment, ones):
    pick = half_masks(LANES)
    turned = pltpu.roll(both, SUBSPACE_EXTENT, 1)
    full = jnp.where(pick, both, turned) if segment == 0 else jnp.where(pick, turned, both)
    return full * ones


def exchange(grid, index, source, slots, rows, send_sem, recv_sem):
    me, copies = index["seq"], []
    for j in range(1, grid.seq):
        target = lax.rem(me + j, grid.seq)
        copy = pltpu.make_async_remote_copy(
            src_ref=source.at[pl.ds(pl.multiple_of(target * rows, 16), rows)],
            dst_ref=slots.at[pl.ds(pl.multiple_of(me * rows, 16), rows)],
            send_sem=send_sem.at[j - 1],
            recv_sem=recv_sem.at[j - 1],
            device_id=(target, index["batch"]),
            device_id_type=MESH,
        )
        copy.start()
        copies.append(copy)
    here = pl.ds(pl.multiple_of(me * rows, 16), rows)
    slots[here, :] = source[here, :]
    return copies


CHUNK = 1024
TALL = 256
LAGS = (0, 1, 3)
AHEAD = 4
PUMPS = (
    0, 0, 1, 0, 0, 0, 2, 0, 0, 0, 0, 0, 1, 0, 0, 0, 0, 1, 0, 1, 0, 0, 1, 0, 0, 0, 0, 1, 1, 0, 0, 0, 1, 0, 1, 1, 0, 0, 0, 0,
    1, 0, 0, 0, 1, 0, 0, 0, 0, 0,
)


def pieces(columns, step):
    return [(at, min(step, columns - at)) for at in range(0, columns, step)]


class Gather:
    def __init__(self, grid, index, digit, shards, fulls, plan, own_sem, send_sem, recv_sem):
        self.grid, self.index, self.digit = grid, index, digit
        self.shards, self.fulls, self.plan = shards, fulls, plan
        self.own_sem, self.send_sem, self.recv_sem = own_sem, send_sem, recv_sem
        self.started, self.pending, self.own = [], {}, {}
        self.tick, self.done, self.places = 0, 0, 0

    def others(self, name):
        size = self.grid.size[name]
        return [lax.rem(self.digit[name] + j, size) for j in range(1, size)]

    def send(self, source, place, name):
        copies = []
        for target in self.others(name):
            slot = len(self.started)
            copy = pltpu.make_async_remote_copy(
                src_ref=source,
                dst_ref=place,
                send_sem=self.send_sem.at[slot],
                recv_sem=self.recv_sem.at[slot],
                device_id=self.grid.peer(self.index, self.digit, name, target),
                device_id_type=MESH,
            )
            copy.start()
            self.started.append(copy)
            copies.append(copy)
        return copies

    def stage(self, unit, number):
        if not 0 <= unit < len(self.plan):
            return
        for piece in range(len(self.plan[unit][1])):
            self.step(unit, piece, number)

    def step(self, unit, piece, number):
        array, parts = self.plan[unit]
        column, columns, first, second = parts[piece]
        digit = self.digit
        window = pl.ds(column, columns)
        full = self.fulls[array]
        key = (unit, piece)

        def at(**fixed):
            place = tuple(fixed.get(name, slice(None)) for name in self.grid.order)
            return full.at[place + (slice(None), window)]

        if number == 0:
            place = at(**digit)
            source = self.shards[array].at[:, window]
            copy = pltpu.make_async_copy(source, place, self.own_sem.at[len(self.own)])
            copy.start()
            self.own[key] = copy
            self.pending[key] = self.send(source, place, "z")
            return
        for copy in self.pending[key]:
            copy.wait_recv()
        if number == 1:
            self.own[key].wait()
            fixed, name = {n: digit[n] for n in ("x", "y", "c")}, first
        elif number == 2:
            fixed, name = {n: digit[n] for n in (second, "c")}, second
        elif number == 3:
            fixed, name = {"c": digit["c"]}, "c"
        else:
            self.pending[key] = []
            return
        place = at(**fixed)
        self.pending[key] = self.send(place, place, name)

    def open(self, ahead):
        self.ahead = ahead
        for piece in range(ahead):
            self.stage(piece, 0)

    def pump(self, count=1):
        for _ in range(count):
            tick = self.tick
            self.tick += 1
            for number in (1, 2, 3):
                self.stage(tick - LAGS[number - 1], number)
            self.stage(tick + self.ahead, 0)

    def point(self):
        count = PUMPS[self.places]
        self.places += 1
        self.pump(count if self.tick < len(self.plan) + LAGS[2] + 1 else 0)

    def ready(self, piece):
        while self.tick < piece + LAGS[2] + 1:
            self.pump()
        while self.done <= piece:
            self.stage(self.done, 4)
            self.done += 1

    def close(self):
        for copy in self.started:
            copy.wait_send()


def gather_plan(arrays):
    plan, starts = [], []
    for array, (columns, step) in enumerate(arrays):
        starts.append(len(plan))
        for column, size in pieces(columns, step):
            half = size // 2
            if half % LANES:
                plan.append((array, [(column, size, "x", "y")]))
            else:
                plan.append((array, [(column, half, "x", "y"), (column + half, half, "y", "x")]))
    return plan, starts


def span(unit):
    return unit[1][0][0], sum(part[1] for part in unit[1])


def column_of(row, length):
    at = lax.broadcasted_iota(jnp.int32, (LANES, LANES), 0)
    lane = lax.broadcasted_iota(jnp.int32, (LANES, LANES), 1)
    spread = jnp.where(at == lane, jnp.broadcast_to(row, (LANES, LANES)), 0.0)
    return jnp.broadcast_to(jnp.sum(spread, axis=1, keepdims=True), (LANES, LANES))


def forward_kernel(grid, length, plan, starts, *refs):
    (
        x_ref, up_ref, att_entry_ref, ffn_entry_ref, start_ref, *shards
    ) = refs[:14]
    stored = refs[14:23]
    result_ref, table_ref, begin_ref, prev_ref = refs[23:27]
    kept = refs[27:39]
    (
        mixed_ref, r_ref, k_ref, v_ref, gate_ref, wkv_ref, attended_ref, middle_ref, mixed2_ref, hidden_ref,
        d_carried_ref, d_recv_ref,
    ) = places = refs[39:51]
    (
        normed_ref, edge_ref, arrive_ref, recv_ref,
        own_ref, got_ref, out_ref, fade_ref,
        own_sem, send_sem, recv_sem, store_sem, save_sem, edge_send, edge_recv, send_a, recv_a, send_b, recv_b,
    ) = refs[60:]
    fulls = refs[51:60]
    saved = []

    def save(*names):
        for name in names:
            at = [place is name for place in places].index(True)
            copy = pltpu.make_async_copy(name, kept[at], save_sem.at[at])
            copy.start()
            saved.append(copy)

    index, digit = grid.place()
    me = index["seq"]
    tokens, width = x_ref.shape
    segments = tokens // length
    pairs, rows = width // LANES, width // grid.seq
    batch_roles = [n for n in grid.order if grid.axis[n] == "batch"]
    gather = Gather(grid, index, digit, shards, fulls, plan, own_sem, send_sem, recv_sem)
    peers = [grid.peer(index, digit, n, t) for n in batch_roles for t in gather.others(n)]
    peers += [(lax.rem(me + j, grid.seq), index["batch"]) for j in range(1, grid.seq)]
    greet(peers)
    gather.open(AHEAD)
    gather.point()

    def first_piece(array):
        return starts[array]

    def await_unit(unit):
        gather.ready(unit)
        array = plan[unit][0]
        column, columns = span(plan[unit])
        window = (slice(None),) * 5 + (pl.ds(column, columns),)
        copy = pltpu.make_async_copy(fulls[array].at[window], stored[array].at[window], store_sem.at[unit])
        copy.start()
        saved.append(copy)
        gather.point()

    def weight(array, window):
        value = fulls[array][(slice(None),) * 5 + (window,)]
        return value.reshape((-1, value.shape[-1]))

    def tile(n, step=256):
        return pl.ds(pl.multiple_of(n * step, step), step)

    def norm(source_ref):
        step = 64

        def run(i, carry):
            at = pl.ds(pl.multiple_of(i * step, step), step)
            value = source_ref[at, :].astype(F32)
            center = value - jnp.mean(value, axis=-1, keepdims=True)
            spread = jnp.mean(center * center, axis=-1, keepdims=True)
            normed_ref[at, :] = center * lax.rsqrt(spread + 1e-05)
            return carry

        lax.fori_loop(0, tokens // step, run, 0)

    norm(x_ref)
    gather.point()

    gather.ready(0)
    ranks = grid.seq * grid.batch
    small = fulls[0][...].astype(F32).reshape((ranks, 16, LANES))
    per = ranks // pairs
    for p in range(pairs):
        total = small[p * per]
        for j in range(1, per):
            total = total + small[p * per + j]
        table_ref[:, p * LANES : (p + 1) * LANES] = total
    gather.point()

    def shift_rows(segment, gain, bias, slot, body):
        step = 64

        def run(i, carry):
            at = pl.ds(pl.multiple_of(segment * length + i * step, step), step)
            current = normed_ref[at, :] * table_ref[gain : gain + 1, :] + table_ref[bias : bias + 1, :]
            row = lax.broadcasted_iota(jnp.int32, (step, 1), 0)
            previous = jnp.where(row == 0, carry, pltpu.roll(current, 1, 0))
            body(at, current, previous)
            return current[step - 1 : step, :]

        lax.fori_loop(0, length // step, run, prev_ref[slot, segment : segment + 1, :])

    def swap_edges(entry_ref, gain, bias, slot):
        edge_ref[...] = jnp.zeros_like(edge_ref)
        for q in range(segments):
            last = (q + 1) * length
            row = normed_ref[last - 8 : last, :][7:8, :]
            edge_ref[q : q + 1, :] = row * table_ref[gain : gain + 1, :] + table_ref[bias : bias + 1, :]
        copy = pltpu.make_async_remote_copy(
            src_ref=edge_ref,
            dst_ref=arrive_ref.at[slot],
            send_sem=edge_send.at[slot],
            recv_sem=edge_recv.at[slot],
            device_id=(lax.rem(me + 1, grid.seq), index["batch"]),
            device_id_type=MESH,
        )
        copy.start()
        gather.point()
        copy.wait()
        first = jnp.where(me == 0, 1.0, 0.0)
        prev_ref[slot] = arrive_ref[slot] * (1.0 - first)
        prev_ref[slot, 0:segments, :] += entry_ref[...].astype(F32) * first

    swap_edges(att_entry_ref, 0, 1, 0)

    def mix_one(at, current, previous):
        for c in range(4):
            blend = table_ref[2 + c : 3 + c, :]
            mixed_ref[c, at, :] = (current * blend + previous * (1.0 - blend)).astype(BF16)

    for q in range(segments):
        shift_rows(q, 0, 1, 0, mix_one)
        gather.point()
    save(mixed_ref)

    def shifted_tile(column, n):
        return pl.ds(pl.multiple_of(column + n * 256, 256), 256)

    def project_to(array, left, target_ref):
        for unit in range(starts[array], starts[array + 1]):
            await_unit(unit)
            column, size = span(plan[unit])

            def run(n, carry, column=column):
                window = shifted_tile(column, n)
                target_ref[:, window] = dot(left[...], weight(array, window), 1, 0).astype(target_ref.dtype)
                return carry

            lax.fori_loop(0, size // 256, run, 0)
            gather.point()

    project_to(1, mixed_ref.at[1], k_ref)
    project_to(2, mixed_ref.at[2], v_ref)
    save(k_ref, v_ref)
    ones, ones16 = block_ones(F32), block_ones(BF16)
    group = lax.div(me * rows, LANES)
    own_log = table_ref[6:7, pl.ds(pl.multiple_of(group * LANES, LANES), LANES)]
    fade_ref[...] = column_of(jnp.exp(-length * jnp.exp(own_log)), length)

    def columns(p):
        return pl.ds(pl.multiple_of(p * LANES, LANES), LANES)

    def rate_of(p):
        return jnp.exp(table_ref[6:7, columns(p)])

    def own_states(p, carry):
        _, _, end = decays(rate_of(p), length)
        both = []
        for q in range(segments):
            token = pl.ds(q * length, length)
            k_end = k_ref[token, columns(p)].astype(F32) * end
            both.append(dot2(k_end, v_ref[token, columns(p)], 0, 0, "own"))
        own_ref[columns(p), :] = fold(both[0], both[1], ones).astype(BF16)
        return carry

    lax.fori_loop(0, pairs, own_states, 0)
    first = exchange(grid, index, own_ref, got_ref, rows, send_a, recv_a)
    gather.point()
    project_to(3, mixed_ref.at[0], r_ref)
    project_to(4, mixed_ref.at[3], gate_ref)
    save(r_ref, gate_ref)
    for copy in first:
        copy.wait_recv()
    state = start_ref[...]
    fade = fade_ref[pl.ds(pl.multiple_of(lax.rem(me * rows, LANES), rows), rows), :]
    for block in range(grid.seq):
        at = pl.ds(block * rows, rows)
        out_ref[at, :] = state.astype(BF16)
        state = fade * state + got_ref[at, :].astype(F32)
    second = exchange(grid, index, out_ref, begin_ref, rows, send_b, recv_b)
    gather.point()

    later = lax.broadcasted_iota(jnp.int32, (length, length), 0) > lax.broadcasted_iota(
        jnp.int32, (length, length), 1
    )
    for copy in second:
        copy.wait_recv()

    def inside(p, carry):
        down, up, _ = decays(rate_of(p), length)
        pick = half_masks(length)
        begin = begin_ref[columns(p), :].astype(F32)
        for q in range(segments):
            token = pl.ds(q * length, length)
            r = r_ref[token, columns(p)].astype(F32)
            k = k_ref[token, columns(p)].astype(F32)
            v = v_ref[token, columns(p)]
            r_down = r * down
            k_up = k * up
            halves = []
            for h in range(2):
                r_head = jnp.where(pick == (h == 0), r_down, 0.0)
                scores = jnp.where(later, dot3(r_head, k_up, 1, 1, "score"), 0.0)
                halves.append(dot2(scores, v, 1, 0, "inner"))
            inner = jnp.where(pick, halves[0], halves[1])
            self_part = head_sum(r * table_ref[7:8, columns(p)] * k, ones16)
            inner = inner + self_part * v.astype(F32)
            state16 = unfold(begin, q, ones).astype(BF16)
            y = (inner + dot2(r_down, state16, 1, 0, "cross")).astype(BF16)
            wkv_ref[token, columns(p)] = y
            center = y.astype(F32) - dot(y, ones16, 1, 0) * (1.0 / SUBSPACE_EXTENT)
            spread = head_sum(center * center, ones16) * (1.0 / SUBSPACE_EXTENT)
            z = center * lax.rsqrt(spread + 0.00064)
            normalized = z * table_ref[8:9, columns(p)] + table_ref[9:10, columns(p)]
            g = gate_ref[token, columns(p)]
            attended_ref[token, columns(p)] = (normalized * g / (1.0 + jnp.exp(-g))).astype(BF16)
        return carry

    for p in range(pairs):
        lax.fori_loop(p, p + 1, inside, 0)
        gather.point()
    save(wkv_ref, attended_ref)

    await_unit(first_piece(5))

    def out_project(n, carry):
        value = dot(attended_ref[...], weight(5, tile(n)), 1, 0)
        middle_ref[:, tile(n)] = x_ref[:, tile(n)].astype(F32) + value
        return carry

    lax.fori_loop(0, width // 256, out_project, 0)
    save(middle_ref)
    gather.point()
    norm(middle_ref)
    gather.point()
    swap_edges(ffn_entry_ref, 10, 11, 1)

    def mix_two(at, current, previous):
        for c in range(2):
            blend = table_ref[12 + c : 13 + c, :]
            mixed2_ref[c, at, :] = (current * blend + previous * (1.0 - blend)).astype(BF16)

    for q in range(segments):
        shift_rows(q, 10, 11, 1, mix_two)
        gather.point()
    save(mixed2_ref)
    await_unit(first_piece(6))

    def receive(n, carry):
        value = dot(mixed2_ref[1], weight(6, tile(n)), 1, 0)
        recv = 1.0 / (1.0 + jnp.exp(-value))
        recv_ref[:, tile(n)] = recv
        d_carried_ref[:, tile(n)] = (recv * up_ref[:, tile(n)].astype(F32)).astype(BF16)
        return carry

    lax.fori_loop(0, width // 256, receive, 0)
    save(d_carried_ref)
    gather.point()

    for piece in range(starts[7], starts[8]):
        column, size = span(plan[piece])
        await_unit(piece)

        def key(n, carry, column=column):
            window = shifted_tile(column, n)
            value = jnp.maximum(dot(mixed2_ref[0], weight(7, window), 1, 0), 0.0)
            hidden_ref[:, window] = (value * value).astype(BF16)
            return carry

        lax.fori_loop(0, size // 256, key, 0)
        gather.point()
    save(hidden_ref)
    for piece in range(starts[8], len(plan)):
        column, size = span(plan[piece])
        await_unit(piece)
        window = pl.ds(column, size)

        def carry_out(m, carry):
            at = tile(m, 256)
            carried = dot(hidden_ref[at, :], weight(8, window), 1, 0)
            recv = recv_ref[at, window]
            result_ref[at, window] = (middle_ref[at, window] + recv * carried).astype(BF16)
            upstream = up_ref[at, window].astype(F32)
            d_recv_ref[at, window] = (recv * (1.0 - recv) * carried * upstream).astype(BF16)
            return carry

        lax.fori_loop(0, tokens // 256, carry_out, 0)
        gather.point()

    save(d_recv_ref)
    for copy in first + second:
        copy.wait_send()
    gather.close()
    for copy in saved:
        copy.wait()


def forward(grid, x, upstream, att_entry, ffn_entry, start, shards, length):
    tokens, width = x.shape
    steps = [LANES, CHUNK // 2] + [CHUNK] * 6 + [TALL]
    plan, starts = gather_plan([(s.shape[1], step) for s, step in zip(shards, steps)])
    total = sum(len(unit[1]) for unit in plan)
    hidden = shards[7].shape[1]
    vmem = pl.BlockSpec(memory_space=pltpu.VMEM)
    anywhere = pl.BlockSpec(memory_space=pl.ANY)
    flat = jax.ShapeDtypeStruct((tokens, width), BF16)
    state = pltpu.VMEM((width, LANES), BF16)
    sems = pltpu.SemaphoreType.DMA((grid.seq - 1,))
    count = total * sum(size - 1 for size in grid.shape)
    kept = [
        ((4, tokens, width), BF16), ((tokens, width), BF16), ((tokens, width), BF16), ((tokens, width), BF16),
        ((tokens, width), F32), ((tokens, width), BF16), ((tokens, width), BF16), ((tokens, width), F32),
        ((2, tokens, width), BF16), ((tokens, hidden), BF16), ((tokens, width), BF16), ((tokens, width), BF16),
    ]
    return pl.pallas_call(
        functools.partial(forward_kernel, grid, length, plan, starts),
        out_shape=[jax.ShapeDtypeStruct(grid.shape + s.shape, s.dtype) for s in shards]
        + [
            flat, jax.ShapeDtypeStruct((16, width), F32), jax.ShapeDtypeStruct((width, LANES), BF16),
            jax.ShapeDtypeStruct((2, 8, width), F32),
        ]
        + [jax.ShapeDtypeStruct(*entry) for entry in kept],
        in_specs=[vmem] * 5 + [anywhere] * 9,
        out_specs=[anywhere] * 9 + [vmem] * 4 + [anywhere] * len(kept),
        scratch_shapes=[pltpu.VMEM(*entry) for entry in kept]
        + [pltpu.VMEM(grid.shape + s.shape, s.dtype) for s in shards]
        + [
            pltpu.VMEM((tokens, width), F32),
            pltpu.VMEM((8, width), F32),
            pltpu.VMEM((2, 8, width), F32),
            pltpu.VMEM((tokens, width), F32),
            state, state, state,
            pltpu.VMEM((LANES, LANES), F32),
            pltpu.SemaphoreType.DMA((total,)),
            pltpu.SemaphoreType.DMA((count,)),
            pltpu.SemaphoreType.DMA((count,)),
            pltpu.SemaphoreType.DMA((len(plan),)),
            pltpu.SemaphoreType.DMA((len(kept),)),
            pltpu.SemaphoreType.DMA((2,)),
            pltpu.SemaphoreType.DMA((2,)),
            sems, sems, sems, sems,
        ],
        compiler_params=pltpu.CompilerParams(
            collective_id=0, has_side_effects=True, vmem_limit_bytes=VMEM_LIMIT
        ),
    )(x, upstream, att_entry, ffn_entry, start, *shards)


STAGES = ("c", "first", "second", "z")
GAPS = (1, 2, 2, 2)
ALL = (0, 1, 2, 3)
SLOTS = (1, 1, 1, 1)
TICKS = (
    4, 0, 1, 1, 4, 0, 1, 1, 0, 0, 0, 4, 0, 0, 0, 0, 1, 1, 0, 0, 0, 0, 3, 1, 0, 0, 0, 0, 1, 1, 3, 3, 0, 1, 4, 3, 0, 0, 1, 0,
    2, 4, 4, 3, 2, 0, 0, 3,
)


class Piece:
    def __init__(self, array, column, columns, tile, first, kind):
        self.array, self.column, self.columns = array, column, columns
        self.first, self.second = (first, "y" if first == "x" else "x")
        self.tile, self.kind = (tile, columns), kind
        self.group = (tile, columns, first, jnp.dtype(kind).name)


def scatter_plan(arrays):
    units, of_array, counts = [], [], {}
    for array, (tile, columns, step, kind) in enumerate(arrays):
        mine = []
        at = 0
        while at < columns:
            unit = []
            for first in ("x", "y"):
                if at < columns:
                    piece = Piece(array, at, step, tile, first, kind)
                    piece.place = counts.get(piece.group, 0)
                    counts[piece.group] = piece.place + 1
                    unit.append(piece)
                    at += step
            mine.append(len(units))
            units.append(unit)
        of_array.append(mine)
    return units, of_array, counts


def stage_shapes(grid, group):
    tile, columns, first, _ = group
    second = "y" if first == "x" else "x"
    end = (tile, columns)
    return [
        grid.sizes("c") + end,
        (grid.size[first] - 1,) + grid.sizes("c" + first) + end,
        (grid.size[second] - 1,) + grid.sizes("cxy") + end,
        (grid.size["z"] - 1,) + end,
    ]


class Scatter:
    def __init__(self, grid, index, digit, units, keeps, gives, landings, loads, outs, send_sem, recv_sem, load_sem):
        self.grid, self.index, self.digit, self.units = grid, index, digit, units
        self.keeps, self.gives, self.landings, self.loads, self.outs = keeps, gives, landings, loads, outs
        self.send_sem, self.recv_sem, self.load_sem = send_sem, recv_sem, load_sem
        self.started, self.pending, self.giving = [], {}, {}
        self.stage, self.when, self.now, self.reading, self.places = {}, {}, 0, [], 0

    def copy(self, source, target, name, digit):
        slot = len(self.started)
        copy = pltpu.make_async_remote_copy(
            src_ref=source,
            dst_ref=target,
            send_sem=self.send_sem.at[slot],
            recv_sem=self.recv_sem.at[slot],
            device_id=self.grid.peer(self.index, self.digit, name, digit),
            device_id_type=MESH,
        )
        copy.start()
        self.started.append([copy, True])
        return copy

    def open(self, unit, number):
        piece = self.units[unit][number]
        if piece.group in self.giving:
            entry = self.giving.pop(piece.group)
            entry[0].wait_send()
            entry[1] = False
        return self.keeps[unit, number], self.gives[piece.group]

    def give(self, unit):
        for number, piece in enumerate(self.units[unit]):
            target = lax.rem(self.digit["c"] + 1, 2)
            copy = self.copy(self.gives[piece.group], self.landings[piece.group][0].at[piece.place], "c", target)
            self.giving[piece.group] = self.started[-1]
            self.pending[unit, number] = [copy]
        self.stage[unit], self.when[unit] = 0, self.now

    def load(self, unit, number, slot):
        piece, stage = self.units[unit][number], self.stage[unit]
        for copy in self.pending[unit, number]:
            copy.wait_recv()
        copy = pltpu.make_async_copy(
            self.landings[piece.group][stage].at[piece.place],
            self.loads[piece.group][stage].at[slot],
            self.load_sem.at[2 * (sum(SLOTS[:stage]) + slot) + number],
        )
        copy.start()
        return copy

    def add(self, unit, number, slot, copy):
        piece, stage = self.units[unit][number], self.stage[unit]
        keep, got = self.keeps[unit, number], self.loads[piece.group][stage].at[slot]
        names = [n for n in self.grid.order if n != "c"]
        fixed = ((), (piece.first,), (piece.first, piece.second), ("x", "y", "z"))[stage]
        free = [n for n in names if n not in fixed]
        copy.wait()
        terms = 1 if stage == 0 else got.shape[0]
        steps = 1
        for n in free:
            steps *= self.grid.size[n]

        def body(i, carry):
            at, rest = {n: self.digit[n] for n in fixed}, i
            for n in reversed(free):
                at[n] = lax.rem(rest, self.grid.size[n])
                rest = lax.div(rest, self.grid.size[n])
            where, inner = tuple(at[n] for n in names), tuple(at[n] for n in free)
            value = keep[where].astype(F32)
            for j in range(terms):
                value = value + got[inner if stage == 0 else (j,) + inner].astype(F32)
            if stage == 3:
                self.outs[piece.array][:, piece.column : piece.column + piece.columns] = value
            else:
                keep[where] = value.astype(keep.dtype)
            return carry

        if steps == 1:
            body(0, 0)
        else:
            lax.fori_loop(0, steps, body, 0)
        if stage == 3:
            return
        name = (piece.first, piece.second, "z")[stage]
        held = {n: self.digit[n] for n in fixed}
        copies = []
        for j in range(1, self.grid.size[name]):
            target = lax.rem(self.digit[name] + j, self.grid.size[name])
            source = self.grid.at(keep, "c", **held, **{name: target})
            copies.append(self.copy(source, self.landings[piece.group][stage + 1].at[piece.place, j - 1], name, target))
        self.pending[unit, number] = copies

    def finish(self):
        for unit, slot, copies in self.reading:
            for number, copy in enumerate(copies):
                self.add(unit, number, slot, copy)
            self.stage[unit] += 1
            self.when[unit] = self.now
            if self.stage[unit] == 4:
                del self.stage[unit]
        self.reading = []

    def tick(self, stages, gaps=GAPS):
        self.now += 1
        self.finish()
        for stage in stages:
            waiting = [u for u in sorted(self.stage) if self.stage[u] == stage and self.now - self.when[u] >= gaps[stage]]
            for slot, unit in enumerate(waiting[: SLOTS[stage]]):
                copies = [self.load(unit, number, slot) for number in range(len(self.units[unit]))]
                self.reading.append((unit, slot, copies))

    def point(self):
        kind = TICKS[self.places]
        self.places += 1
        for stages in ((), (ALL,), (ALL, ALL), ((0,),), (tuple(n for n in ALL if n),))[kind]:
            self.tick(stages)

    def close(self):
        while self.stage:
            self.tick((0, 1, 2, 3), gaps=(1, 1, 1, 1))
            self.finish()
        for copy, waiting in self.started:
            if waiting:
                copy.wait_send()


def backward_kernel(grid, length, units, of_array, groups, *refs):
    it = iter(refs)

    def take(count):
        return [next(it) for _ in range(count)]

    (table_ref, prev_ref, begin_ref) = take(3)
    (
        x_hbm, up_hbm, mixed_hbm, r_hbm, k_hbm, v_hbm, gate_hbm, wkv_hbm, attended_hbm, middle_hbm, mixed2_hbm,
        hidden_hbm, d_carried_hbm, d_recv_hbm,
    ) = take(14)
    w_k, w_v, w_r, w_g, w_o, f_r, f_k, f_v = take(8)
    (d_input_ref,) = take(1)
    outs = take(len(of_array))
    landings = {group: take(4) for group in groups}
    keeps = {(u, n): next(it) for u, unit in enumerate(units) for n in range(len(unit))}
    gives = {group: next(it) for group in groups}
    loads = {group: take(4) for group in groups}
    (
        hid, dc, dr, m2, dkey, wide, tall, dn, db, mid, nrm, up, dmid, rr, kk, vv, wk, dgate,
        own_ref, got_ref, out_ref, end_ref, fade_ref, acc, edge_ref, arrive_ref,
        send_sem, recv_sem, load_sem, in_sem, wide_sem, edge_send, edge_recv, send_a, recv_a, send_b, recv_b,
    ) = it
    index, digit = grid.place()
    me = index["seq"]
    tokens, width = dc.shape
    segments = tokens // length
    pairs, rows = width // LANES, width // grid.seq
    n0 = grid.shape[0]
    c_at = grid.order.index("c") - 1
    scatter = Scatter(grid, index, digit, units, keeps, gives, landings, loads, outs, send_sem, recv_sem, load_sem)
    batch_roles = [n for n in grid.order if grid.axis[n] == "batch"]
    peers = [
        grid.peer(index, digit, n, lax.rem(digit[n] + j, grid.size[n])) for n in batch_roles for j in range(1, grid.size[n])
    ]
    peers += [(lax.rem(me + j, grid.seq), index["batch"]) for j in range(1, grid.seq)]

    fetched = {}

    def fetch(name, source, target, slot):
        copy = pltpu.make_async_copy(source, target, in_sem.at[slot])
        copy.start()
        fetched[name] = copy

    def have(*names):
        for name in names:
            fetched.pop(name).wait()

    fetch("hid", hidden_hbm, hid, 0)
    fetch("dc", d_carried_hbm, dc, 1)
    fetch("tall", f_v.at[0], tall, 2)
    fetch("m2", mixed2_hbm, m2, 3)
    fetch("dr", d_recv_hbm, dr, 4)
    fetch("mid", middle_hbm, mid, 5)
    fetch("up", up_hbm, up, 6)
    fetch("att", attended_hbm, dgate, 7)
    fetch("rr", r_hbm, rr, 8)
    fetch("kk", k_hbm, kk, 9)
    fetch("vv", v_hbm, vv, 10)
    fetch("wk", wkv_hbm, wk, 11)
    acc[...] = jnp.zeros_like(acc)
    greet(peers)

    everything = (slice(None),) * 5

    def weight_load(array, column, columns, slot):
        copy = pltpu.make_async_copy(
            array.at[everything + (pl.ds(column, columns),)],
            wide.at[(slot,) + everything + (pl.ds(0, columns),)],
            wide_sem.at[slot],
        )
        copy.start()
        return copy

    def weight(slot, columns):
        return wide[(slot,) + everything + (pl.ds(0, columns),)].reshape((-1, columns))

    def tile(n, step):
        return pl.ds(pl.multiple_of(n * step, step), step)

    def gradient(unit, left_ref, right_ref):
        parts = units[unit]
        targets = [scatter.open(unit, number) for number in range(len(parts))]
        span, narrow = left_ref.shape[1] // n0, parts[0].columns < 256
        for batch in [list(range(len(parts)))] if narrow else [[number] for number in range(len(parts))]:
            first = parts[batch[0]]
            width_all = sum(parts[number].columns for number in batch)

            def run(y, carry, batch=batch, first=first, width_all=width_all):
                total = dot(left_ref[:, tile(y, span)], right_ref[:, first.column : first.column + width_all], 0, 0)
                is_zero = digit["c"] == 0
                for number in batch:
                    keep, give = targets[number]
                    at = parts[number].column - first.column
                    value = total[:, at : at + parts[number].columns].reshape(grid.shape[1:] + parts[number].tile)
                    zero = value[(slice(None),) * c_at + (0,)]
                    one = value[(slice(None),) * c_at + (1,)]
                    keep[y] = jnp.where(is_zero, zero, one).astype(keep.dtype)
                    give[y] = jnp.where(is_zero, one, zero).astype(give.dtype)
                return carry

            lax.fori_loop(0, n0, run, 0)
        scatter.give(unit)

    U = dict(zip(("fv", "fr", "fk", "o", "g", "r", "k", "v", "small"), of_array))

    have("hid", "dc")
    for unit in U["fv"]:
        gradient(unit, hid, dc)
        scatter.point()
    span = hid.shape[1] // n0
    loading = weight_load(f_r, 0, width, 0)
    chunks = pieces(hid.shape[1], CHUNK)
    for y in range(n0):
        have("tall")

        def key(m, carry, y=y):
            at = tile(m, 256)
            window = slice(y * span, (y + 1) * span)
            d_hidden = dot(dc[at, :], tall[...].reshape((span, width)), 1, 1)
            dkey[at, window] = (2.0 * jnp.sqrt(hid[at, window].astype(F32)) * d_hidden).astype(BF16)
            return carry

        lax.fori_loop(0, tokens // 256, key, 0)
        if y + 1 < n0:
            fetch("tall", f_v.at[y + 1], tall, 2)
        if y < 2:
            scatter.point()
        if y == 0:
            have("m2", "dr")
            gradient(U["fr"][0], m2.at[1], dr)
            scatter.point()
            loading.wait()
            loading = weight_load(f_k, *chunks[0], 1)

            def through_recv(m, carry):
                at = tile(m, 256)
                db[at, :] = dot(dr[at, :], weight(0, width), 1, 1)
                return carry

            lax.fori_loop(0, tokens // 256, through_recv, 0)
            scatter.point()
    for c in range(3):
        fetch("mx%d" % c, mixed_hbm.at[c], hid.at[:, pl.ds(c * width, width)], c)
    for number, unit in enumerate(U["fk"]):
        gradient(unit, m2.at[0], dkey)
        scatter.point()
        column, columns = chunks[number]
        slot = (number + 1) % 2
        loading.wait()
        if number + 1 < len(chunks):
            loading = weight_load(f_k, *chunks[number + 1], 1 - slot)

        def through_key(m, carry, number=number, column=column, columns=columns, slot=slot):
            at = tile(m, 256)
            value = dot(dkey[at, column : column + columns], weight(slot, columns), 1, 1)
            dn[at, :] = value if number == 0 else dn[at, :] + value
            return carry

        lax.fori_loop(0, tokens // 256, through_key, 0)
        scatter.point()
    fetch("mx3", mixed_hbm.at[3], m2.at[0], 3)
    loading = weight_load(w_o, 0, width, 0)

    step = 64

    def fold_rows(value):
        return jnp.sum(value.reshape((step // 8, 8, width)), axis=0)

    def norm(source_ref, gain, bias):
        def run(i, carry):
            at = tile(i, step)
            value = source_ref[at, :].astype(F32)
            center = value - jnp.mean(value, axis=-1, keepdims=True)
            spread = jnp.mean(center * center, axis=-1, keepdims=True)
            nrm[at, :] = center * lax.rsqrt(spread + 1e-05) * table_ref[gain : gain + 1, :] + table_ref[bias : bias + 1, :]
            return carry

        lax.fori_loop(0, tokens // step, run, 0)

    def swap_edges(slot):
        edge_ref[...] = jnp.zeros_like(edge_ref)
        for q in range(segments):
            edge_ref[q : q + 1, :] = db[q * length : q * length + 8, :][0:1, :]
        copy = pltpu.make_async_remote_copy(
            src_ref=edge_ref,
            dst_ref=arrive_ref.at[slot],
            send_sem=edge_send.at[slot],
            recv_sem=edge_recv.at[slot],
            device_id=(lax.rem(me + grid.seq - 1, grid.seq), index["batch"]),
            device_id_type=MESH,
        )
        copy.start()
        return copy

    def norm_back(source_ref, gain, bias, slot, base_ref, put):
        keep_next = jnp.where(me == grid.seq - 1, 0.0, 1.0)
        for q in range(segments):
            count = length // step

            def run(i, carry, q=q):
                at = tile(q * count + count - 1 - i, step)
                value = source_ref[at, :].astype(F32)
                center = value - jnp.mean(value, axis=-1, keepdims=True)
                spread = jnp.mean(center * center, axis=-1, keepdims=True)
                scale = lax.rsqrt(spread + 1e-05)
                z = center * scale
                before = db[at, :]
                row = lax.broadcasted_iota(jnp.int32, (step, 1), 0)
                d_normed = dn[at, :] + jnp.where(row == step - 1, carry, pltpu.roll(before, step - 1, 0))
                acc[gain] += fold_rows(z * d_normed)
                acc[bias] += fold_rows(d_normed)
                e = d_normed * table_ref[gain : gain + 1, :]
                back = (e - jnp.mean(e, axis=-1, keepdims=True) - z * jnp.mean(e * z, axis=-1, keepdims=True)) * scale
                put(at, base_ref[at, :].astype(F32) + back)
                return before[0:1, :]

            lax.fori_loop(0, count, run, arrive_ref[slot, q : q + 1, :] * keep_next)
            scatter.point()

    have("mid")
    norm(mid, 10, 11)
    scatter.point()

    def blend_two(q, first, last, carry):
        def run(i, carry):
            at = tile(q * (length // step) + i, step)
            current = nrm[at, :]
            row = lax.broadcasted_iota(jnp.int32, (step, 1), 0)
            difference = current - jnp.where(row == 0, carry, pltpu.roll(current, 1, 0))
            here, before = dn[at, :], db[at, :]
            acc[12] += fold_rows(difference * here)
            acc[13] += fold_rows(difference * before)
            a, b = table_ref[12:13, :], table_ref[13:14, :]
            dn[at, :] = here * a + before * b
            db[at, :] = here * (1.0 - a) + before * (1.0 - b)
            return current[step - 1 : step, :]

        return lax.fori_loop(first, last, run, carry)

    above = [blend_two(q, 0, 1, prev_ref[1, q : q + 1, :]) for q in range(segments)]
    moving = swap_edges(0)
    scatter.point()
    for q in range(segments):
        blend_two(q, 1, length // step, above[q])
        scatter.point()
    have("up")
    moving.wait()

    def put_middle(at, value):
        dmid[at, :] = value
        dr[at, :] = value.astype(BF16)

    norm_back(mid, 10, 11, 0, up, put_middle)
    fetch("mid", gate_hbm, mid, 5)
    fetch("up", x_hbm, up, 6)
    have("att")
    gradient(U["o"][0], dgate, dr)
    scatter.point()
    loading.wait()

    def through_out(m, carry):
        at = tile(m, 256)
        nrm[at, :] = dot(dr[at, :], weight(0, width), 1, 1)
        return carry

    lax.fori_loop(0, tokens // 256, through_out, 0)
    scatter.point()

    ones, ones16 = block_ones(F32), block_ones(BF16)
    share = 1.0 / SUBSPACE_EXTENT

    def columns(p, base=0):
        return pl.ds(pl.multiple_of(base + p * LANES, LANES), LANES)

    def rate_of(p):
        return jnp.exp(table_ref[6:7, columns(p)])

    group = lax.div(me * rows, LANES)
    own_log = table_ref[6:7, pl.ds(pl.multiple_of(group * LANES, LANES), LANES)]
    fade_ref[...] = column_of(jnp.exp(-length * jnp.exp(own_log)), length)
    have("wk", "mid", "rr")

    def own_states(p, carry):
        down, _, _ = decays(rate_of(p), length)
        both = []
        gain_sum, bias_sum = jnp.zeros((1, LANES), F32), jnp.zeros((1, LANES), F32)
        for q in range(segments):
            token = pl.ds(q * length, length)
            y = wk[token, columns(p)]
            center = y.astype(F32) - dot(y, ones16, 1, 0) * share
            spread = head_sum(center * center, ones16) * share
            scale = lax.rsqrt(spread + 0.00064)
            z = center * scale
            gain = table_ref[8:9, columns(p)]
            normalized = z * gain + table_ref[9:10, columns(p)]
            g = mid[token, columns(p)]
            s = 1.0 / (1.0 + jnp.exp(-g))
            d_att = nrm[token, columns(p)]
            dgate[token, columns(p)] = (d_att * normalized * s * (1.0 + g * (1.0 - s))).astype(BF16)
            d_norm = d_att * g * s
            gain_sum = gain_sum + jnp.sum(d_norm * z, axis=0, keepdims=True)
            bias_sum = bias_sum + jnp.sum(d_norm, axis=0, keepdims=True)
            e = d_norm * gain
            dy = ((e - head_sum(e, ones16) * share - z * (head_sum(e * z, ones16) * share)) * scale).astype(BF16)
            dc[token, columns(p)] = dy
            both.append(dot2(rr[token, columns(p)].astype(F32) * down, dy, 0, 0, "own"))
        acc[8, 0:1, columns(p)] = gain_sum
        acc[9, 0:1, columns(p)] = bias_sum
        own_ref[columns(p), :] = fold(both[0], both[1], ones).astype(BF16)
        return carry

    for quarter in range(4):
        lax.fori_loop(quarter * pairs // 4, (quarter + 1) * pairs // 4, own_states, 0)
        scatter.point()
    first = exchange(grid, index, own_ref, got_ref, rows, send_a, recv_a)
    have("mx3")
    gradient(U["g"][0], m2.at[0], dgate)
    scatter.point()
    for copy in first:
        copy.wait_recv()
    fade = fade_ref[pl.ds(pl.multiple_of(lax.rem(me * rows, LANES), rows), rows), :]
    state = jnp.zeros_like(fade)
    for block in reversed(range(grid.seq)):
        at = pl.ds(block * rows, rows)
        out_ref[at, :] = state.astype(BF16)
        state = fade * state + got_ref[at, :].astype(F32)
    second = exchange(grid, index, out_ref, end_ref, rows, send_b, recv_b)
    scatter.point()
    have("up")
    norm(up, 0, 1)
    scatter.point()
    have("kk", "vv")
    for copy in second:
        copy.wait_recv()
    later = lax.broadcasted_iota(jnp.int32, (length, length), 0) > lax.broadcasted_iota(
        jnp.int32, (length, length), 1
    )
    time = lax.broadcasted_iota(jnp.int32, (length, LANES), 0).astype(F32)

    def inside(p, carry):
        rate = rate_of(p)
        reward = table_ref[7:8, columns(p)]
        down, up_, end = decays(rate, length)
        pick = half_masks(length)
        begins, ends = begin_ref[columns(p), :].astype(F32), end_ref[columns(p), :].astype(F32)
        reward_sum, rate_sum = jnp.zeros((1, LANES), F32), jnp.zeros((1, LANES), F32)
        for q in range(segments):
            token = pl.ds(q * length, length)
            r = rr[token, columns(p)].astype(F32)
            k = kk[token, columns(p)].astype(F32)
            v = vv[token, columns(p)]
            dy = dc[token, columns(p)]
            begin, finish = unfold(begins, q, ones), unfold(ends, q, ones)
            begin16, finish16 = begin.astype(BF16), finish.astype(BF16)
            r_down = (r * down).astype(BF16)
            k_up = (k * up_).astype(BF16)
            k_end = k * end
            zero = jnp.zeros_like(r_down)
            d_r, d_k, d_v = [], [], []
            for h in range(2):
                here = pick == (h == 0)
                scores = jnp.where(later, dot(jnp.where(here, r_down, zero), k_up, 1, 1), 0.0)
                d_scores = jnp.where(later, dot(jnp.where(here, dy, zero), v, 1, 1), 0.0).astype(BF16)
                d_r.append(dot(d_scores, k_up, 1, 0))
                d_k.append(dot(d_scores, r_down, 0, 0))
                d_v.append(dot2(scores, dy, 0, 0, "inner"))
            from_r = jnp.where(pick, d_r[0], d_r[1]) + dot(dy, begin16, 1, 1)
            from_k = jnp.where(pick, d_k[0], d_k[1])
            from_end = dot(v, finish16, 1, 1)
            v32, dy32 = v.astype(F32), dy.astype(F32)
            v_dy = head_sum(v32 * dy32, ones16)
            self_part = head_sum(r * reward * k, ones16)
            dkey[token, columns(p)] = (from_r * down + reward * k * v_dy).astype(BF16)
            dkey[token, columns(p, width)] = (from_k * up_ + from_end * end + reward * r * v_dy).astype(BF16)
            dkey[token, columns(p, 2 * width)] = (
                jnp.where(pick, d_v[0], d_v[1]) + dot2(k_end, finish16, 1, 0, "cross") + self_part * dy32
            ).astype(BF16)
            reward_sum = reward_sum + jnp.sum(r * k * v_dy, axis=0, keepdims=True)
            terms = (
                (time + 1.0) * k_up.astype(F32) * from_k
                - time * r_down.astype(F32) * from_r
                - (length - 1.0 - time) * k_end * from_end
            )
            through = lax.dot_general(
                jnp.ones((8, LANES), F32), begin * finish, (((1,), (1,)), ((), ())),
                precision=lax.Precision.HIGHEST, preferred_element_type=F32,
            )[0:1, :]
            rate_sum = rate_sum + jnp.sum(terms, axis=0, keepdims=True) - length * jnp.exp(-rate * length) * through
        acc[7, 0:1, columns(p)] = reward_sum
        acc[6, 0:1, columns(p)] = rate_sum * rate
        return carry

    for p in range(pairs):
        lax.fori_loop(p, p + 1, inside, 0)
        scatter.point()
    have("mx0", "mx1", "mx2")
    weights = (w_r, w_k, w_v, w_g)
    grads = [dkey.at[:, pl.ds(c * width, width)] for c in range(3)] + [dgate]

    def load_rows(y):
        copies = []
        for c in range(4):
            copy = pltpu.make_async_copy(weights[c].at[y], wide.at[c // n0, c % n0], in_sem.at[8 + c])
            copy.start()
            copies.append(copy)
        return copies

    loading = load_rows(0)
    for c, name in enumerate("rkv"):
        gradient(U[name][0], hid.at[:, pl.ds(c * width, width)], grads[c])
        scatter.point()
    span = width // n0
    for y in range(n0):
        for copy in loading:
            copy.wait()
        window = slice(y * span, (y + 1) * span)

        def through_mix(m, carry, y=y, window=window):
            at = tile(m, length)
            current = nrm[at, window]
            given = prev_ref[0, 0:1, window]
            for q in range(1, segments):
                given = jnp.where(m == q, prev_ref[0, q : q + 1, window], given)
            row = lax.broadcasted_iota(jnp.int32, (length, 1), 0)
            difference = current - jnp.where(row == 0, given, pltpu.roll(current, 1, 0))
            here, before = None, None
            for c in range(4):
                value = dot(grads[c][at, :], wide[c // n0, c % n0].reshape((span, width)), 1, 1)
                acc[2 + c, :, window] += jnp.sum((difference * value).reshape((length // 8, 8, span)), axis=0)
                blend = table_ref[2 + c : 3 + c, window]
                here = blend * value if c == 0 else here + blend * value
                before = (1.0 - blend) * value if c == 0 else before + (1.0 - blend) * value
            dn[at, window] = here
            db[at, window] = before
            return carry

        lax.fori_loop(0, segments, through_mix, 0)
        if y + 1 < n0:
            loading = load_rows(y + 1)
        if y < 2:
            scatter.point()
    moving = swap_edges(1)
    scatter.point()
    moving.wait()

    def put_input(at, value):
        dr[at, :] = value.astype(BF16)

    norm_back(up, 0, 1, 1, dmid, put_input)
    fetch("result", dr, d_input_ref, 4)

    sums = [jnp.sum(acc[i], axis=0, keepdims=True) for i in range(14)]
    for i in range(14):
        edge_ref[0:1, :] = sums[i]
        nrm[i : i + 1, :] = edge_ref[0:1, :]
    nrm[14:16, :] = jnp.zeros((2, width), F32)
    keep, give = scatter.open(U["small"][0], 0)
    per = grid.seq * grid.batch // pairs
    names = [n for n in grid.order if n != "c"]

    def spread(i, carry):
        at, rest = {}, i
        for n in reversed(names):
            at[n] = lax.rem(rest, grid.size[n])
            rest = lax.div(rest, grid.size[n])
        for target, core in ((keep, digit["c"]), (give, 1 - digit["c"])):
            spot = dict(at, c=core)
            rank = 0
            for n in grid.order:
                rank = rank * grid.size[n] + spot[n]
            target[tuple(at[n] for n in names)] = nrm[0:16, columns(lax.div(rank, per))]
        return carry

    steps = 1
    for n in names:
        steps *= grid.size[n]
    lax.fori_loop(0, steps, spread, 0)
    scatter.give(U["small"][0])
    scatter.point()
    for copy in first + second:
        copy.wait_send()
    scatter.close()
    have("result")


def backward(grid, length, table, prev, begin, stored, weights):
    tokens, width = stored[0].shape
    hidden = stored[11].shape[1]
    blk, tall = weights[0].shape[4], weights[7].shape[4]
    arrays = [
        (tall, width, LANES, BF16), (blk, width, 512, BF16), (blk, hidden, 512, BF16), (blk, width, 512, BF16),
        (blk, width, 512, BF16), (blk, width, 512, BF16), (blk, width, 512, BF16), (blk, width, 512, BF16),
        (16, LANES, LANES, F32),
    ]
    units, of_array, counts = scatter_plan(arrays)
    groups = list(counts)
    kinds = {group: jnp.dtype(group[3]) for group in groups}
    shapes = {group: stage_shapes(grid, group) for group in groups}
    vmem = pl.BlockSpec(memory_space=pltpu.VMEM)
    anywhere = pl.BlockSpec(memory_space=pl.ANY)
    flat16, flat32 = pltpu.VMEM((tokens, width), BF16), pltpu.VMEM((tokens, width), F32)
    state = pltpu.VMEM((width, LANES), BF16)
    sems = pltpu.SemaphoreType.DMA((grid.seq - 1,))
    dma = pltpu.SemaphoreType.DMA
    count = sum(len(unit) for unit in units) * sum(size - 1 for size in grid.shape)
    landing = [
        jax.ShapeDtypeStruct((counts[group],) + shape, kinds[group]) for group in groups for shape in shapes[group]
    ]
    outs = pl.pallas_call(
        functools.partial(backward_kernel, grid, length, units, of_array, groups),
        out_shape=[jax.ShapeDtypeStruct((tokens, width), BF16)]
        + [jax.ShapeDtypeStruct((a[0], a[1]), F32) for a in arrays]
        + landing,
        in_specs=[vmem] * 3 + [anywhere] * 22,
        out_specs=[anywhere] + [vmem] * len(arrays) + [anywhere] * len(landing),
        scratch_shapes=[pltpu.VMEM(grid.sizes("c") + p.tile, p.kind) for unit in units for p in unit]
        + [pltpu.VMEM(shapes[group][0], kinds[group]) for group in groups]
        + [pltpu.VMEM((slots,) + shape, kinds[group]) for group in groups for slots, shape in zip(SLOTS, shapes[group])]
        + [
            pltpu.VMEM((tokens, hidden), BF16), flat16, flat16, pltpu.VMEM((2, tokens, width), BF16),
            pltpu.VMEM((tokens, hidden), BF16),
            pltpu.VMEM((2,) + grid.shape + (blk, CHUNK), BF16),
            pltpu.VMEM(grid.shape[1:] + (tall, width), BF16),
            flat32, flat32, flat32, flat32, flat16, flat32, flat16, flat16, flat16, flat16, flat16,
            state, state, state, state,
            pltpu.VMEM((LANES, LANES), F32),
            pltpu.VMEM((14, 8, width), F32),
            pltpu.VMEM((8, width), F32),
            pltpu.VMEM((2, 8, width), F32),
            dma((count,)), dma((count,)), dma((2 * sum(SLOTS),)), dma((12,)), dma((2,)), dma((2,)), dma((2,)),
            sems, sems, sems, sems,
        ],
        compiler_params=pltpu.CompilerParams(
            collective_id=1, has_side_effects=True, vmem_limit_bytes=VMEM_LIMIT
        ),
    )(table, prev, begin, *stored, *weights)
    return outs[0], outs[1 : 1 + len(arrays)]


def local(grid, *args):
    (
        incoming, att_entry, ffn_entry, memory, upstream,
        ln1_gain, ln1_bias, att_mix, w_recept, w_key, w_value, w_gate, decay_log, reward,
        gn_gain, gn_bias, w_out, ln2_gain, ln2_bias, ffn_mix, f_key, f_value, f_recept,
    ) = args
    segments, length, width = incoming.shape
    tokens = segments * length
    ranks = grid.seq * grid.batch
    share = width // ranks

    per = LANES // share
    rank = lax.axis_index(("seq", "batch"))
    small = jnp.stack(
        [ln1_gain, ln1_bias] + [att_mix[:, c] for c in range(4)] + [decay_log, reward, gn_gain, gn_bias, ln2_gain, ln2_bias]
        + [ffn_mix[:, c] for c in range(2)]
    )
    small = jnp.tile(jnp.pad(small, ((0, 2), (0, 0))), (1, per))
    lane = lax.broadcasted_iota(jnp.int32, small.shape, 1)
    small = jnp.where(lane // share == rank % per, small, jnp.zeros_like(small))
    rows = width // grid.seq
    row = lax.axis_index("seq") * rows
    start = memory.transpose(1, 2, 0, 3).reshape(width, segments * SUBSPACE_EXTENT)
    start = lax.dynamic_slice_in_dim(start, row, rows, 0)
    shards = [small, w_key, w_value, w_recept, w_gate, w_out, f_recept, f_key, f_value]
    outs = forward(
        grid, incoming.reshape(tokens, width), upstream.reshape(tokens, width), att_entry, ffn_entry, start, shards, length
    )
    (
        result, table, begin, prev, mixed, r, k, v, gate_pre, wkv, attended, middle, mixed2, hidden, d_carried, d_recv,
    ) = outs[9:]
    stored = [
        incoming.reshape(tokens, width), upstream.reshape(tokens, width), mixed, r, k, v, gate_pre, wkv, attended, middle,
        mixed2, hidden, d_carried, d_recv,
    ]
    d_input, (s_fv, s_fr, s_fk, s_o, s_g, s_r, s_k, s_v, s_small) = backward(
        grid, length, table, prev, begin, stored, outs[1:9]
    )
    s = lax.dynamic_slice_in_dim(s_small, (rank % per) * share, share, 1)
    shape = incoming.shape
    return (
        result.reshape(shape), d_input.reshape(shape),
        s[0], s[1], s[2:6].T, s_r, s_k, s_v, s_g, s[6], s[7], s[8], s[9], s_o, s[10], s[11], s[12:14].T,
        s_fk, s_fv, s_fr,
    )


def solution(mesh):
    grid = Grid(mesh.shape["seq"], mesh.shape["batch"])
    both, rows = P(("seq", "batch")), P(("seq", "batch"), None)
    tokens, entry = P("batch", "seq", None), P("batch", None)
    return jax.shard_map(
        functools.partial(local, grid),
        mesh=mesh,
        in_specs=(
            tokens, entry, entry, P("batch", None, None, None), tokens,
            both, both, rows, rows, rows, rows, rows, both, both, both, both, rows, both, both, rows, rows, rows, rows,
        ),
        out_specs=(
            tokens, tokens, both, both, rows, rows, rows, rows, rows, both, both, both, both, rows, both, both, rows,
            rows, rows, rows,
        ),
        check_vma=False,
    )
```

```python
import functools

import jax
import jax.numpy as jnp
from jax import lax
from jax.experimental import pallas as pl
from jax.experimental.pallas import tpu as pltpu
from jax.sharding import PartitionSpec as P

WKV_PARTITIONS = 16
SUBSPACE_EXTENT = 64
LANES = 128
MESH = pl.DeviceIdType.MESH
F32 = jnp.float32
BF16 = jnp.bfloat16
VMEM_LIMIT = 63 * 1024 * 1024


class Grid:
    def __init__(self, seq, batch):
        self.seq, self.batch = seq, batch
        if seq == 8 and batch == 4:
            digits = [("y", "seq", 4, 2), ("x", "seq", 2, 2), ("c", "seq", 1, 2), ("z", "batch", 1, 4)]
        elif seq == 16 and batch == 8:
            digits = [("y", "seq", 4, 4), ("x", "seq", 1, 4), ("z", "batch", 2, 4), ("c", "batch", 1, 2)]
        else:
            raise ValueError("unknown mesh")
        self.order = [name for name, *_ in digits]
        self.axis = {name: axis for name, axis, *_ in digits}
        self.stride = {name: stride for name, _, stride, _ in digits}
        self.size = {name: size for name, *_, size in digits}
        self.shape = tuple(self.size[name] for name in self.order)

    def place(self):
        index = {"seq": lax.axis_index("seq"), "batch": lax.axis_index("batch")}
        return index, {
            name: (index[self.axis[name]] // self.stride[name]) % self.size[name] for name in self.order
        }

    def peer(self, index, digit, name, target):
        where = dict(index)
        axis = self.axis[name]
        where[axis] = index[axis] + (target - digit[name]) * self.stride[name]
        return (where["seq"], where["batch"])

    def at(self, ref, gone="", **fixed):
        return ref.at[tuple(fixed.get(name, slice(None)) for name in self.order if name not in gone)]

    def sizes(self, gone=""):
        return tuple(self.size[name] for name in self.order if name not in gone)


def greet(peers):
    barrier = pltpu.get_barrier_semaphore()
    for peer in peers:
        pl.semaphore_signal(barrier, inc=1, device_id=peer, device_id_type=MESH)
    pl.semaphore_wait(barrier, len(peers))


def dot(a, b, da, db):
    return lax.dot_general(a, b, (((da,), (db,)), ((), ())), preferred_element_type=F32)


PRECISE = dict(score=0, inner=1, cross=1, own=1, back=0)


def parts_of(value):
    high = value.astype(BF16)
    return high, (value - high.astype(F32)).astype(BF16)


def dot2(a, b, da, db, name):
    if not PRECISE[name]:
        return dot(a.astype(BF16), b, da, db)
    high, low = parts_of(a)
    return dot(high, b, da, db) + dot(low, b, da, db)


def dot3(a, b, da, db, name):
    if not PRECISE[name]:
        return dot(a.astype(BF16), b.astype(BF16), da, db)
    a_high, a_low = parts_of(a)
    b_high, b_low = parts_of(b)
    return dot(a_high, b_high, da, db) + (dot(a_low, b_high, da, db) + dot(a_high, b_low, da, db))


def half_masks(rows):
    lane = lax.broadcasted_iota(jnp.int32, (rows, LANES), 1)
    return lane < SUBSPACE_EXTENT


def block_ones(kind):
    row = lax.broadcasted_iota(jnp.int32, (LANES, LANES), 0) // SUBSPACE_EXTENT
    lane = lax.broadcasted_iota(jnp.int32, (LANES, LANES), 1) // SUBSPACE_EXTENT
    return (row == lane).astype(kind)


def head_sum(value, ones):
    high = value.astype(BF16)
    low = (value - high.astype(F32)).astype(BF16)
    return dot(high, ones, 1, 0) + dot(low, ones, 1, 0)


def decays(rate, length):
    step = lax.broadcasted_iota(jnp.int32, (length, LANES), 0).astype(F32)
    return jnp.exp(-rate * step), jnp.exp(rate * (step + 1.0)), jnp.exp(-rate * (length - 1.0 - step))


def fold(first, second, ones):
    pick = half_masks(LANES)
    a, b = first * ones, second * ones
    a = a + pltpu.roll(a, SUBSPACE_EXTENT, 1)
    b = b + pltpu.roll(b, SUBSPACE_EXTENT, 1)
    return jnp.where(pick, a, b)


def unfold(both, segment, ones):
    pick = half_masks(LANES)
    turned = pltpu.roll(both, SUBSPACE_EXTENT, 1)
    full = jnp.where(pick, both, turned) if segment == 0 else jnp.where(pick, turned, both)
    return full * ones


def exchange(grid, index, source, slots, rows, send_sem, recv_sem):
    me, copies = index["seq"], []
    for j in range(1, grid.seq):
        target = lax.rem(me + j, grid.seq)
        copy = pltpu.make_async_remote_copy(
            src_ref=source.at[pl.ds(pl.multiple_of(target * rows, 16), rows)],
            dst_ref=slots.at[pl.ds(pl.multiple_of(me * rows, 16), rows)],
            send_sem=send_sem.at[j - 1],
            recv_sem=recv_sem.at[j - 1],
            device_id=(target, index["batch"]),
            device_id_type=MESH,
        )
        copy.start()
        copies.append(copy)
    here = pl.ds(pl.multiple_of(me * rows, 16), rows)
    slots[here, :] = source[here, :]
    return copies


CHUNK = 1024
TALL = 256
LAGS = (0, 1, 3)
AHEAD = 4
PUMPS = (
    0, 0, 1, 0, 0, 0, 2, 0, 0, 0, 0, 0, 1, 0, 0, 0, 0, 1, 0, 1, 0, 0, 1, 0, 0, 0, 0, 1, 1, 0, 0, 0, 1, 0, 1, 1, 0, 0, 0, 0,
    1, 0, 0, 0, 1, 0, 0, 0, 0, 0,
)


def pieces(columns, step):
    return [(at, min(step, columns - at)) for at in range(0, columns, step)]


class Gather:
    def __init__(self, grid, index, digit, shards, fulls, plan, own_sem, send_sem, recv_sem):
        self.grid, self.index, self.digit = grid, index, digit
        self.shards, self.fulls, self.plan = shards, fulls, plan
        self.own_sem, self.send_sem, self.recv_sem = own_sem, send_sem, recv_sem
        self.started, self.pending, self.own = [], {}, {}
        self.tick, self.done, self.places = 0, 0, 0

    def others(self, name):
        size = self.grid.size[name]
        return [lax.rem(self.digit[name] + j, size) for j in range(1, size)]

    def send(self, source, place, name):
        copies = []
        for target in self.others(name):
            slot = len(self.started)
            copy = pltpu.make_async_remote_copy(
                src_ref=source,
                dst_ref=place,
                send_sem=self.send_sem.at[slot],
                recv_sem=self.recv_sem.at[slot],
                device_id=self.grid.peer(self.index, self.digit, name, target),
                device_id_type=MESH,
            )
            copy.start()
            self.started.append(copy)
            copies.append(copy)
        return copies

    def stage(self, unit, number):
        if not 0 <= unit < len(self.plan):
            return
        for piece in range(len(self.plan[unit][1])):
            self.step(unit, piece, number)

    def step(self, unit, piece, number):
        array, parts = self.plan[unit]
        column, columns, first, second = parts[piece]
        digit = self.digit
        window = pl.ds(column, columns)
        full = self.fulls[array]
        key = (unit, piece)

        def at(**fixed):
            place = tuple(fixed.get(name, slice(None)) for name in self.grid.order)
            return full.at[place + (slice(None), window)]

        if number == 0:
            place = at(**digit)
            source = self.shards[array].at[:, window]
            copy = pltpu.make_async_copy(source, place, self.own_sem.at[len(self.own)])
            copy.start()
            self.own[key] = copy
            self.pending[key] = self.send(source, place, "z")
            return
        for copy in self.pending[key]:
            copy.wait_recv()
        if number == 1:
            self.own[key].wait()
            fixed, name = {n: digit[n] for n in ("x", "y", "c")}, first
        elif number == 2:
            fixed, name = {n: digit[n] for n in (second, "c")}, second
        elif number == 3:
            fixed, name = {"c": digit["c"]}, "c"
        else:
            self.pending[key] = []
            return
        place = at(**fixed)
        self.pending[key] = self.send(place, place, name)

    def open(self, ahead):
        self.ahead = ahead
        for piece in range(ahead):
            self.stage(piece, 0)

    def pump(self, count=1):
        for _ in range(count):
            tick = self.tick
            self.tick += 1
            for number in (1, 2, 3):
                self.stage(tick - LAGS[number - 1], number)
            self.stage(tick + self.ahead, 0)

    def point(self):
        count = PUMPS[self.places]
        self.places += 1
        self.pump(count if self.tick < len(self.plan) + LAGS[2] + 1 else 0)

    def ready(self, piece):
        while self.tick < piece + LAGS[2] + 1:
            self.pump()
        while self.done <= piece:
            self.stage(self.done, 4)
            self.done += 1

    def close(self):
        for copy in self.started:
            copy.wait_send()


def gather_plan(arrays):
    plan, starts = [], []
    for array, (columns, step) in enumerate(arrays):
        starts.append(len(plan))
        for column, size in pieces(columns, step):
            half = size // 2
            if half % LANES:
                plan.append((array, [(column, size, "x", "y")]))
            else:
                plan.append((array, [(column, half, "x", "y"), (column + half, half, "y", "x")]))
    return plan, starts


def span(unit):
    return unit[1][0][0], sum(part[1] for part in unit[1])


def column_of(row, length):
    at = lax.broadcasted_iota(jnp.int32, (LANES, LANES), 0)
    lane = lax.broadcasted_iota(jnp.int32, (LANES, LANES), 1)
    spread = jnp.where(at == lane, jnp.broadcast_to(row, (LANES, LANES)), 0.0)
    return jnp.broadcast_to(jnp.sum(spread, axis=1, keepdims=True), (LANES, LANES))


def forward_kernel(grid, length, plan, starts, *refs):
    (
        x_ref, up_ref, att_entry_ref, ffn_entry_ref, start_ref, *shards
    ) = refs[:14]
    stored = refs[14:23]
    result_ref, table_ref, begin_ref, prev_ref = refs[23:27]
    kept = refs[27:39]
    (
        mixed_ref, r_ref, k_ref, v_ref, gate_ref, wkv_ref, attended_ref, middle_ref, mixed2_ref, hidden_ref,
        d_carried_ref, d_recv_ref,
    ) = places = refs[39:51]
    (
        normed_ref, edge_ref, arrive_ref, recv_ref,
        own_ref, got_ref, out_ref, fade_ref,
        own_sem, send_sem, recv_sem, store_sem, save_sem, edge_send, edge_recv, send_a, recv_a, send_b, recv_b,
    ) = refs[60:]
    fulls = refs[51:60]
    saved = []

    def save(*names):
        for name in names:
            at = [place is name for place in places].index(True)
            copy = pltpu.make_async_copy(name, kept[at], save_sem.at[at])
            copy.start()
            saved.append(copy)

    index, digit = grid.place()
    me = index["seq"]
    tokens, width = x_ref.shape
    segments = tokens // length
    pairs, rows = width // LANES, width // grid.seq
    batch_roles = [n for n in grid.order if grid.axis[n] == "batch"]
    gather = Gather(grid, index, digit, shards, fulls, plan, own_sem, send_sem, recv_sem)
    peers = [grid.peer(index, digit, n, t) for n in batch_roles for t in gather.others(n)]
    peers += [(lax.rem(me + j, grid.seq), index["batch"]) for j in range(1, grid.seq)]
    greet(peers)
    gather.open(AHEAD)
    gather.point()

    def first_piece(array):
        return starts[array]

    def await_unit(unit):
        gather.ready(unit)
        array = plan[unit][0]
        column, columns = span(plan[unit])
        window = (slice(None),) * 5 + (pl.ds(column, columns),)
        copy = pltpu.make_async_copy(fulls[array].at[window], stored[array].at[window], store_sem.at[unit])
        copy.start()
        saved.append(copy)
        gather.point()

    def weight(array, window):
        value = fulls[array][(slice(None),) * 5 + (window,)]
        return value.reshape((-1, value.shape[-1]))

    def tile(n, step=256):
        return pl.ds(pl.multiple_of(n * step, step), step)

    def norm(source_ref):
        step = 64

        def run(i, carry):
            at = pl.ds(pl.multiple_of(i * step, step), step)
            value = source_ref[at, :].astype(F32)
            center = value - jnp.mean(value, axis=-1, keepdims=True)
            spread = jnp.mean(center * center, axis=-1, keepdims=True)
            normed_ref[at, :] = center * lax.rsqrt(spread + 1e-05)
            return carry

        lax.fori_loop(0, tokens // step, run, 0)

    norm(x_ref)
    gather.point()

    gather.ready(0)
    ranks = grid.seq * grid.batch
    small = fulls[0][...].astype(F32).reshape((ranks, 16, LANES))
    per = ranks // pairs
    for p in range(pairs):
        total = small[p * per]
        for j in range(1, per):
            total = total + small[p * per + j]
        table_ref[:, p * LANES : (p + 1) * LANES] = total
    gather.point()

    def shift_rows(segment, gain, bias, slot, body):
        step = 64

        def run(i, carry):
            at = pl.ds(pl.multiple_of(segment * length + i * step, step), step)
            current = normed_ref[at, :] * table_ref[gain : gain + 1, :] + table_ref[bias : bias + 1, :]
            row = lax.broadcasted_iota(jnp.int32, (step, 1), 0)
            previous = jnp.where(row == 0, carry, pltpu.roll(current, 1, 0))
            body(at, current, previous)
            return current[step - 1 : step, :]

        lax.fori_loop(0, length // step, run, prev_ref[slot, segment : segment + 1, :])

    def swap_edges(entry_ref, gain, bias, slot):
        edge_ref[...] = jnp.zeros_like(edge_ref)
        for q in range(segments):
            last = (q + 1) * length
            row = normed_ref[last - 8 : last, :][7:8, :]
            edge_ref[q : q + 1, :] = row * table_ref[gain : gain + 1, :] + table_ref[bias : bias + 1, :]
        copy = pltpu.make_async_remote_copy(
            src_ref=edge_ref,
            dst_ref=arrive_ref.at[slot],
            send_sem=edge_send.at[slot],
            recv_sem=edge_recv.at[slot],
            device_id=(lax.rem(me + 1, grid.seq), index["batch"]),
            device_id_type=MESH,
        )
        copy.start()
        gather.point()
        copy.wait()
        first = jnp.where(me == 0, 1.0, 0.0)
        prev_ref[slot] = arrive_ref[slot] * (1.0 - first)
        prev_ref[slot, 0:segments, :] += entry_ref[...].astype(F32) * first

    swap_edges(att_entry_ref, 0, 1, 0)

    def mix_one(at, current, previous):
        for c in range(4):
            blend = table_ref[2 + c : 3 + c, :]
            mixed_ref[c, at, :] = (current * blend + previous * (1.0 - blend)).astype(BF16)

    for q in range(segments):
        shift_rows(q, 0, 1, 0, mix_one)
        gather.point()
    save(mixed_ref)

    def shifted_tile(column, n):
        return pl.ds(pl.multiple_of(column + n * 256, 256), 256)

    def project_to(array, left, target_ref):
        for unit in range(starts[array], starts[array + 1]):
            await_unit(unit)
            column, size = span(plan[unit])

            def run(n, carry, column=column):
                window = shifted_tile(column, n)
                target_ref[:, window] = dot(left[...], weight(array, window), 1, 0).astype(target_ref.dtype)
                return carry

            lax.fori_loop(0, size // 256, run, 0)
            gather.point()

    project_to(1, mixed_ref.at[1], k_ref)
    project_to(2, mixed_ref.at[2], v_ref)
    save(k_ref, v_ref)
    ones, ones16 = block_ones(F32), block_ones(BF16)
    group = lax.div(me * rows, LANES)
    own_log = table_ref[6:7, pl.ds(pl.multiple_of(group * LANES, LANES), LANES)]
    fade_ref[...] = column_of(jnp.exp(-length * jnp.exp(own_log)), length)

    def columns(p):
        return pl.ds(pl.multiple_of(p * LANES, LANES), LANES)

    def rate_of(p):
        return jnp.exp(table_ref[6:7, columns(p)])

    def own_states(p, carry):
        _, _, end = decays(rate_of(p), length)
        both = []
        for q in range(segments):
            token = pl.ds(q * length, length)
            k_end = k_ref[token, columns(p)].astype(F32) * end
            both.append(dot2(k_end, v_ref[token, columns(p)], 0, 0, "own"))
        own_ref[columns(p), :] = fold(both[0], both[1], ones).astype(BF16)
        return carry

    lax.fori_loop(0, pairs, own_states, 0)
    first = exchange(grid, index, own_ref, got_ref, rows, send_a, recv_a)
    gather.point()
    project_to(3, mixed_ref.at[0], r_ref)
    project_to(4, mixed_ref.at[3], gate_ref)
    save(r_ref, gate_ref)
    for copy in first:
        copy.wait_recv()
    state = start_ref[...]
    fade = fade_ref[pl.ds(pl.multiple_of(lax.rem(me * rows, LANES), rows), rows), :]
    for block in range(grid.seq):
        at = pl.ds(block * rows, rows)
        out_ref[at, :] = state.astype(BF16)
        state = fade * state + got_ref[at, :].astype(F32)
    second = exchange(grid, index, out_ref, begin_ref, rows, send_b, recv_b)
    gather.point()

    later = lax.broadcasted_iota(jnp.int32, (length, length), 0) > lax.broadcasted_iota(
        jnp.int32, (length, length), 1
    )
    for copy in second:
        copy.wait_recv()

    def inside(p, carry):
        down, up, _ = decays(rate_of(p), length)
        pick = half_masks(length)
        begin = begin_ref[columns(p), :].astype(F32)
        for q in range(segments):
            token = pl.ds(q * length, length)
            r = r_ref[token, columns(p)].astype(F32)
            k = k_ref[token, columns(p)].astype(F32)
            v = v_ref[token, columns(p)]
            r_down = r * down
            k_up = k * up
            halves = []
            for h in range(2):
                r_head = jnp.where(pick == (h == 0), r_down, 0.0)
                scores = jnp.where(later, dot3(r_head, k_up, 1, 1, "score"), 0.0)
                halves.append(dot2(scores, v, 1, 0, "inner"))
            inner = jnp.where(pick, halves[0], halves[1])
            self_part = head_sum(r * table_ref[7:8, columns(p)] * k, ones16)
            inner = inner + self_part * v.astype(F32)
            state16 = unfold(begin, q, ones).astype(BF16)
            y = (inner + dot2(r_down, state16, 1, 0, "cross")).astype(BF16)
            wkv_ref[token, columns(p)] = y
            center = y.astype(F32) - dot(y, ones16, 1, 0) * (1.0 / SUBSPACE_EXTENT)
            spread = head_sum(center * center, ones16) * (1.0 / SUBSPACE_EXTENT)
            z = center * lax.rsqrt(spread + 0.00064)
            normalized = z * table_ref[8:9, columns(p)] + table_ref[9:10, columns(p)]
            g = gate_ref[token, columns(p)]
            attended_ref[token, columns(p)] = (normalized * g / (1.0 + jnp.exp(-g))).astype(BF16)
        return carry

    for p in range(pairs):
        lax.fori_loop(p, p + 1, inside, 0)
        gather.point()
    save(wkv_ref, attended_ref)

    await_unit(first_piece(5))

    def out_project(n, carry):
        value = dot(attended_ref[...], weight(5, tile(n)), 1, 0)
        middle_ref[:, tile(n)] = x_ref[:, tile(n)].astype(F32) + value
        return carry

    lax.fori_loop(0, width // 256, out_project, 0)
    save(middle_ref)
    gather.point()
    norm(middle_ref)
    gather.point()
    swap_edges(ffn_entry_ref, 10, 11, 1)

    def mix_two(at, current, previous):
        for c in range(2):
            blend = table_ref[12 + c : 13 + c, :]
            mixed2_ref[c, at, :] = (current * blend + previous * (1.0 - blend)).astype(BF16)

    for q in range(segments):
        shift_rows(q, 10, 11, 1, mix_two)
        gather.point()
    save(mixed2_ref)
    await_unit(first_piece(6))

    def receive(n, carry):
        value = dot(mixed2_ref[1], weight(6, tile(n)), 1, 0)
        recv = 1.0 / (1.0 + jnp.exp(-value))
        recv_ref[:, tile(n)] = recv
        d_carried_ref[:, tile(n)] = (recv * up_ref[:, tile(n)].astype(F32)).astype(BF16)
        return carry

    lax.fori_loop(0, width // 256, receive, 0)
    save(d_carried_ref)
    gather.point()

    for piece in range(starts[7], starts[8]):
        column, size = span(plan[piece])
        await_unit(piece)

        def key(n, carry, column=column):
            window = shifted_tile(column, n)
            value = jnp.maximum(dot(mixed2_ref[0], weight(7, window), 1, 0), 0.0)
            hidden_ref[:, window] = (value * value).astype(BF16)
            return carry

        lax.fori_loop(0, size // 256, key, 0)
        gather.point()
    save(hidden_ref)
    for piece in range(starts[8], len(plan)):
        column, size = span(plan[piece])
        await_unit(piece)
        window = pl.ds(column, size)

        def carry_out(m, carry):
            at = tile(m, 256)
            carried = dot(hidden_ref[at, :], weight(8, window), 1, 0)
            recv = recv_ref[at, window]
            result_ref[at, window] = (middle_ref[at, window] + recv * carried).astype(BF16)
            upstream = up_ref[at, window].astype(F32)
            d_recv_ref[at, window] = (recv * (1.0 - recv) * carried * upstream).astype(BF16)
            return carry

        lax.fori_loop(0, tokens // 256, carry_out, 0)
        gather.point()

    save(d_recv_ref)
    for copy in first + second:
        copy.wait_send()
    gather.close()
    for copy in saved:
        copy.wait()


def forward(grid, x, upstream, att_entry, ffn_entry, start, shards, length):
    tokens, width = x.shape
    steps = [LANES, CHUNK // 2] + [CHUNK] * 6 + [TALL]
    plan, starts = gather_plan([(s.shape[1], step) for s, step in zip(shards, steps)])
    total = sum(len(unit[1]) for unit in plan)
    hidden = shards[7].shape[1]
    vmem = pl.BlockSpec(memory_space=pltpu.VMEM)
    anywhere = pl.BlockSpec(memory_space=pl.ANY)
    flat = jax.ShapeDtypeStruct((tokens, width), BF16)
    state = pltpu.VMEM((width, LANES), BF16)
    sems = pltpu.SemaphoreType.DMA((grid.seq - 1,))
    count = total * sum(size - 1 for size in grid.shape)
    kept = [
        ((4, tokens, width), BF16), ((tokens, width), BF16), ((tokens, width), BF16), ((tokens, width), BF16),
        ((tokens, width), F32), ((tokens, width), BF16), ((tokens, width), BF16), ((tokens, width), F32),
        ((2, tokens, width), BF16), ((tokens, hidden), BF16), ((tokens, width), BF16), ((tokens, width), BF16),
    ]
    return pl.pallas_call(
        functools.partial(forward_kernel, grid, length, plan, starts),
        out_shape=[jax.ShapeDtypeStruct(grid.shape + s.shape, s.dtype) for s in shards]
        + [
            flat, jax.ShapeDtypeStruct((16, width), F32), jax.ShapeDtypeStruct((width, LANES), BF16),
            jax.ShapeDtypeStruct((2, 8, width), F32),
        ]
        + [jax.ShapeDtypeStruct(*entry) for entry in kept],
        in_specs=[vmem] * 5 + [anywhere] * 9,
        out_specs=[anywhere] * 9 + [vmem] * 4 + [anywhere] * len(kept),
        scratch_shapes=[pltpu.VMEM(*entry) for entry in kept]
        + [pltpu.VMEM(grid.shape + s.shape, s.dtype) for s in shards]
        + [
            pltpu.VMEM((tokens, width), F32),
            pltpu.VMEM((8, width), F32),
            pltpu.VMEM((2, 8, width), F32),
            pltpu.VMEM((tokens, width), F32),
            state, state, state,
            pltpu.VMEM((LANES, LANES), F32),
            pltpu.SemaphoreType.DMA((total,)),
            pltpu.SemaphoreType.DMA((count,)),
            pltpu.SemaphoreType.DMA((count,)),
            pltpu.SemaphoreType.DMA((len(plan),)),
            pltpu.SemaphoreType.DMA((len(kept),)),
            pltpu.SemaphoreType.DMA((2,)),
            pltpu.SemaphoreType.DMA((2,)),
            sems, sems, sems, sems,
        ],
        compiler_params=pltpu.CompilerParams(
            collective_id=0, has_side_effects=True, vmem_limit_bytes=VMEM_LIMIT
        ),
    )(x, upstream, att_entry, ffn_entry, start, *shards)


STAGES = ("c", "first", "second", "z")
GAPS = (1, 2, 2, 2)
ALL = (0, 1, 2, 3)
SLOTS = (1, 1, 1, 1)
TICKS = (
    4, 0, 1, 1, 4, 0, 1, 1, 0, 0, 0, 4, 0, 0, 0, 0, 1, 1, 0, 0, 0, 0, 3, 1, 0, 0, 0, 0, 1, 1, 3, 3, 0, 1, 4, 3, 0, 0, 1, 0,
    2, 4, 4, 3, 2, 0, 0, 3,
)


class Piece:
    def __init__(self, array, column, columns, tile, first, kind):
        self.array, self.column, self.columns = array, column, columns
        self.first, self.second = (first, "y" if first == "x" else "x")
        self.tile, self.kind = (tile, columns), kind
        self.group = (tile, columns, first, jnp.dtype(kind).name)


def scatter_plan(arrays):
    units, of_array, counts = [], [], {}
    for array, (tile, columns, step, kind) in enumerate(arrays):
        mine = []
        at = 0
        while at < columns:
            unit = []
            for first in ("x", "y"):
                if at < columns:
                    piece = Piece(array, at, step, tile, first, kind)
                    piece.place = counts.get(piece.group, 0)
                    counts[piece.group] = piece.place + 1
                    unit.append(piece)
                    at += step
            mine.append(len(units))
            units.append(unit)
        of_array.append(mine)
    return units, of_array, counts


def stage_shapes(grid, group):
    tile, columns, first, _ = group
    second = "y" if first == "x" else "x"
    end = (tile, columns)
    return [
        grid.sizes("c") + end,
        (grid.size[first] - 1,) + grid.sizes("c" + first) + end,
        (grid.size[second] - 1,) + grid.sizes("cxy") + end,
        (grid.size["z"] - 1,) + end,
    ]


class Scatter:
    def __init__(self, grid, index, digit, units, keeps, gives, landings, loads, outs, send_sem, recv_sem, load_sem):
        self.grid, self.index, self.digit, self.units = grid, index, digit, units
        self.keeps, self.gives, self.landings, self.loads, self.outs = keeps, gives, landings, loads, outs
        self.send_sem, self.recv_sem, self.load_sem = send_sem, recv_sem, load_sem
        self.started, self.pending, self.giving = [], {}, {}
        self.stage, self.when, self.now, self.reading, self.places = {}, {}, 0, [], 0

    def copy(self, source, target, name, digit):
        slot = len(self.started)
        copy = pltpu.make_async_remote_copy(
            src_ref=source,
            dst_ref=target,
            send_sem=self.send_sem.at[slot],
            recv_sem=self.recv_sem.at[slot],
            device_id=self.grid.peer(self.index, self.digit, name, digit),
            device_id_type=MESH,
        )
        copy.start()
        self.started.append([copy, True])
        return copy

    def open(self, unit, number):
        piece = self.units[unit][number]
        if piece.group in self.giving:
            entry = self.giving.pop(piece.group)
            entry[0].wait_send()
            entry[1] = False
        return self.keeps[unit, number], self.gives[piece.group]

    def give(self, unit):
        for number, piece in enumerate(self.units[unit]):
            target = lax.rem(self.digit["c"] + 1, 2)
            copy = self.copy(self.gives[piece.group], self.landings[piece.group][0].at[piece.place], "c", target)
            self.giving[piece.group] = self.started[-1]
            self.pending[unit, number] = [copy]
        self.stage[unit], self.when[unit] = 0, self.now

    def load(self, unit, number, slot):
        piece, stage = self.units[unit][number], self.stage[unit]
        for copy in self.pending[unit, number]:
            copy.wait_recv()
        copy = pltpu.make_async_copy(
            self.landings[piece.group][stage].at[piece.place],
            self.loads[piece.group][stage].at[slot],
            self.load_sem.at[2 * (sum(SLOTS[:stage]) + slot) + number],
        )
        copy.start()
        return copy

    def add(self, unit, number, slot, copy):
        piece, stage = self.units[unit][number], self.stage[unit]
        keep, got = self.keeps[unit, number], self.loads[piece.group][stage].at[slot]
        names = [n for n in self.grid.order if n != "c"]
        fixed = ((), (piece.first,), (piece.first, piece.second), ("x", "y", "z"))[stage]
        free = [n for n in names if n not in fixed]
        copy.wait()
        terms = 1 if stage == 0 else got.shape[0]
        steps = 1
        for n in free:
            steps *= self.grid.size[n]

        def body(i, carry):
            at, rest = {n: self.digit[n] for n in fixed}, i
            for n in reversed(free):
                at[n] = lax.rem(rest, self.grid.size[n])
                rest = lax.div(rest, self.grid.size[n])
            where, inner = tuple(at[n] for n in names), tuple(at[n] for n in free)
            value = keep[where].astype(F32)
            for j in range(terms):
                value = value + got[inner if stage == 0 else (j,) + inner].astype(F32)
            if stage == 3:
                self.outs[piece.array][:, piece.column : piece.column + piece.columns] = value
            else:
                keep[where] = value.astype(keep.dtype)
            return carry

        if steps == 1:
            body(0, 0)
        else:
            lax.fori_loop(0, steps, body, 0)
        if stage == 3:
            return
        name = (piece.first, piece.second, "z")[stage]
        held = {n: self.digit[n] for n in fixed}
        copies = []
        for j in range(1, self.grid.size[name]):
            target = lax.rem(self.digit[name] + j, self.grid.size[name])
            source = self.grid.at(keep, "c", **held, **{name: target})
            copies.append(self.copy(source, self.landings[piece.group][stage + 1].at[piece.place, j - 1], name, target))
        self.pending[unit, number] = copies

    def finish(self):
        for unit, slot, copies in self.reading:
            for number, copy in enumerate(copies):
                self.add(unit, number, slot, copy)
            self.stage[unit] += 1
            self.when[unit] = self.now
            if self.stage[unit] == 4:
                del self.stage[unit]
        self.reading = []

    def tick(self, stages, gaps=GAPS):
        self.now += 1
        self.finish()
        for stage in stages:
            waiting = [u for u in sorted(self.stage) if self.stage[u] == stage and self.now - self.when[u] >= gaps[stage]]
            for slot, unit in enumerate(waiting[: SLOTS[stage]]):
                copies = [self.load(unit, number, slot) for number in range(len(self.units[unit]))]
                self.reading.append((unit, slot, copies))

    def point(self):
        kind = TICKS[self.places]
        self.places += 1
        for stages in ((), (ALL,), (ALL, ALL), ((0,),), (tuple(n for n in ALL if n),))[kind]:
            self.tick(stages)

    def close(self):
        while self.stage:
            self.tick((0, 1, 2, 3), gaps=(1, 1, 1, 1))
            self.finish()
        for copy, waiting in self.started:
            if waiting:
                copy.wait_send()


def backward_kernel(grid, length, units, of_array, groups, *refs):
    it = iter(refs)

    def take(count):
        return [next(it) for _ in range(count)]

    (table_ref, prev_ref, begin_ref) = take(3)
    (
        x_hbm, up_hbm, mixed_hbm, r_hbm, k_hbm, v_hbm, gate_hbm, wkv_hbm, attended_hbm, middle_hbm, mixed2_hbm,
        hidden_hbm, d_carried_hbm, d_recv_hbm,
    ) = take(14)
    w_k, w_v, w_r, w_g, w_o, f_r, f_k, f_v = take(8)
    (d_input_ref,) = take(1)
    outs = take(len(of_array))
    landings = {group: take(4) for group in groups}
    keeps = {(u, n): next(it) for u, unit in enumerate(units) for n in range(len(unit))}
    gives = {group: next(it) for group in groups}
    loads = {group: take(4) for group in groups}
    (
        hid, dc, dr, m2, dkey, wide, tall, dn, db, mid, nrm, up, dmid, rr, kk, vv, wk, dgate,
        own_ref, got_ref, out_ref, end_ref, fade_ref, acc, edge_ref, arrive_ref,
        send_sem, recv_sem, load_sem, in_sem, wide_sem, edge_send, edge_recv, send_a, recv_a, send_b, recv_b,
    ) = it
    index, digit = grid.place()
    me = index["seq"]
    tokens, width = dc.shape
    segments = tokens // length
    pairs, rows = width // LANES, width // grid.seq
    n0 = grid.shape[0]
    c_at = grid.order.index("c") - 1
    scatter = Scatter(grid, index, digit, units, keeps, gives, landings, loads, outs, send_sem, recv_sem, load_sem)
    batch_roles = [n for n in grid.order if grid.axis[n] == "batch"]
    peers = [
        grid.peer(index, digit, n, lax.rem(digit[n] + j, grid.size[n])) for n in batch_roles for j in range(1, grid.size[n])
    ]
    peers += [(lax.rem(me + j, grid.seq), index["batch"]) for j in range(1, grid.seq)]

    fetched = {}

    def fetch(name, source, target, slot):
        copy = pltpu.make_async_copy(source, target, in_sem.at[slot])
        copy.start()
        fetched[name] = copy

    def have(*names):
        for name in names:
            fetched.pop(name).wait()

    fetch("hid", hidden_hbm, hid, 0)
    fetch("dc", d_carried_hbm, dc, 1)
    fetch("tall", f_v.at[0], tall, 2)
    fetch("m2", mixed2_hbm, m2, 3)
    fetch("dr", d_recv_hbm, dr, 4)
    fetch("mid", middle_hbm, mid, 5)
    fetch("up", up_hbm, up, 6)
    fetch("att", attended_hbm, dgate, 7)
    fetch("rr", r_hbm, rr, 8)
    fetch("kk", k_hbm, kk, 9)
    fetch("vv", v_hbm, vv, 10)
    fetch("wk", wkv_hbm, wk, 11)
    acc[...] = jnp.zeros_like(acc)
    greet(peers)

    everything = (slice(None),) * 5

    def weight_load(array, column, columns, slot):
        copy = pltpu.make_async_copy(
            array.at[everything + (pl.ds(column, columns),)],
            wide.at[(slot,) + everything + (pl.ds(0, columns),)],
            wide_sem.at[slot],
        )
        copy.start()
        return copy

    def weight(slot, columns):
        return wide[(slot,) + everything + (pl.ds(0, columns),)].reshape((-1, columns))

    def tile(n, step):
        return pl.ds(pl.multiple_of(n * step, step), step)

    def gradient(unit, left_ref, right_ref):
        parts = units[unit]
        targets = [scatter.open(unit, number) for number in range(len(parts))]
        span = left_ref.shape[1] // n0
        for batch in [list(range(len(parts)))]:
            first = parts[batch[0]]
            width_all = sum(parts[number].columns for number in batch)

            def run(y, carry, batch=batch, first=first, width_all=width_all):
                total = dot(left_ref[:, tile(y, span)], right_ref[:, first.column : first.column + width_all], 0, 0)
                is_zero = digit["c"] == 0
                for number in batch:
                    keep, give = targets[number]
                    at = parts[number].column - first.column
                    value = total[:, at : at + parts[number].columns].reshape(grid.shape[1:] + parts[number].tile)
                    zero = value[(slice(None),) * c_at + (0,)]
                    one = value[(slice(None),) * c_at + (1,)]
                    keep[y] = jnp.where(is_zero, zero, one).astype(keep.dtype)
                    give[y] = jnp.where(is_zero, one, zero).astype(give.dtype)
                return carry

            lax.fori_loop(0, n0, run, 0)
        scatter.give(unit)

    U = dict(zip(("fv", "fr", "fk", "o", "g", "r", "k", "v", "small"), of_array))

    have("hid", "dc")
    for unit in U["fv"]:
        gradient(unit, hid, dc)
        scatter.point()
    span = hid.shape[1] // n0
    loading = weight_load(f_r, 0, width, 0)
    chunks = pieces(hid.shape[1], CHUNK)
    for y in range(n0):
        have("tall")

        def key(m, carry, y=y):
            at = tile(m, 256)
            window = slice(y * span, (y + 1) * span)
            d_hidden = dot(dc[at, :], tall[...].reshape((span, width)), 1, 1)
            dkey[at, window] = (2.0 * jnp.sqrt(hid[at, window].astype(F32)) * d_hidden).astype(BF16)
            return carry

        lax.fori_loop(0, tokens // 256, key, 0)
        if y + 1 < n0:
            fetch("tall", f_v.at[y + 1], tall, 2)
        if y < 2:
            scatter.point()
        if y == 0:
            have("m2", "dr")
            gradient(U["fr"][0], m2.at[1], dr)
            scatter.point()
            loading.wait()
            loading = weight_load(f_k, *chunks[0], 1)

            def through_recv(m, carry):
                at = tile(m, 256)
                db[at, :] = dot(dr[at, :], weight(0, width), 1, 1)
                return carry

            lax.fori_loop(0, tokens // 256, through_recv, 0)
            scatter.point()
    for c in range(3):
        fetch("mx%d" % c, mixed_hbm.at[c], hid.at[:, pl.ds(c * width, width)], c)
    for number, unit in enumerate(U["fk"]):
        gradient(unit, m2.at[0], dkey)
        scatter.point()
        column, columns = chunks[number]
        slot = (number + 1) % 2
        loading.wait()
        if number + 1 < len(chunks):
            loading = weight_load(f_k, *chunks[number + 1], 1 - slot)

        def through_key(m, carry, number=number, column=column, columns=columns, slot=slot):
            at = tile(m, 256)
            value = dot(dkey[at, column : column + columns], weight(slot, columns), 1, 1)
            dn[at, :] = value if number == 0 else dn[at, :] + value
            return carry

        lax.fori_loop(0, tokens // 256, through_key, 0)
        scatter.point()
    fetch("mx3", mixed_hbm.at[3], m2.at[0], 3)
    loading = weight_load(w_o, 0, width, 0)

    step = 64

    def fold_rows(value):
        return jnp.sum(value.reshape((step // 8, 8, width)), axis=0)

    def norm(source_ref, gain, bias):
        def run(i, carry):
            at = tile(i, step)
            value = source_ref[at, :].astype(F32)
            center = value - jnp.mean(value, axis=-1, keepdims=True)
            spread = jnp.mean(center * center, axis=-1, keepdims=True)
            nrm[at, :] = center * lax.rsqrt(spread + 1e-05) * table_ref[gain : gain + 1, :] + table_ref[bias : bias + 1, :]
            return carry

        lax.fori_loop(0, tokens // step, run, 0)

    def swap_edges(slot):
        edge_ref[...] = jnp.zeros_like(edge_ref)
        for q in range(segments):
            edge_ref[q : q + 1, :] = db[q * length : q * length + 8, :][0:1, :]
        copy = pltpu.make_async_remote_copy(
            src_ref=edge_ref,
            dst_ref=arrive_ref.at[slot],
            send_sem=edge_send.at[slot],
            recv_sem=edge_recv.at[slot],
            device_id=(lax.rem(me + grid.seq - 1, grid.seq), index["batch"]),
            device_id_type=MESH,
        )
        copy.start()
        return copy

    def norm_back(source_ref, gain, bias, slot, base_ref, put):
        keep_next = jnp.where(me == grid.seq - 1, 0.0, 1.0)
        for q in range(segments):
            count = length // step

            def run(i, carry, q=q):
                at = tile(q * count + count - 1 - i, step)
                value = source_ref[at, :].astype(F32)
                center = value - jnp.mean(value, axis=-1, keepdims=True)
                spread = jnp.mean(center * center, axis=-1, keepdims=True)
                scale = lax.rsqrt(spread + 1e-05)
                z = center * scale
                before = db[at, :]
                row = lax.broadcasted_iota(jnp.int32, (step, 1), 0)
                d_normed = dn[at, :] + jnp.where(row == step - 1, carry, pltpu.roll(before, step - 1, 0))
                acc[gain] += fold_rows(z * d_normed)
                acc[bias] += fold_rows(d_normed)
                e = d_normed * table_ref[gain : gain + 1, :]
                back = (e - jnp.mean(e, axis=-1, keepdims=True) - z * jnp.mean(e * z, axis=-1, keepdims=True)) * scale
                put(at, base_ref[at, :].astype(F32) + back)
                return before[0:1, :]

            lax.fori_loop(0, count, run, arrive_ref[slot, q : q + 1, :] * keep_next)
            scatter.point()

    have("mid")
    norm(mid, 10, 11)
    scatter.point()

    def blend_two(q, first, last, carry):
        def run(i, carry):
            at = tile(q * (length // step) + i, step)
            current = nrm[at, :]
            row = lax.broadcasted_iota(jnp.int32, (step, 1), 0)
            difference = current - jnp.where(row == 0, carry, pltpu.roll(current, 1, 0))
            here, before = dn[at, :], db[at, :]
            acc[12] += fold_rows(difference * here)
            acc[13] += fold_rows(difference * before)
            a, b = table_ref[12:13, :], table_ref[13:14, :]
            dn[at, :] = here * a + before * b
            db[at, :] = here * (1.0 - a) + before * (1.0 - b)
            return current[step - 1 : step, :]

        return lax.fori_loop(first, last, run, carry)

    above = [blend_two(q, 0, 1, prev_ref[1, q : q + 1, :]) for q in range(segments)]
    moving = swap_edges(0)
    scatter.point()
    for q in range(segments):
        blend_two(q, 1, length // step, above[q])
        scatter.point()
    have("up")
    moving.wait()

    def put_middle(at, value):
        dmid[at, :] = value
        dr[at, :] = value.astype(BF16)

    norm_back(mid, 10, 11, 0, up, put_middle)
    fetch("mid", gate_hbm, mid, 5)
    fetch("up", x_hbm, up, 6)
    have("att")
    gradient(U["o"][0], dgate, dr)
    scatter.point()
    loading.wait()

    def through_out(m, carry):
        at = tile(m, 256)
        nrm[at, :] = dot(dr[at, :], weight(0, width), 1, 1)
        return carry

    lax.fori_loop(0, tokens // 256, through_out, 0)
    scatter.point()

    ones, ones16 = block_ones(F32), block_ones(BF16)
    share = 1.0 / SUBSPACE_EXTENT

    def columns(p, base=0):
        return pl.ds(pl.multiple_of(base + p * LANES, LANES), LANES)

    def rate_of(p):
        return jnp.exp(table_ref[6:7, columns(p)])

    group = lax.div(me * rows, LANES)
    own_log = table_ref[6:7, pl.ds(pl.multiple_of(group * LANES, LANES), LANES)]
    fade_ref[...] = column_of(jnp.exp(-length * jnp.exp(own_log)), length)
    have("wk", "mid", "rr")

    def own_states(p, carry):
        down, _, _ = decays(rate_of(p), length)
        both = []
        gain_sum, bias_sum = jnp.zeros((1, LANES), F32), jnp.zeros((1, LANES), F32)
        for q in range(segments):
            token = pl.ds(q * length, length)
            y = wk[token, columns(p)]
            center = y.astype(F32) - dot(y, ones16, 1, 0) * share
            spread = head_sum(center * center, ones16) * share
            scale = lax.rsqrt(spread + 0.00064)
            z = center * scale
            gain = table_ref[8:9, columns(p)]
            normalized = z * gain + table_ref[9:10, columns(p)]
            g = mid[token, columns(p)]
            s = 1.0 / (1.0 + jnp.exp(-g))
            d_att = nrm[token, columns(p)]
            dgate[token, columns(p)] = (d_att * normalized * s * (1.0 + g * (1.0 - s))).astype(BF16)
            d_norm = d_att * g * s
            gain_sum = gain_sum + jnp.sum(d_norm * z, axis=0, keepdims=True)
            bias_sum = bias_sum + jnp.sum(d_norm, axis=0, keepdims=True)
            e = d_norm * gain
            dy = ((e - head_sum(e, ones16) * share - z * (head_sum(e * z, ones16) * share)) * scale).astype(BF16)
            dc[token, columns(p)] = dy
            both.append(dot2(rr[token, columns(p)].astype(F32) * down, dy, 0, 0, "own"))
        acc[8, 0:1, columns(p)] = gain_sum
        acc[9, 0:1, columns(p)] = bias_sum
        own_ref[columns(p), :] = fold(both[0], both[1], ones).astype(BF16)
        return carry

    for quarter in range(4):
        lax.fori_loop(quarter * pairs // 4, (quarter + 1) * pairs // 4, own_states, 0)
        scatter.point()
    first = exchange(grid, index, own_ref, got_ref, rows, send_a, recv_a)
    have("mx3")
    gradient(U["g"][0], m2.at[0], dgate)
    scatter.point()
    for copy in first:
        copy.wait_recv()
    fade = fade_ref[pl.ds(pl.multiple_of(lax.rem(me * rows, LANES), rows), rows), :]
    state = jnp.zeros_like(fade)
    for block in reversed(range(grid.seq)):
        at = pl.ds(block * rows, rows)
        out_ref[at, :] = state.astype(BF16)
        state = fade * state + got_ref[at, :].astype(F32)
    second = exchange(grid, index, out_ref, end_ref, rows, send_b, recv_b)
    scatter.point()
    have("up")
    norm(up, 0, 1)
    scatter.point()
    have("kk", "vv")
    for copy in second:
        copy.wait_recv()
    later = lax.broadcasted_iota(jnp.int32, (length, length), 0) > lax.broadcasted_iota(
        jnp.int32, (length, length), 1
    )
    time = lax.broadcasted_iota(jnp.int32, (length, LANES), 0).astype(F32)

    def inside(p, carry):
        rate = rate_of(p)
        reward = table_ref[7:8, columns(p)]
        down, up_, end = decays(rate, length)
        pick = half_masks(length)
        begins, ends = begin_ref[columns(p), :].astype(F32), end_ref[columns(p), :].astype(F32)
        reward_sum, rate_sum = jnp.zeros((1, LANES), F32), jnp.zeros((1, LANES), F32)
        for q in range(segments):
            token = pl.ds(q * length, length)
            r = rr[token, columns(p)].astype(F32)
            k = kk[token, columns(p)].astype(F32)
            v = vv[token, columns(p)]
            dy = dc[token, columns(p)]
            begin, finish = unfold(begins, q, ones), unfold(ends, q, ones)
            begin16, finish16 = begin.astype(BF16), finish.astype(BF16)
            r_down = (r * down).astype(BF16)
            k_up = (k * up_).astype(BF16)
            k_end = k * end
            zero = jnp.zeros_like(r_down)
            d_r, d_k, d_v = [], [], []
            for h in range(2):
                here = pick == (h == 0)
                scores = jnp.where(later, dot(jnp.where(here, r_down, zero), k_up, 1, 1), 0.0)
                d_scores = jnp.where(later, dot(jnp.where(here, dy, zero), v, 1, 1), 0.0).astype(BF16)
                d_r.append(dot(d_scores, k_up, 1, 0))
                d_k.append(dot(d_scores, r_down, 0, 0))
                d_v.append(dot2(scores, dy, 0, 0, "inner"))
            from_r = jnp.where(pick, d_r[0], d_r[1]) + dot(dy, begin16, 1, 1)
            from_k = jnp.where(pick, d_k[0], d_k[1])
            from_end = dot(v, finish16, 1, 1)
            v32, dy32 = v.astype(F32), dy.astype(F32)
            v_dy = head_sum(v32 * dy32, ones16)
            self_part = head_sum(r * reward * k, ones16)
            dkey[token, columns(p)] = (from_r * down + reward * k * v_dy).astype(BF16)
            dkey[token, columns(p, width)] = (from_k * up_ + from_end * end + reward * r * v_dy).astype(BF16)
            dkey[token, columns(p, 2 * width)] = (
                jnp.where(pick, d_v[0], d_v[1]) + dot2(k_end, finish16, 1, 0, "cross") + self_part * dy32
            ).astype(BF16)
            reward_sum = reward_sum + jnp.sum(r * k * v_dy, axis=0, keepdims=True)
            terms = (
                (time + 1.0) * k_up.astype(F32) * from_k
                - time * r_down.astype(F32) * from_r
                - (length - 1.0 - time) * k_end * from_end
            )
            through = lax.dot_general(
                jnp.ones((8, LANES), F32), begin * finish, (((1,), (1,)), ((), ())),
                precision=lax.Precision.HIGHEST, preferred_element_type=F32,
            )[0:1, :]
            rate_sum = rate_sum + jnp.sum(terms, axis=0, keepdims=True) - length * jnp.exp(-rate * length) * through
        acc[7, 0:1, columns(p)] = reward_sum
        acc[6, 0:1, columns(p)] = rate_sum * rate
        return carry

    for p in range(pairs):
        lax.fori_loop(p, p + 1, inside, 0)
        scatter.point()
    have("mx0", "mx1", "mx2")
    weights = (w_r, w_k, w_v, w_g)
    grads = [dkey.at[:, pl.ds(c * width, width)] for c in range(3)] + [dgate]

    def load_rows(y):
        copies = []
        for c in range(4):
            copy = pltpu.make_async_copy(weights[c].at[y], wide.at[c // n0, c % n0], in_sem.at[8 + c])
            copy.start()
            copies.append(copy)
        return copies

    loading = load_rows(0)
    for c, name in enumerate("rkv"):
        gradient(U[name][0], hid.at[:, pl.ds(c * width, width)], grads[c])
        scatter.point()
    span = width // n0
    for y in range(n0):
        for copy in loading:
            copy.wait()
        window = slice(y * span, (y + 1) * span)

        def through_mix(m, carry, y=y, window=window):
            at = tile(m, length)
            current = nrm[at, window]
            given = prev_ref[0, 0:1, window]
            for q in range(1, segments):
                given = jnp.where(m == q, prev_ref[0, q : q + 1, window], given)
            row = lax.broadcasted_iota(jnp.int32, (length, 1), 0)
            difference = current - jnp.where(row == 0, given, pltpu.roll(current, 1, 0))
            here, before = None, None
            for c in range(4):
                value = dot(grads[c][at, :], wide[c // n0, c % n0].reshape((span, width)), 1, 1)
                acc[2 + c, :, window] += jnp.sum((difference * value).reshape((length // 8, 8, span)), axis=0)
                blend = table_ref[2 + c : 3 + c, window]
                here = blend * value if c == 0 else here + blend * value
                before = (1.0 - blend) * value if c == 0 else before + (1.0 - blend) * value
            dn[at, window] = here
            db[at, window] = before
            return carry

        lax.fori_loop(0, segments, through_mix, 0)
        if y + 1 < n0:
            loading = load_rows(y + 1)
        if y < 2:
            scatter.point()
    moving = swap_edges(1)
    scatter.point()
    moving.wait()

    def put_input(at, value):
        dr[at, :] = value.astype(BF16)

    norm_back(up, 0, 1, 1, dmid, put_input)
    fetch("result", dr, d_input_ref, 4)

    sums = [jnp.sum(acc[i], axis=0, keepdims=True) for i in range(14)]
    for i in range(14):
        edge_ref[0:1, :] = sums[i]
        nrm[i : i + 1, :] = edge_ref[0:1, :]
    nrm[14:16, :] = jnp.zeros((2, width), F32)
    keep, give = scatter.open(U["small"][0], 0)
    per = grid.seq * grid.batch // pairs
    names = [n for n in grid.order if n != "c"]

    def spread(i, carry):
        at, rest = {}, i
        for n in reversed(names):
            at[n] = lax.rem(rest, grid.size[n])
            rest = lax.div(rest, grid.size[n])
        for target, core in ((keep, digit["c"]), (give, 1 - digit["c"])):
            spot = dict(at, c=core)
            rank = 0
            for n in grid.order:
                rank = rank * grid.size[n] + spot[n]
            target[tuple(at[n] for n in names)] = nrm[0:16, columns(lax.div(rank, per))]
        return carry

    steps = 1
    for n in names:
        steps *= grid.size[n]
    lax.fori_loop(0, steps, spread, 0)
    scatter.give(U["small"][0])
    scatter.point()
    for copy in first + second:
        copy.wait_send()
    scatter.close()
    have("result")


def backward(grid, length, table, prev, begin, stored, weights):
    tokens, width = stored[0].shape
    hidden = stored[11].shape[1]
    blk, tall = weights[0].shape[4], weights[7].shape[4]
    arrays = [
        (tall, width, LANES, BF16), (blk, width, 512, BF16), (blk, hidden, 512, BF16), (blk, width, 512, BF16),
        (blk, width, 512, BF16), (blk, width, 512, BF16), (blk, width, 512, BF16), (blk, width, 512, BF16),
        (16, LANES, LANES, F32),
    ]
    units, of_array, counts = scatter_plan(arrays)
    groups = list(counts)
    kinds = {group: jnp.dtype(group[3]) for group in groups}
    shapes = {group: stage_shapes(grid, group) for group in groups}
    vmem = pl.BlockSpec(memory_space=pltpu.VMEM)
    anywhere = pl.BlockSpec(memory_space=pl.ANY)
    flat16, flat32 = pltpu.VMEM((tokens, width), BF16), pltpu.VMEM((tokens, width), F32)
    state = pltpu.VMEM((width, LANES), BF16)
    sems = pltpu.SemaphoreType.DMA((grid.seq - 1,))
    dma = pltpu.SemaphoreType.DMA
    count = sum(len(unit) for unit in units) * sum(size - 1 for size in grid.shape)
    landing = [
        jax.ShapeDtypeStruct((counts[group],) + shape, kinds[group]) for group in groups for shape in shapes[group]
    ]
    outs = pl.pallas_call(
        functools.partial(backward_kernel, grid, length, units, of_array, groups),
        out_shape=[jax.ShapeDtypeStruct((tokens, width), BF16)]
        + [jax.ShapeDtypeStruct((a[0], a[1]), F32) for a in arrays]
        + landing,
        in_specs=[vmem] * 3 + [anywhere] * 22,
        out_specs=[anywhere] + [vmem] * len(arrays) + [anywhere] * len(landing),
        scratch_shapes=[pltpu.VMEM(grid.sizes("c") + p.tile, p.kind) for unit in units for p in unit]
        + [pltpu.VMEM(shapes[group][0], kinds[group]) for group in groups]
        + [pltpu.VMEM((slots,) + shape, kinds[group]) for group in groups for slots, shape in zip(SLOTS, shapes[group])]
        + [
            pltpu.VMEM((tokens, hidden), BF16), flat16, flat16, pltpu.VMEM((2, tokens, width), BF16),
            pltpu.VMEM((tokens, hidden), BF16),
            pltpu.VMEM((2,) + grid.shape + (blk, CHUNK), BF16),
            pltpu.VMEM(grid.shape[1:] + (tall, width), BF16),
            flat32, flat32, flat32, flat32, flat16, flat32, flat16, flat16, flat16, flat16, flat16,
            state, state, state, state,
            pltpu.VMEM((LANES, LANES), F32),
            pltpu.VMEM((14, 8, width), F32),
            pltpu.VMEM((8, width), F32),
            pltpu.VMEM((2, 8, width), F32),
            dma((count,)), dma((count,)), dma((2 * sum(SLOTS),)), dma((12,)), dma((2,)), dma((2,)), dma((2,)),
            sems, sems, sems, sems,
        ],
        compiler_params=pltpu.CompilerParams(
            collective_id=1, has_side_effects=True, vmem_limit_bytes=VMEM_LIMIT
        ),
    )(table, prev, begin, *stored, *weights)
    return outs[0], outs[1 : 1 + len(arrays)]


def local(grid, *args):
    (
        incoming, att_entry, ffn_entry, memory, upstream,
        ln1_gain, ln1_bias, att_mix, w_recept, w_key, w_value, w_gate, decay_log, reward,
        gn_gain, gn_bias, w_out, ln2_gain, ln2_bias, ffn_mix, f_key, f_value, f_recept,
    ) = args
    segments, length, width = incoming.shape
    tokens = segments * length
    ranks = grid.seq * grid.batch
    share = width // ranks

    per = LANES // share
    rank = lax.axis_index(("seq", "batch"))
    small = jnp.stack(
        [ln1_gain, ln1_bias] + [att_mix[:, c] for c in range(4)] + [decay_log, reward, gn_gain, gn_bias, ln2_gain, ln2_bias]
        + [ffn_mix[:, c] for c in range(2)]
    )
    small = jnp.tile(jnp.pad(small, ((0, 2), (0, 0))), (1, per))
    lane = lax.broadcasted_iota(jnp.int32, small.shape, 1)
    small = jnp.where(lane // share == rank % per, small, jnp.zeros_like(small))
    rows = width // grid.seq
    row = lax.axis_index("seq") * rows
    start = memory.transpose(1, 2, 0, 3).reshape(width, segments * SUBSPACE_EXTENT)
    start = lax.dynamic_slice_in_dim(start, row, rows, 0)
    shards = [small, w_key, w_value, w_recept, w_gate, w_out, f_recept, f_key, f_value]
    outs = forward(
        grid, incoming.reshape(tokens, width), upstream.reshape(tokens, width), att_entry, ffn_entry, start, shards, length
    )
    (
        result, table, begin, prev, mixed, r, k, v, gate_pre, wkv, attended, middle, mixed2, hidden, d_carried, d_recv,
    ) = outs[9:]
    stored = [
        incoming.reshape(tokens, width), upstream.reshape(tokens, width), mixed, r, k, v, gate_pre, wkv, attended, middle,
        mixed2, hidden, d_carried, d_recv,
    ]
    d_input, (s_fv, s_fr, s_fk, s_o, s_g, s_r, s_k, s_v, s_small) = backward(
        grid, length, table, prev, begin, stored, outs[1:9]
    )
    s = lax.dynamic_slice_in_dim(s_small, (rank % per) * share, share, 1)
    shape = incoming.shape
    return (
        result.reshape(shape), d_input.reshape(shape),
        s[0], s[1], s[2:6].T, s_r, s_k, s_v, s_g, s[6], s[7], s[8], s[9], s_o, s[10], s[11], s[12:14].T,
        s_fk, s_fv, s_fr,
    )


def solution(mesh):
    grid = Grid(mesh.shape["seq"], mesh.shape["batch"])
    both, rows = P(("seq", "batch")), P(("seq", "batch"), None)
    tokens, entry = P("batch", "seq", None), P("batch", None)
    return jax.shard_map(
        functools.partial(local, grid),
        mesh=mesh,
        in_specs=(
            tokens, entry, entry, P("batch", None, None, None), tokens,
            both, both, rows, rows, rows, rows, rows, both, both, both, both, rows, both, both, rows, rows, rows, rows,
        ),
        out_specs=(
            tokens, tokens, both, both, rows, rows, rows, rows, rows, both, both, both, both, rows, both, both, rows,
            rows, rows, rows,
        ),
        check_vma=False,
    )
```
